128 devices in a mesh: lon: 16 (over x, y_hi, core), lat: 4 (over z), grp: 2 (over y_lo).
Axes of the slice: x: 4, y: 4 (y_hi: 2, y_lo: 2; y = y_hi * 2 + y_lo), z: 4, core: 2. Of those that a mesh axis runs over, the one named last changes fastest.
Arguments:
- east_vel: float32 [8, 1024, 2048], P('grp', 'lon', 'lat'), may hold values from -6 to 6
- north_vel: float32 [8, 1024, 2048], P('grp', 'lon', 'lat'), may hold values from -6 to 6
- buoyancy: float32 [8, 1024, 2048], P('grp', 'lon', 'lat'), may hold values from -6 to 6
- wet_mask: int32 [8, 1024, 2048], P('grp', 'lon', 'lat'), may hold values from 0 to 1, as said below
- bottom_level: int32 [1024, 2048], P('lon', 'lat'), may hold values from 0 to 8
- surface: float32 [1024, 2048], P('lon', 'lat'), may hold values from -3 to 3
- w_in: bfloat16 [9, 8, 32], replicated, may hold values from -0.75 to 0.75
- b_in: float32 [32], replicated, may hold values from -3 to 3
- w_mid: bfloat16 [9, 32, 32], replicated, may hold values from -0.375 to 0.375
- b_mid: float32 [32], replicated, may hold values from -3 to 3
- w_out: bfloat16 [9, 32, 8], replicated, may hold values from -0.375 to 0.375
Outputs:
- east_new: float32 [8, 1024, 2048], P('grp', 'lon', 'lat')
- north_new: float32 [8, 1024, 2048], P('grp', 'lon', 'lat')
- surface_new: float32 [1024, 2048], P('lon', 'lat')
The draws below stay inside these ranges and needn't reach their ends.
Inputs may be any that keep to these rules, and one draw needn't show every extreme that they name: wet_mask is 1 exactly at the levels below bottom_level of the column.
All inputs are finite; a program needn't handle non-finite values.
Results may differ from the reference program's by a relative error of at most 0.002.
Values may be sent and summed in bfloat16 or wider, within the bound.
No kernel may reach another device: no remote copies, remote signals or barrier semaphores. Data moves between devices by JAX's collectives and lax.ppermute only.
A program may use at most 128 MiB of HBM per device.

```python
import jax
import jax.numpy as jnp
from jax import lax

CX = 64
LEV_DEV = 4
CHAN = 32
NSUB = 8
LEVELS = 8
NX = 1024
NY = 2048


def column_levels(key):
    return jax.random.randint(jax.random.fold_in(key, 7), (NX, NY), 0, LEVELS + 1)


def draw_bottom_level(key, part):
    return column_levels(key).astype(jnp.int32)


def draw_wet_mask(key, part):
    levels = column_levels(key)
    return (jnp.arange(LEVELS)[:, None, None] < levels[None]).astype(jnp.int32)


def steps_of(rng, extent, split, low, largest):
    gain, own = 1.0, jax.random.fold_in(rng, 6)
    for position, blocks in split:
        draws = jnp.exp(jax.random.uniform(jax.random.fold_in(own, position), (blocks,), jnp.float32, low / len(split), largest / len(split)))
        gain = gain * jnp.repeat(draws, extent[position] // blocks).reshape([-1 if axis == position else 1 for axis in range(len(extent))])
    return gain


def normal_values(rng, shape, scale, most, split=(), kind=jnp.bfloat16):
    result = jax.random.normal(rng, shape, jnp.float32) * scale
    if len(split) > 0:
        result = steps_of(rng, shape, split, -0.22, 0.18) * result
    return jnp.clip(result, min=-most, max=most).astype(kind)


def setup_inputs(seed: int = 0) -> dict:
    streams_of = jax.random.split(jax.random.key(seed), 12)
    return {
        "east_vel": normal_values(streams_of[0], (LEVELS, NX, NY), 1.0, 6.0, ((0, 2), (1, 16), (2, 4)), jnp.float32),
        "north_vel": normal_values(streams_of[1], (LEVELS, NX, NY), 1.0, 6.0, ((0, 2), (1, 16), (2, 4)), jnp.float32),
        "buoyancy": normal_values(streams_of[2], (LEVELS, NX, NY), 1.0, 6.0, ((0, 2), (1, 16), (2, 4)), jnp.float32),
        "wet_mask": draw_wet_mask(jax.random.fold_in(streams_of[11], 71), 0),
        "bottom_level": draw_bottom_level(jax.random.fold_in(streams_of[11], 71), 0),
        "surface": normal_values(streams_of[5], (NX, NY), 0.5, 3.0, ((0, 16), (1, 4)), jnp.float32),
        "w_in": normal_values(streams_of[6], (9, 2 * LEV_DEV, CHAN), (18 * LEV_DEV) ** -0.5, 0.75),
        "b_in": normal_values(streams_of[7], (CHAN,), 0.5, 3.0, (), jnp.float32),
        "w_mid": normal_values(streams_of[8], (9, CHAN, CHAN), (9 * CHAN) ** -0.5, 0.375),
        "b_mid": normal_values(streams_of[9], (CHAN,), 0.5, 3.0, (), jnp.float32),
        "w_out": normal_values(streams_of[10], (9, CHAN, 2 * LEV_DEV), (9 * CHAN) ** -0.5, 0.375),
    }


coriolis_base = 0.6
coriolis_slope = 0.8
press_coef = 0.3
drag_coef = 0.5
step_dt = 0.2
closure_coef = 0.5
gravity = 1.0
sub_dt = 0.4


def thickness(count):
    return 1.0 + 0.25 * jnp.arange(count).astype(jnp.float32)


def conv_layer(field, weight, bias):
    width = field.shape[1] - 2
    height = field.shape[2] - 2
    total = jnp.zeros((weight.shape[2], width, height), jnp.float32)
    for offset in range(9):
        shift_x = offset // 3
        shift_y = offset % 3
        window = field[:, shift_x:shift_x + width, shift_y:shift_y + height]
        total = total + jnp.einsum("io,ixy->oxy", weight[offset].astype(jnp.float32), window.astype(jnp.float32))
    return total + bias[:, None, None]


def closure_stack(padded, inside, w_in, b_in, w_mid, b_mid, w_out):
    source = jnp.where(inside[None, None, :] > 0, padded, jnp.zeros_like(padded))
    first = jnp.maximum(conv_layer(source, w_in, b_in), 0.0)
    first = jnp.where(inside[None, None, 1:-1] > 0, first, 0.0).astype(jnp.bfloat16)
    second = jnp.maximum(conv_layer(first, w_mid, b_mid), 0.0)
    second = jnp.where(inside[None, None, 2:-2] > 0, second, 0.0).astype(jnp.bfloat16)
    final = conv_layer(second, w_out, jnp.zeros((w_out.shape[2],), jnp.float32))
    return (closure_coef * final).astype(jnp.bfloat16)


def ddx_wrap(field):
    return (jnp.roll(field, -1, -2) - jnp.roll(field, 1, -2)) * 0.5


def ddy_zero(field):
    widths = [(0, 0)] * (field.ndim - 1) + [(1, 1)]
    padded = jnp.pad(field, widths)
    return (padded[..., 2:] - padded[..., :-2]) * 0.5


def reference(east_vel, north_vel, buoyancy, wet_mask, bottom_level, surface, w_in, b_in, w_mid, b_mid, w_out):
    thick = thickness(LEVELS)
    wetf = wet_mask.astype(jnp.float32)
    upper = jnp.concatenate([east_vel[:LEV_DEV] * wetf[:LEV_DEV], north_vel[:LEV_DEV] * wetf[:LEV_DEV]], 0).astype(jnp.bfloat16)
    padded = jnp.concatenate([upper[:, -3:], upper, upper[:, :3]], 1)
    padded = jnp.pad(padded, ((0, 0), (0, 0), (3, 3)))
    rows = jnp.arange(-3, NY + 3)
    inside = ((rows >= 0) & (rows < NY)).astype(jnp.float32)
    half = CX // 2

    def strip(index):
        piece = lax.dynamic_slice_in_dim(padded, (index * half).astype(jnp.int32), half + 6, 1)
        return closure_stack(piece, inside, w_in, b_in, w_mid, b_mid, w_out)

    strips = lax.map(strip, jnp.arange(NX // half).astype(jnp.int32))
    forcing = strips.transpose(1, 0, 2, 3).reshape(2 * LEV_DEV, NX, NY).astype(jnp.float32)
    rest = jnp.zeros((LEVELS - LEV_DEV, NX, NY), jnp.float32)
    force_east = jnp.concatenate([forcing[:LEV_DEV], rest], 0)
    force_north = jnp.concatenate([forcing[LEV_DEV:], rest], 0)

    weighted = buoyancy * wetf * thick[:, None, None]
    pressure = jnp.cumsum(weighted, 0) - 0.5 * weighted
    grad_x = ddx_wrap(pressure)
    grad_y = ddy_zero(pressure)
    coriolis = coriolis_base + coriolis_slope * (jnp.arange(NY).astype(jnp.float32) / NY - 0.5)
    level_ids = jnp.arange(LEVELS)[:, None, None]
    bottom = (level_ids == bottom_level[None] - 1).astype(jnp.float32)
    tend_east = wetf * (coriolis * north_vel - press_coef * grad_x + force_east - drag_coef * bottom * east_vel)
    tend_north = wetf * (-coriolis * east_vel - press_coef * grad_y + force_north - drag_coef * bottom * north_vel)

    column_thick = (level_ids < bottom_level[None]).astype(jnp.float32) * thick[:, None, None]
    depth = jnp.sum(column_thick, 0)
    floored = jnp.maximum(depth, 1.0)
    relative = depth / jnp.sum(thick)
    column = (bottom_level > 0).astype(jnp.float32)
    weights_col = wetf * thick[:, None, None]
    mean_te = jnp.sum(weights_col * tend_east, 0) / floored
    mean_tn = jnp.sum(weights_col * tend_north, 0) / floored
    east_start = jnp.sum(weights_col * east_vel, 0) / floored
    north_start = jnp.sum(weights_col * north_vel, 0) / floored

    east_bar, north_bar, level_now = east_start, north_start, surface
    for step in range(NSUB):
        east_bar = column * (east_bar + sub_dt * (-gravity * ddx_wrap(level_now) + mean_te))
        north_bar = column * (north_bar + sub_dt * (-gravity * ddy_zero(level_now) + mean_tn))
        level_now = level_now - sub_dt * (ddx_wrap(relative * east_bar) + ddy_zero(relative * north_bar))

    east_new = wetf * (east_vel + step_dt * (tend_east - mean_te) - east_start + east_bar)
    north_new = wetf * (north_vel + step_dt * (tend_north - mean_tn) - north_start + north_bar)
    return (east_new, north_new, level_now)
```

```python
import functools

import jax
import jax.numpy as jnp
from jax import lax
from jax.experimental import pallas as pl
from jax.experimental.pallas import tpu as pltpu
from jax.sharding import PartitionSpec as P

NSUB = 8
TX, TY = 64, 512
LANES = 640
ROWS = 104
TOP = 20
EDGE = 18
FIELDS = 14
F32 = jnp.float32
BF = jnp.bfloat16

coriolis_base = 0.6
coriolis_slope = 0.8
press_coef = 0.3
drag_coef = 0.5
step_dt = 0.2
closure_coef = 0.5
gravity = 1.0
sub_dt = 0.4
TOTAL_DEPTH = 15.0

VMEM = pl.BlockSpec(memory_space=pltpu.VMEM)
SMEM = pl.BlockSpec(memory_space=pltpu.SMEM)
PARAMS = pltpu.CompilerParams(vmem_limit_bytes=48 * 2**20)


def sds(shape, dtype=F32):
    return jax.ShapeDtypeStruct(shape, dtype)


def wet_of(bl, level):
    return jnp.where(bl > level, 1.0, 0.0)


def latitudes(lat, shape):
    lane = lax.broadcasted_iota(jnp.int32, shape, len(shape) - 1)
    return lat * TY + jnp.where(lane < TY + 64, lane, lane - LANES)


def inside_of(lat, total, shape):
    y = latitudes(lat, shape)
    return jnp.where((y >= 0) & (y < total), 1.0, 0.0)


def pack_lat(sc, u0, v0, b0, l0, s0, u3, v3, b3, l3, s3, to_down, to_up):
    base = 4 * sc[0]
    lane = lax.broadcasted_iota(jnp.int32, (TX, 128), 1)

    def fields(u, v, b, l, s):
        bl = l[...].astype(F32)
        wets = [wet_of(bl, (base + k).astype(F32)) for k in range(4)]
        for a in (u, v, b):
            for k in range(4):
                yield a[k] * wets[k]
        yield bl
        yield s[...]

    for out, args, origin in ((to_down, (u0, v0, b0, l0, s0), 0), (to_up, (u3, v3, b3, l3, s3), 128 - EDGE)):
        for i, field in enumerate(fields(*args)):
            tile, place = divmod(i, 7)
            if place == 0:
                acc = jnp.zeros((TX, 128), F32)
            moved = pltpu.roll(field, (EDGE * place - origin) % 128, 1)
            acc = jnp.where((lane >= EDGE * place) & (lane < EDGE * (place + 1)), moved, acc)
            if place == 6:
                out[tile] = acc.astype(BF)


def pack_lon(sc, before, after, *refs):
    tops, bots, extra_t, extra_b = refs[0:5], refs[5:10], refs[10:13], refs[13:16]
    hal, to_down, to_up, work = refs[16:]
    base = 4 * sc[0]
    lane = lax.broadcasted_iota(jnp.int32, (TX, 128), 1)
    for tile in range(2):
        low, high = before[tile].astype(F32), after[tile].astype(F32)
        for place in range(7):
            a = pltpu.roll(high, (-EDGE * place) % 128, 1)
            b = pltpu.roll(low, (128 - EDGE - EDGE * place) % 128, 1)
            hal[tile * 7 + place] = jnp.where(lane < EDGE, a, jnp.where(lane >= 128 - EDGE, b, 0.0))
    for out, (u, v, b, l, s), row in ((to_down, tops, 0), (to_up, bots, TX - 16)):
        bl = l[...].astype(F32)
        for k in range(4):
            wet = wet_of(bl, (base + k).astype(F32))
            for n, a in enumerate((u, v, b)):
                out[4 * n + k, :, :TY] = (a[k] * wet).astype(BF)
        out[12, :, :TY] = bl.astype(BF)
        out[13, :, :TY] = s[...].astype(BF)
        for i in range(FIELDS):
            out[i, :, TY:] = hal[i, row : row + 16, :].astype(BF)
    for out, (u, v, l), first, row in ((to_down, extra_t, 0, 16), (to_up, extra_b, 6, 46)):
        bl = l[first : first + 2, :].astype(F32)
        for k in range(4):
            wet = wet_of(bl, (base + k).astype(F32))
            for n, a in enumerate((u, v)):
                work[2 * (4 * n + k) : 2 * (4 * n + k) + 2, :TY] = a[k, first : first + 2, :] * wet
        for i in range(8):
            work[2 * i : 2 * i + 2, TY:] = hal[i, row : row + 2, :]
        out[14] = work[...].astype(BF)


def build_weights(w_in, b_in, w_mid, b_mid, w_out, w1, w2, w3, b1, b2, spread):
    def across(parts, rows, cols):
        rows_all = sum(p.shape[0] for p in parts)
        full = jnp.concatenate(parts + [jnp.zeros((128 - rows_all, 128), F32)], 0)
        return full.T[:rows, :]

    def wide(a):
        return jnp.concatenate([a, jnp.zeros((a.shape[0], 128 - a.shape[1]), F32)], 1)

    zero8 = jnp.zeros((8, 128), F32)
    parts = []
    for a in range(3):
        parts += [wide(w_in[3 * a + b].astype(F32)) for b in range(3)] + [zero8]
    first = across(parts, 32, 96)
    first = jnp.concatenate([first, jnp.zeros((32, 128), F32)], 1)
    for p in range(6):
        w1[32 * p : 32 * p + 32, :] = pltpu.roll(first, 32 * p, 1).astype(BF)
    for b in range(3):
        mid = across([wide(w_mid[3 * a + b].astype(F32)) for a in range(3)], 32, 96)
        mid = jnp.concatenate([mid, jnp.zeros((32, 128), F32)], 1)
        for p in range(6):
            w2[192 * b + 32 * p : 192 * b + 32 * p + 32, :] = pltpu.roll(mid, 32 * p, 1).astype(BF)
        last = across([wide(w_out[3 * a + b].astype(F32)) for a in range(3)], 8, 96)
        last = jnp.concatenate([last, jnp.zeros((8, 256), F32)], 1)
        for p in range(8):
            spread[:, p, :] = pltpu.roll(last, 32 * p, 1)
        w3[64 * b : 64 * b + 64, :] = spread[...].reshape(64, 384)[:, :320].astype(BF)
    eye = lax.broadcasted_iota(jnp.int32, (32, 32), 0) == lax.broadcasted_iota(jnp.int32, (32, 32), 1)
    for src, dst in ((b_in, b1), (b_mid, b2)):
        column = jnp.sum(jnp.where(eye, src[...], 0.0), 1, keepdims=True)
        for p in range(6):
            dst[32 * p : 32 * p + 32, :] = jnp.broadcast_to(column, (32, 128))


def load_slots(up, start, count, in0):
    def one(s, _):
        c = up[:, start + s, :]
        r = pl.multiple_of(s * 32, 32)
        in0[pl.ds(r, 16), :] = jnp.concatenate([pltpu.roll(c, 1, 1), c], 0).astype(BF)
        in0[pl.ds(r + 16, 16), :] = jnp.concatenate([pltpu.roll(c, LANES - 1, 1), jnp.zeros_like(c)], 0).astype(BF)
        return 0

    lax.fori_loop(0, count, one, 0, unroll=2)


def closure(in0, act1, act2, weights, inside, n1, n2, n3, shift, store, unroll):
    w1, w2, w3, b1, b2 = weights
    bias1, bias2 = b1[:, :1], b2[:, :1]

    def combined(o, m):
        return pltpu.roll(o[:m], 1, 1) + o[m : 2 * m] + pltpu.roll(o[2 * m :], LANES - 1, 1)

    def first(j, _):
        x = in0[pl.ds(pl.multiple_of(j * 192, 64), 256), :]
        o = jnp.dot(w1[...], x, preferred_element_type=F32)
        act1[pl.ds(pl.multiple_of(j * 192, 64), 192), :] = (jnp.maximum(o + bias1, 0.0) * inside).astype(BF)
        return 0

    def second(j, _):
        x = act1[pl.ds(pl.multiple_of(j * 192, 64), 256), :]
        o = combined(jnp.dot(w2[...], x, preferred_element_type=F32), 192)
        o = (jnp.maximum(o + bias2, 0.0) * inside).astype(BF)
        act2[pl.ds(pl.multiple_of(j * 192 + 32 * shift, 32), 192), :] = o
        return 0

    def third(j, _):
        x = act2[pl.ds(pl.multiple_of(j * 256, 256), 320), :]
        o = combined(jnp.dot(w3[...], x, preferred_element_type=F32), 64)
        store(j, (closure_coef * o).astype(BF).astype(F32).reshape(8, 8, LANES))
        return 0

    lax.fori_loop(0, n1, first, 0, unroll=unroll)
    lax.fori_loop(0, n2, second, 0, unroll=unroll)
    lax.fori_loop(0, n3, third, 0, unroll=min(unroll, n3))


def interior(total, sc, u, v, bl, hal, w1, w2, w3, b1, b2, out, up, in0, act1, act2):
    @pl.when(sc[0] == 0)
    def _():
        level = bl[...].astype(F32)
        for k in range(4):
            wet = wet_of(level, float(k))
            up[k, :, :TY] = u[k] * wet
            up[4 + k, :, :TY] = v[k] * wet
        for i in range(8):
            up[i, :, TY:] = hal[i]
        load_slots(up, 1, 62, in0)
        act1[1920:1984, :] = jnp.zeros((64, LANES), BF)
        inside = inside_of(sc[1], total, (1, LANES))

        def store(j, f):
            out[:, pl.ds(pl.multiple_of(8 * j, 8), 8), :] = f

        closure(in0, act1, act2, (w1, w2, w3, b1, b2), inside, 10, 10, 7, 0, store, 5)

    @pl.when(sc[0] != 0)
    def _():
        out[...] = jnp.zeros_like(out)


def assemble(sc, u, v, b, bl, s, hal, low, high, ext):
    base = 4 * sc[0]
    level = bl[...].astype(F32)
    for i in range(FIELDS):
        ext[i, 0:8, :] = jnp.zeros((8, LANES), F32)
        ext[i, 96:104, :] = jnp.zeros((8, LANES), F32)
        ext[i, 4:20, :] = low[i].astype(F32)
        ext[i, 84:100, :] = high[i].astype(F32)
        ext[i, 20:84, TY:] = hal[i]
    for k in range(4):
        wet = wet_of(level, (base + k).astype(F32))
        for n, a in enumerate((u, v, b)):
            ext[4 * n + k, 20:84, :TY] = a[k] * wet
    ext[12, 20:84, :TY] = level
    ext[13, 20:84, :TY] = s[...]
    more_low, more_high = low[14].astype(F32), high[14].astype(F32)
    for i in range(8):
        ext[i, 2:4, :] = more_low[2 * i : 2 * i + 2, :]
        ext[i, 100:102, :] = more_high[2 * i : 2 * i + 2, :]


def pressures(base, ext, pr, load, rows):
    for r in range(0, rows, 8):
        run = jnp.zeros((8, LANES), F32)
        for k in range(4):
            weighted = ext[8 + k, r : r + 8, :] * (1.0 + 0.25 * (base + k).astype(F32))
            pr[k, r + 8 : r + 16, :] = run + 0.5 * weighted
            run = run + weighted
        load[r + 8 : r + 16, :] = run


def grads(ref, r):
    here = ref[r + 8 : r + 16, :]
    gx = (ref[r + 9 : r + 17, :] - ref[r + 7 : r + 15, :]) * 0.5
    gy = (pltpu.roll(here, LANES - 1, 1) - pltpu.roll(here, 1, 1)) * 0.5
    return gx, gy


def column_sums(total, sc, u, v, b, bl, s, hal, low, high, sums, early, two, edge, ext, pr, load):
    assemble(sc, u, v, b, bl, s, hal, low, high, ext)
    base = 4 * sc[0]
    upper = jnp.where(sc[0] == 0, 1.0, 0.0)
    pr4 = [pr.at[k] for k in range(4)]
    for ref in pr4 + [load]:
        ref[0:8, :] = jnp.zeros((8, LANES), F32)
        ref[ROWS + 8 : ROWS + 16, :] = jnp.zeros((8, LANES), F32)
    pressures(base, ext, pr, load, ROWS)
    y = latitudes(sc[1], (8, LANES)).astype(F32)
    coriolis = coriolis_base + coriolis_slope * (y * (1.0 / total) - 0.5)
    for r in range(0, ROWS, 8):
        rr = slice(r, r + 8)
        level = ext[12, rr, :]
        te = jnp.zeros((8, LANES), F32)
        tn, us, vs = te, te, te
        for k in range(4):
            number = (base + k).astype(F32)
            thick = 1.0 + 0.25 * number
            weight = jnp.where(level > number, thick, 0.0)
            drag = jnp.where(level == number + 1.0, drag_coef, 0.0)
            east, north = ext[k, rr, :], ext[4 + k, rr, :]
            gx, gy = grads(pr4[k], r)
            te = te + weight * (coriolis * north - press_coef * gx - drag * east)
            tn = tn + weight * (-coriolis * east - press_coef * gy - drag * north)
            us = us + thick * east
            vs = vs + thick * north
        below = jnp.zeros((8, LANES), F32)
        for k in range(4, 8):
            below = below + jnp.where(level > float(k), 1.0 + 0.25 * k, 0.0)
        gx, gy = grads(load, r)
        below = below * (press_coef * upper)
        sums[0, rr, :] = te - below * gx
        sums[1, rr, :] = tn - below * gy
        sums[2, rr, :] = us
        sums[3, rr, :] = vs
        for i, a in enumerate((us, vs, gx, gy)):
            early[i, rr, :] = a.astype(BF)
        two[0, rr, :] = level
        two[1, rr, :] = ext[13, rr, :]
    edge[:, 0:32, :] = ext[0:8, 0:32, :]
    edge[:, 32:64, :] = ext[0:8, 72:104, :]


def edges(total, sc, edge, inner, two, sums, w1, w2, w3, b1, b2, out, force, in0, act1, act2):
    @pl.when(sc[0] == 0)
    def _():
        inside = inside_of(sc[1], total, (1, LANES))
        for side, (start, shift) in enumerate(((2, 5), (37, 0))):
            load_slots(edge, start, 26, in0)
            act1[768:832, :] = jnp.zeros((64, LANES), BF)
            act2[...] = jnp.zeros_like(act2)

            def store(j, f, side=side):
                force[:, pl.ds(pl.multiple_of(8 * j + 24 * side, 8), 8), :] = f

            closure(in0, act1, act2, (w1, w2, w3, b1, b2), inside, 4, 4, 3, shift, store, 4)
        for r in range(0, ROWS, 8):
            rr = slice(r, r + 8)
            level = two[0, rr, :]
            te, tn = sums[0, rr, :], sums[1, rr, :]
            for k in range(4):
                weight = jnp.where(level > float(k), 1.0 + 0.25 * k, 0.0)
                if r < 24:
                    fe, fn = force[k, rr, :], force[4 + k, rr, :]
                elif r >= 80:
                    fe, fn = force[k, r - 56 : r - 48, :], force[4 + k, r - 56 : r - 48, :]
                else:
                    fe, fn = inner[k, r - 24 : r - 16, :], inner[4 + k, r - 24 : r - 16, :]
                te = te + weight * fe
                tn = tn + weight * fn
            out[0, rr, :] = te
            out[1, rr, :] = tn

    @pl.when(sc[0] != 0)
    def _():
        out[...] = sums[0:2]
        force[...] = jnp.zeros_like(force)


def own_part(total, sc, u, v, b, bl, hal, low, high, inner, force, out, pb, pr, load):
    base = 4 * sc[0]
    level = bl[...].astype(F32)
    for k in range(4):
        number = (base + k).astype(F32)
        pb[8 + k, 0:8, :] = low[8 + k, 8:16, :].astype(F32)
        pb[8 + k, 72:80, :] = high[8 + k, 0:8, :].astype(F32)
        pb[8 + k, 8:72, :TY] = b[k] * wet_of(level, number)
        pb[8 + k, 8:72, TY:] = hal[8 + k]
    pressures(base, pb, pr, load, 80)
    y = latitudes(sc[1], (8, LANES)).astype(F32)
    coriolis = (coriolis_base + coriolis_slope * (y * (1.0 / total) - 0.5))[:, :TY]
    for r in range(0, TX, 8):
        rr = slice(r, r + 8)
        lev = bl[rr, :].astype(F32)
        for k in range(4):
            number = (base + k).astype(F32)
            wet = wet_of(lev, number)
            drag = jnp.where(lev == number + 1.0, drag_coef, 0.0)
            east, north = u[k, rr, :], v[k, rr, :]
            gx, gy = grads(pr.at[k], r + 8)
            r20 = r + TOP

            def forcing(c):
                pieces, at = [], r20
                while at < r20 + 8:
                    if at < 24:
                        end, piece = min(24, r20 + 8), lambda s, e: force[c, s:e, :TY]
                    elif at < 80:
                        end, piece = min(80, r20 + 8), lambda s, e: inner[c, s - 24 : e - 24, :TY]
                    else:
                        end, piece = r20 + 8, lambda s, e: force[c, s - 56 : e - 56, :TY]
                    pieces.append(piece(at, end))
                    at = end
                return pieces[0] if len(pieces) == 1 else jnp.concatenate(pieces, 0)

            te = coriolis * north - press_coef * gx[:, :TY] + forcing(k) - drag * east
            tn = -coriolis * east - press_coef * gy[:, :TY] + forcing(4 + k) - drag * north
            out[k, rr, :] = wet * (east + step_dt * te)
            out[4 + k, rr, :] = wet * (north + step_dt * tn)


def finish(total, sc, two, mine, theirs, sums, early, own, east_out, north_out, surface_out, lv, fx, fy, eb, nb, ae, an, rel, c2):
    upper = jnp.where(sc[0] == 0, 0.0, 1.0)
    zero8 = jnp.zeros((8, LANES), F32)
    for ref in (lv, fx):
        ref[0:8, :] = zero8
        ref[ROWS + 8 : ROWS + 16, :] = zero8
    for r in range(0, ROWS, 8):
        rr = slice(r, r + 8)
        level = two[0, rr, :]
        depth = level + 0.125 * level * (level - 1.0)
        over = 1.0 / jnp.maximum(depth, 1.0)
        rel[rr, :] = depth * (1.0 / TOTAL_DEPTH)
        c2[rr, :] = jnp.where(level > 0.0, 0.5 * sub_dt * gravity, 0.0)
        ae[rr, :] = sub_dt * (mine[0, rr, :] + theirs[0, rr, :]) * over
        an[rr, :] = sub_dt * (mine[1, rr, :] + theirs[1, rr, :]) * over
        eb[rr, :] = (sums[2, rr, :] + early[0, rr, :].astype(F32)) * over
        nb[rr, :] = (sums[3, rr, :] + early[1, rr, :].astype(F32)) * over
        lv[r + 8 : r + 16, :] = two[1, rr, :]
    inside = inside_of(sc[1], total, (8, LANES)) * 1.0

    def step(_, carry):
        for r in range(0, ROWS, 8):
            rr = slice(r, r + 8)
            here = lv[r + 8 : r + 16, :]
            dx = lv[r + 9 : r + 17, :] - lv[r + 7 : r + 15, :]
            dy = pltpu.roll(here, LANES - 1, 1) - pltpu.roll(here, 1, 1)
            c = c2[rr, :]
            e = eb[rr, :] + (ae[rr, :] - c * dx)
            n = nb[rr, :] + (an[rr, :] - c * dy)
            eb[rr, :] = e
            nb[rr, :] = n
            fx[r + 8 : r + 16, :] = rel[rr, :] * e
            fy[rr, :] = rel[rr, :] * n
        for r in range(0, ROWS, 8):
            rr = slice(r, r + 8)
            dx = fx[r + 9 : r + 17, :] - fx[r + 7 : r + 15, :]
            f = fy[rr, :]
            dy = pltpu.roll(f, LANES - 1, 1) - pltpu.roll(f, 1, 1)
            lv[r + 8 : r + 16, :] = inside * (lv[r + 8 : r + 16, :] - (0.5 * sub_dt) * (dx + dy))
        return carry

    lax.fori_loop(0, NSUB, step, 0)
    base = 4 * sc[0]
    for r in range(TOP, TOP + TX, 8):
        rr, at = slice(r, r + 8), slice(r - TOP, r - TOP + 8)
        level = two[0, rr, :TY]
        depth = level + 0.125 * level * (level - 1.0)
        over = 1.0 / jnp.maximum(depth, 1.0)
        back = (step_dt * press_coef) * upper
        gx, gy = early[2, rr, :TY].astype(F32), early[3, rr, :TY].astype(F32)
        estart = (sums[2, rr, :TY] + early[0, rr, :TY].astype(F32)) * over
        nstart = (sums[3, rr, :TY] + early[1, rr, :TY].astype(F32)) * over
        fe = eb[rr, :TY] - estart - (step_dt / sub_dt) * ae[rr, :TY] - back * gx
        fn = nb[rr, :TY] - nstart - (step_dt / sub_dt) * an[rr, :TY] - back * gy
        for k in range(4):
            wet = wet_of(level, (base + k).astype(F32))
            east_out[k, at, :] = own[k, at, :] + wet * fe
            north_out[k, at, :] = own[4 + k, at, :] + wet * fn
        surface_out[at, :] = lv[r + 8 : r + 16, :TY]


def call(kernel, name, out_shape, n_in, scratch=(), in_specs=None, cost=None, grid=()):
    single = not isinstance(out_shape, (list, tuple))
    return pl.pallas_call(
        kernel,
        name=name,
        grid=grid,
        out_shape=out_shape,
        in_specs=in_specs or [SMEM] + [VMEM] * (n_in - 1),
        out_specs=VMEM if single else [VMEM] * len(out_shape),
        scratch_shapes=list(scratch),
        compiler_params=PARAMS,
        cost_estimate=cost,
    )


def micros(us):
    return pl.CostEstimate(flops=int(us * 1e6), bytes_accessed=int(us * 3e6), transcendentals=0)


def shifted(x, axis, by, ring):
    size = lax.axis_size(axis)
    pairs = [(i, (i + by) % size) for i in range(size) if ring or 0 <= i + by < size]
    return lax.ppermute(x, axis, pairs)


def local(u, v, b, wet_mask, bl, s, w_in, b_in, w_mid, b_mid, w_out):
    total = TY * lax.axis_size("lat")
    sc = jnp.stack([lax.axis_index("grp"), lax.axis_index("lat")]).astype(jnp.int32)

    def lanes(i):
        return [pl.BlockSpec((4, TX, 128), lambda _: (0, 0, i))] * 3 + [pl.BlockSpec((TX, 128), lambda _: (0, i))] * 2

    half = sds((2, TX, 128), BF)
    to_down, to_up = call(pack_lat, "pack_lat", [half, half], 11, in_specs=[SMEM] + lanes(0) + lanes(3), grid=(1,))(
        sc, u, v, b, bl, s, u, v, b, bl, s
    )
    before = shifted(to_up, "lat", 1, False)
    after = shifted(to_down, "lat", -1, False)
    vb = [sds((192, 256), BF), sds((576, 256), BF), sds((192, 320), BF), sds((192, 128)), sds((192, 128))]
    weights = call(build_weights, "weights", vb, 5, [pltpu.VMEM((8, 8, 384), F32)], in_specs=[VMEM] * 5)(
        w_in, b_in[None, :], w_mid, b_mid[None, :], w_out
    )

    def rows(n, i, three):
        return [pl.BlockSpec((4, n, TY), lambda _: (0, i, 0))] * three + [pl.BlockSpec((n, TY), lambda _: (i, 0))] * (three - 1)

    out = sds((15, 16, LANES), BF)
    hal, down, up = call(
        pack_lon,
        "pack_lon",
        [sds((FIELDS, TX, 128)), out, out],
        19,
        [pltpu.VMEM((16, LANES), F32)],
        in_specs=[SMEM, VMEM, VMEM] + rows(16, 0, 3) + rows(16, 3, 3) + rows(8, 2, 2) + rows(8, 5, 2),
        grid=(1,),
    )(sc, before, after, u, v, b, bl, s, u, v, b, bl, s, u, v, bl, u, v, bl)
    low = shifted(up, "lon", 1, True)
    high = shifted(down, "lon", -1, True)
    inner = call(
        functools.partial(interior, total),
        "interior",
        sds((8, 56, LANES)),
        10,
        [
            pltpu.VMEM((8, TX, LANES), F32),
            pltpu.VMEM((62 * 32, LANES), BF),
            pltpu.VMEM((62 * 32, LANES), BF),
            pltpu.VMEM((60 * 32, LANES), BF),
        ],
        cost=micros(6),
    )(sc, u, v, bl, hal, *weights)
    ext2 = sds((2, ROWS, LANES))
    sums, early, two, edge = call(
        functools.partial(column_sums, total),
        "column_sums",
        [sds((4, ROWS, LANES)), sds((4, ROWS, LANES), BF), ext2, sds((8, 64, LANES))],
        9,
        [
            pltpu.VMEM((FIELDS, ROWS, LANES), F32),
            pltpu.VMEM((4, ROWS + 16, LANES), F32),
            pltpu.VMEM((ROWS + 16, LANES), F32),
        ],
        cost=micros(3),
    )(sc, u, v, b, bl, s, hal, low, high)
    early_in = shifted(early, "grp", 1, True)
    mine, force = call(
        functools.partial(edges, total),
        "edges",
        [ext2, sds((8, 48, LANES))],
        10,
        [pltpu.VMEM((26 * 32, LANES), BF), pltpu.VMEM((26 * 32, LANES), BF), pltpu.VMEM((29 * 32, LANES), BF)],
        cost=micros(5),
    )(sc, edge, inner, two, sums, *weights)
    theirs = shifted(mine, "grp", 1, True)
    own = call(
        functools.partial(own_part, total),
        "own_part",
        sds((8, TX, TY)),
        10,
        [pltpu.VMEM((12, 80, LANES), F32), pltpu.VMEM((4, 96, LANES), F32), pltpu.VMEM((96, LANES), F32)],
        cost=micros(3),
    )(sc, u, v, b, bl, hal, low, high, inner, force)
    plane = pltpu.VMEM((ROWS, LANES), F32)
    tall = pltpu.VMEM((ROWS + 16, LANES), F32)
    return tuple(
        call(
            functools.partial(finish, total),
            "finish",
            [sds((4, TX, TY)), sds((4, TX, TY)), sds((TX, TY))],
            7,
            [tall, tall, plane, plane, plane, plane, plane, plane, plane],
            cost=micros(5),
        )(sc, two, mine, theirs, sums, early_in, own)
    )


def solution(mesh):
    tile = P("grp", "lon", "lat")
    flat = P("lon", "lat")
    return jax.shard_map(
        local,
        mesh=mesh,
        in_specs=(tile, tile, tile, tile, flat, flat, P(), P(), P(), P(), P()),
        out_specs=(tile, tile, flat),
        check_vma=False,
    )
```

```python
import jax
import jax.numpy as jnp
from jax import lax
from jax.experimental import pallas as pl
from jax.experimental.pallas import tpu as pltpu
from jax.sharding import PartitionSpec as P

NSUB = 8
TX, TY = 64, 512
LANES = 640
ROWS = 96
HALO = 16
RIM = 24
EDGE = 18
FORCED = 104
FIELDS = 14
F32 = jnp.float32
BF = jnp.bfloat16

coriolis_base = 0.6
coriolis_slope = 0.8
press_coef = 0.3
drag_coef = 0.5
step_dt = 0.2
closure_coef = 0.5
gravity = 1.0
sub_dt = 0.4
TOTAL_DEPTH = 15.0

TOKEN = jax.ShapeDtypeStruct((8, 128), jnp.float32)
VMEM = pl.BlockSpec(memory_space=pltpu.VMEM)


def sds(shape, dtype=F32):
    return jax.ShapeDtypeStruct(shape, dtype)


def wet_of(bl, level):
    return jnp.where(bl > level, 1.0, 0.0)


def latitudes(lat, shape):
    lane = lax.broadcasted_iota(jnp.int32, shape, len(shape) - 1)
    return lat * TY + jnp.where(lane < TY + 64, lane, lane - LANES)


def inside_of(lat, total, shape):
    y = latitudes(lat, shape)
    return jnp.where((y >= 0) & (y < total), 1.0, 0.0)


def pack_lat(sc, u, v, b, l, s, to_down, to_up, ub, vb, bb, lb, sb, sem):
    base = 4 * sc[0]
    lane = lax.broadcasted_iota(jnp.int32, (TX, 128), 1)
    copies = []
    for side, at in enumerate((0, TY - 128)):
        for n, (src, dst) in enumerate(((u, ub), (v, vb), (b, bb))):
            copies.append(pltpu.make_async_copy(src.at[:, :, at : at + 128], dst.at[side], sem.at[side, n]))
        for n, (src, dst) in enumerate(((l, lb), (s, sb))):
            copies.append(pltpu.make_async_copy(src.at[:, at : at + 128], dst.at[side], sem.at[side, 3 + n]))
    for copy in copies:
        copy.start()
    for copy in copies:
        copy.wait()

    def fields(side):
        bl = lb[side].astype(F32)
        wets = [wet_of(bl, (base + k).astype(F32)) for k in range(4)]
        for a in (ub, vb, bb):
            for k in range(4):
                yield a[side, k] * wets[k]
        yield bl
        yield sb[side]

    for side, (out, origin) in enumerate(((to_down, 0), (to_up, 128 - EDGE))):
        for i, field in enumerate(fields(side)):
            tile, place = divmod(i, 7)
            if place == 0:
                acc = jnp.zeros((TX, 128), F32)
            moved = pltpu.roll(field, (EDGE * place - origin) % 128, 1)
            acc = jnp.where((lane >= EDGE * place) & (lane < EDGE * (place + 1)), moved, acc)
            if place == 6:
                out[tile] = acc.astype(BF)


def pack_lon(sc, ready, before, after, *refs):
    tops, bots, extra_t, extra_b = refs[0:5], refs[5:10], refs[10:13], refs[13:16]
    hal, to_down, to_up, work = refs[16:]
    base = 4 * sc[0]
    lane = lax.broadcasted_iota(jnp.int32, (TX, 128), 1)
    for tile in range(2):
        low, high = before[tile].astype(F32), after[tile].astype(F32)
        for place in range(7):
            a = pltpu.roll(high, (-EDGE * place) % 128, 1)
            b = pltpu.roll(low, (128 - EDGE - EDGE * place) % 128, 1)
            hal[tile * 7 + place] = jnp.where(lane < EDGE, a, jnp.where(lane >= 128 - EDGE, b, 0.0))
    for out, (u, v, b, l, s), row in ((to_down, tops, 0), (to_up, bots, TX - 16)):
        bl = l[...].astype(F32)
        for k in range(4):
            wet = wet_of(bl, (base + k).astype(F32))
            for n, a in enumerate((u, v, b)):
                out[4 * n + k, :, :TY] = (a[k] * wet).astype(BF)
        out[12, :, :TY] = bl.astype(BF)
        out[13, :, :TY] = s[...].astype(BF)
        for i in range(FIELDS):
            out[i, :, TY:] = hal[i, row : row + 16, :].astype(BF)
    for out, (u, v, l), first, row in ((to_down, extra_t, 0, 16), (to_up, extra_b, 6, 46)):
        bl = l[first : first + 2, :].astype(F32)
        for k in range(4):
            wet = wet_of(bl, (base + k).astype(F32))
            for n, a in enumerate((u, v)):
                work[2 * (4 * n + k) : 2 * (4 * n + k) + 2, :TY] = a[k, first : first + 2, :] * wet
        for i in range(8):
            work[2 * i : 2 * i + 2, TY:] = hal[i, row : row + 2, :]
        out[14] = work[...].astype(BF)


def build_weights(sc, w_in, b_in, w_mid, b_mid, w_out, w1, w2, w3, b1, b2, done, spread):
    done[...] = jnp.zeros_like(done)

    def across(parts, rows, cols):
        rows_all = sum(p.shape[0] for p in parts)
        full = jnp.concatenate(parts + [jnp.zeros((128 - rows_all, 128), F32)], 0)
        return full.T[:rows, :]

    def wide(a):
        return jnp.concatenate([a, jnp.zeros((a.shape[0], 128 - a.shape[1]), F32)], 1)

    zero8 = jnp.zeros((8, 128), F32)
    parts = []
    for a in range(3):
        parts += [wide(w_in[3 * a + b].astype(F32)) for b in range(3)] + [zero8]
    first = across(parts, 32, 96)
    first = jnp.concatenate([first, jnp.zeros((32, 128), F32)], 1)
    for p in range(6):
        w1[32 * p : 32 * p + 32, :] = pltpu.roll(first, 32 * p, 1).astype(BF)
    for b in range(3):
        mid = across([wide(w_mid[3 * a + b].astype(F32)) for a in range(3)], 32, 96)
        mid = jnp.concatenate([mid, jnp.zeros((32, 128), F32)], 1)
        for p in range(6):
            w2[192 * b + 32 * p : 192 * b + 32 * p + 32, :] = pltpu.roll(mid, 32 * p, 1).astype(BF)
        last = across([wide(w_out[3 * a + b].astype(F32)) for a in range(3)], 8, 96)
        last = jnp.concatenate([last, jnp.zeros((8, 256), F32)], 1)
        for p in range(8):
            spread[:, p, :] = pltpu.roll(last, 32 * p, 1)
        w3[64 * b : 64 * b + 64, :] = spread[...].reshape(64, 384)[:, :320].astype(BF)
    eye = lax.broadcasted_iota(jnp.int32, (32, 32), 0) == lax.broadcasted_iota(jnp.int32, (32, 32), 1)
    for src, dst in ((b_in, b1), (b_mid, b2)):
        column = jnp.sum(jnp.where(eye, src[...], 0.0), 1, keepdims=True)
        for p in range(6):
            dst[32 * p : 32 * p + 32, :] = jnp.broadcast_to(column, (32, 128))


def load_slots(up, start, count, in0, at):
    for i in range(count):
        c = up[:, start + i, :]
        r = 32 * (at + i)
        in0[r : r + 16, :] = jnp.concatenate([pltpu.roll(c, 1, 1), c], 0).astype(BF)
        in0[r + 16 : r + 32, :] = jnp.concatenate([pltpu.roll(c, LANES - 1, 1), jnp.zeros_like(c)], 0).astype(BF)


def closure(in0, act1, act2, weights, inside, parts, store):
    w1, w2, w3, b1, b2 = weights
    bias1, bias2 = b1[:, :1], b2[:, :1]

    def combined(o, m):
        return pltpu.roll(o[:m], 1, 1) + o[m : 2 * m] + pltpu.roll(o[2 * m :], LANES - 1, 1)

    for s1, _, _, n1, _, _ in parts:
        for j in range(n1):
            r = 32 * (s1 + 6 * j)
            o = jnp.dot(w1[...], in0[r : r + 256, :], preferred_element_type=F32)
            act1[r : r + 192, :] = (jnp.maximum(o + bias1, 0.0) * inside).astype(BF)
    for s1, s2, shift, _, n2, _ in parts:
        for j in range(n2):
            r, to = 32 * (s1 + 6 * j), 32 * (s2 + shift + 6 * j)
            o = combined(jnp.dot(w2[...], act1[r : r + 256, :], preferred_element_type=F32), 192)
            act2[to : to + 192, :] = (jnp.maximum(o + bias2, 0.0) * inside).astype(BF)
    for part, (_, s2, _, _, _, n3) in enumerate(parts):
        for j in range(n3):
            r = 32 * (s2 + 8 * j)
            o = combined(jnp.dot(w3[...], act2[r : r + 320, :], preferred_element_type=F32), 64)
            store(part, j, (closure_coef * o).astype(BF).astype(F32).reshape(8, 8, LANES))


def interior(total, sc, u, v, bl, hal, w1, w2, w3, b1, b2, out, done, up, in0, act1, act2):
    done[...] = jnp.zeros_like(done)

    @pl.when(sc[0] == 0)
    def _():
        level = bl[...].astype(F32)
        for k in range(4):
            wet = wet_of(level, float(k))
            up[k, :, :TY] = u[k] * wet
            up[4 + k, :, :TY] = v[k] * wet
        for i in range(8):
            up[i, :, TY:] = hal[i]
        load_slots(up, 1, 62, in0, 0)
        act1[1920:1984, :] = jnp.zeros((64, LANES), BF)

        def store(part, j, f):
            out[:, 24 + 8 * j : 32 + 8 * j, :] = f

        closure(in0, act1, act2, (w1, w2, w3, b1, b2), inside_of(sc[1], total, (1, LANES)), [(0, 0, 0, 10, 10, 7)], store)


def edges(total, sc, edge, w1, w2, w3, b1, b2, inner, out, in0, act1, act2):
    @pl.when(sc[0] == 0)
    def _():
        for at, start in ((0, 6), (26, 33)):
            load_slots(edge, start, 26, in0, at)
            act1[32 * at + 768 : 32 * at + 832, :] = jnp.zeros((64, LANES), BF)
        act2[0:160, :] = jnp.zeros((160, LANES), BF)
        act2[29 * 32 + 768 :, :] = jnp.zeros((64, LANES), BF)

        def store(part, j, f):
            row = 80 * part + 8 * j
            out[:, row : row + 8, :] = f

        parts = [(0, 0, 5, 4, 4, 3), (26, 29, 0, 4, 4, 3)]
        closure(in0, act1, act2, (w1, w2, w3, b1, b2), inside_of(sc[1], total, (1, LANES)), parts, store)


def pressures(base, b_rows, pr, load, rows):
    for r in range(0, rows, 8):
        run = jnp.zeros((8, LANES), F32)
        for k in range(4):
            weighted = b_rows(k, r) * (1.0 + 0.25 * (base + k).astype(F32))
            pr[k, r + 8 : r + 16, :] = run + 0.5 * weighted
            run = run + weighted
        load[r + 8 : r + 16, :] = run


def grads(ref, r):
    here = ref[r + 8 : r + 16, :]
    gx = (ref[r + 9 : r + 17, :] - ref[r + 7 : r + 15, :]) * 0.5
    gy = (pltpu.roll(here, LANES - 1, 1) - pltpu.roll(here, 1, 1)) * 0.5
    return gx, gy


def coriolis_of(lat, total, shape):
    return coriolis_base + coriolis_slope * (latitudes(lat, shape).astype(F32) * (1.0 / total) - 0.5)


def sums_of(sc, coriolis, level, east, north, pr, load, r):
    base = 4 * sc[0]
    te = jnp.zeros((8, LANES), F32)
    tn, us, vs = te, te, te
    for k in range(4):
        number = (base + k).astype(F32)
        thick = 1.0 + 0.25 * number
        weight = jnp.where(level > number, thick, 0.0)
        drag = jnp.where(level == number + 1.0, drag_coef, 0.0)
        e, n = east(k), north(k)
        gx, gy = grads(pr.at[k], r)
        te = te + weight * (coriolis * n - press_coef * gx - drag * e)
        tn = tn + weight * (-coriolis * e - press_coef * gy - drag * n)
        us = us + thick * e
        vs = vs + thick * n
    below = jnp.zeros((8, LANES), F32)
    for k in range(4, 8):
        below = below + jnp.where(level > float(k), 1.0 + 0.25 * k, 0.0)
    gx, gy = grads(load, r)
    below = below * (press_coef * jnp.where(sc[0] == 0, 1.0, 0.0))
    return te - below * gx, tn - below * gy, us, vs, gx, gy


def middle_sums(total, sc, u, v, b, bl, hal, sums, send, ext, lev, pr, load):
    base = 4 * sc[0]
    level = bl[...].astype(F32)
    for k in range(4):
        wet = wet_of(level, (base + k).astype(F32))
        for n, a in enumerate((u, v, b)):
            ext[4 * n + k, :, :TY] = a[k] * wet
    for i in range(12):
        ext[i, :, TY:] = hal[i]
    lev[:, :TY] = level
    lev[:, TY:] = hal[12]
    pressures(base, lambda k, r: ext[8 + k, r : r + 8, :], pr, load, TX)
    coriolis = coriolis_of(sc[1], total, (8, LANES))
    for q in range(0, 48, 16):
        halves = []
        for r in (q + 8, q + 16):
            rr = slice(r, r + 8)
            found = sums_of(sc, coriolis, lev[rr, :], lambda k: ext[k, rr, :], lambda k: ext[4 + k, rr, :], pr, load, r)
            for i, a in enumerate(found):
                sums[i, r - 8 : r, :] = a
            halves.append(found)
        for i in range(4):
            a = jnp.concatenate([halves[0][i], halves[1][i]], 0)
            high = a.astype(BF)
            send[i, q : q + 16, :] = high
            if i < 2:
                send[4 + i, q : q + 16, :] = (a - high.astype(F32)).astype(BF)


def rim_sums(total, sc, ready, u, v, b, bl, s, hal, low, high, sums, send, two, edge, ext, pr, load):
    base = 4 * sc[0]
    tall = 32
    for side, halo in ((0, low), (1, high)):
        own = slice(0, 16) if side == 0 else slice(TX - 16, TX)
        hr, orr = (slice(0, 16), slice(16, 32)) if side == 0 else (slice(16, 32), slice(0, 16))
        level = bl[own, :].astype(F32)
        for i in range(13):
            ext[i, hr, :] = halo[i].astype(F32)
            ext[i, orr, TY:] = hal[i, own, :]
        for k in range(4):
            wet = wet_of(level, (base + k).astype(F32))
            for n, a in enumerate((u, v, b)):
                ext[4 * n + k, orr, :TY] = a[k, own, :] * wet
        ext[12, orr, :TY] = level
        pressures(base, lambda k, r: ext[8 + k, r : r + 8, :], pr, load, tall)
        for ref in [pr.at[k] for k in range(4)] + [load]:
            if side == 0:
                ref[0:8, :] = jnp.zeros((8, LANES), F32)
            else:
                ref[40:48, :] = jnp.zeros((8, LANES), F32)
        coriolis = coriolis_of(sc[1], total, (8, LANES))
        for j in range(3):
            r = 8 * j + 8 * side
            rr = slice(r, r + 8)
            found = sums_of(sc, coriolis, ext[12, rr, :], lambda k: ext[k, rr, :], lambda k: ext[4 + k, rr, :], pr, load, r)
            for i, a in enumerate(found):
                sums[i, RIM * side + 8 * j : RIM * side + 8 * j + 8, :] = a
        more = halo[14].astype(F32)
        for i in range(8):
            if side == 0:
                edge[i, 0:8, :] = jnp.zeros((8, LANES), F32)
                edge[i, 8:32, :] = ext[i, 0:24, :]
                edge[i, 6:8, :] = more[2 * i : 2 * i + 2, :]
            else:
                edge[i, 32:56, :] = ext[i, 8:32, :]
                edge[i, 56:64, :] = jnp.zeros((8, LANES), F32)
                edge[i, 56:58, :] = more[2 * i : 2 * i + 2, :]
        at = slice(0, 16) if side == 0 else slice(80, 96)
        two[0, at, :] = halo[12].astype(F32)
        two[1, at, :] = halo[13].astype(F32)
    two[0, 16:80, :TY] = bl[...].astype(F32)
    two[1, 16:80, :TY] = s[...]
    for i in range(2):
        two[i, 16:80, TY:] = hal[12 + i]
    for i in range(4):
        send[i] = sums[i].astype(BF)


def own_part(total, sc, u, v, b, bl, hal, low, high, force, out, pr, load):
    base = 4 * sc[0]
    upper = jnp.where(sc[0] == 0, step_dt, 0.0)

    def b_rows(k, r):
        if r == 0:
            return low[8 + k].astype(F32)[8:16]
        if r == TX + 8:
            return high[8 + k].astype(F32)[0:8]
        at = slice(r - 8, r)
        wet = wet_of(bl[at, :].astype(F32), (base + k).astype(F32))
        return jnp.concatenate([b[k, at, :] * wet, hal[8 + k, at, :]], 1)

    pressures(base, b_rows, pr, load, TX + 16)
    coriolis = coriolis_of(sc[1], total, (8, LANES))[:, :TY]
    for r in range(0, TX, 8):
        rr = slice(r, r + 8)
        lev = bl[rr, :].astype(F32)
        for k in range(4):
            number = (base + k).astype(F32)
            wet = wet_of(lev, number)
            drag = jnp.where(lev == number + 1.0, drag_coef, 0.0)
            east, north = u[k, rr, :], v[k, rr, :]
            gx, gy = grads(pr.at[k], r + 8)
            te = coriolis * north - press_coef * gx[:, :TY] - drag * east
            tn = -coriolis * east - press_coef * gy[:, :TY] - drag * north
            at = slice(r + 20, r + 28)
            fe = jnp.where(upper > 0.0, force[k, at, :TY], 0.0)
            fn = jnp.where(upper > 0.0, force[4 + k, at, :TY], 0.0)
            out[k, rr, :] = wet * (east + step_dt * (te + fe))
            out[4 + k, rr, :] = wet * (north + step_dt * (tn + fn))


def substeps(total, sc, two, mid, rim, mid_in, rim_in, force, fin, send, lv, fx, fy, eb, nb, ae, an, es, ns, rel, c2):
    @pl.when(sc[0] == 0)
    def _():
        zero8 = jnp.zeros((8, LANES), F32)
        for ref in (lv, fx):
            ref[0:8, :] = zero8
            ref[ROWS + 8 : ROWS + 16, :] = zero8
        for r in range(0, ROWS, 8):
            rr = slice(r, r + 8)
            level = two[0, rr, :]
            depth = level + 0.125 * level * (level - 1.0)
            over = 1.0 / jnp.maximum(depth, 1.0)
            rel[rr, :] = depth * (1.0 / TOTAL_DEPTH)
            c2[rr, :] = jnp.where(level > 0.0, 0.5 * sub_dt * gravity, 0.0)
            middle = RIM <= r < ROWS - RIM
            at = r - RIM if middle else (r if r < RIM else r - 48)
            at = slice(at, at + 8)
            mine, theirs = (mid, mid_in) if middle else (rim, rim_in)
            pair, half = at.start // 16 * 16, at.start % 16

            def other(i):
                return theirs[i, pair : pair + 16, :].astype(F32)[half : half + 8]

            found = [mine[i, at, :] + other(i) for i in range(4)]
            if middle:
                found[:2] = [found[i] + other(4 + i) for i in range(2)]
            for k in range(4):
                weight = jnp.where(level > float(k), 1.0 + 0.25 * k, 0.0)
                found[0] = found[0] + weight * force[k, r + 4 : r + 12, :]
                found[1] = found[1] + weight * force[4 + k, r + 4 : r + 12, :]
            ae[rr, :] = sub_dt * found[0] * over
            an[rr, :] = sub_dt * found[1] * over
            e, n = found[2] * over, found[3] * over
            es[rr, :], ns[rr, :] = e, n
            eb[rr, :], nb[rr, :] = e, n
            lv[r + 8 : r + 16, :] = two[1, rr, :]
        inside = inside_of(sc[1], total, (8, LANES))

        def step(_, carry):
            for r in range(0, ROWS, 8):
                rr = slice(r, r + 8)
                here = lv[r + 8 : r + 16, :]
                dx = lv[r + 9 : r + 17, :] - lv[r + 7 : r + 15, :]
                dy = pltpu.roll(here, LANES - 1, 1) - pltpu.roll(here, 1, 1)
                c = c2[rr, :]
                e = eb[rr, :] + (ae[rr, :] - c * dx)
                n = nb[rr, :] + (an[rr, :] - c * dy)
                eb[rr, :] = e
                nb[rr, :] = n
                fx[r + 8 : r + 16, :] = rel[rr, :] * e
                fy[rr, :] = rel[rr, :] * n
            for r in range(0, ROWS, 8):
                rr = slice(r, r + 8)
                dx = fx[r + 9 : r + 17, :] - fx[r + 7 : r + 15, :]
                f = fy[rr, :]
                dy = pltpu.roll(f, LANES - 1, 1) - pltpu.roll(f, 1, 1)
                lv[r + 8 : r + 16, :] = inside * (lv[r + 8 : r + 16, :] - (0.5 * sub_dt) * (dx + dy))
            return carry

        lax.fori_loop(0, NSUB, step, 0)
        for q in range(0, TX, 16):
            r = q + HALO
            rr, at = slice(r, r + 16), slice(q, q + 16)
            fe = eb[rr, :TY] - es[rr, :TY] - (step_dt / sub_dt) * ae[rr, :TY]
            fn = nb[rr, :TY] - ns[rr, :TY] - (step_dt / sub_dt) * an[rr, :TY]
            fin[0, at, :], fin[1, at, :] = fe, fn
            slopes = []
            for i in (4, 5):
                pieces = []
                for p in (r, r + 8):
                    if RIM <= p < ROWS - RIM:
                        pieces.append(mid[i, p - RIM : p - RIM + 8, :TY])
                    else:
                        p = p if p < RIM else p - 48
                        pieces.append(rim[i, p : p + 8, :TY])
                slopes.append(jnp.concatenate(pieces, 0))
            send[0, at, :] = (fe - (step_dt * press_coef) * slopes[0]).astype(BF)
            send[1, at, :] = (fn - (step_dt * press_coef) * slopes[1]).astype(BF)
            level = lv[r + 8 : r + 24, :TY]
            high = level.astype(BF)
            send[2, at, :] = high
            send[3, at, :] = (level - high.astype(F32)).astype(BF)


def finish(sc, bl, fin, mine, theirs, own, east_out, north_out, surface_out):
    base = 4 * sc[0]
    upper = jnp.where(sc[0] == 0, 1.0, 0.0) > 0.0
    for r in range(0, TX, 16):
        rr = slice(r, r + 16)
        level = bl[rr, :].astype(F32)
        fe = jnp.where(upper, fin[0, rr, :], theirs[0, rr, :].astype(F32))
        fn = jnp.where(upper, fin[1, rr, :], theirs[1, rr, :].astype(F32))
        for k in range(4):
            wet = wet_of(level, (base + k).astype(F32))
            east_out[k, rr, :] = own[k, rr, :] + wet * fe
            north_out[k, rr, :] = own[4 + k, rr, :] + wet * fn
        parts = [jnp.where(upper, mine[i, rr, :].astype(F32), theirs[i, rr, :].astype(F32)) for i in (2, 3)]
        surface_out[rr, :] = parts[0] + parts[1]


def call(kernel, name, out_shape, n_in, scratch=(), in_specs=None, cost=None, grid=(), aliases=None, room=28):
    single = not isinstance(out_shape, (list, tuple))

    def placed(*refs):
        kernel((lax.axis_index("grp"), lax.axis_index("lat")), *refs)

    return pl.pallas_call(
        placed,
        name=name,
        grid=grid,
        out_shape=out_shape,
        in_specs=in_specs or [VMEM] * n_in,
        out_specs=VMEM if single else [VMEM] * len(out_shape),
        scratch_shapes=list(scratch),
        compiler_params=pltpu.CompilerParams(vmem_limit_bytes=room * 2**20),
        cost_estimate=cost,
        input_output_aliases=aliases or {},
    )


def with_total(kernel, total):
    return lambda sc, *refs: kernel(total, sc, *refs)


def micros(us):
    return pl.CostEstimate(flops=int(us * 1e6), bytes_accessed=int(us * 3e6), transcendentals=0)


def shifted(x, axis, by, ring):
    size = lax.axis_size(axis)
    pairs = [(i, (i + by) % size) for i in range(size) if ring or 0 <= i + by < size]
    return lax.ppermute(x, axis, pairs)


def local(u, v, b, wet_mask, bl, s, w_in, b_in, w_mid, b_mid, w_out):
    total = TY * lax.axis_size("lat")
    wide, half = pltpu.VMEM((2, 4, TX, 128), F32), sds((2, TX, 128), BF)
    to_down, to_up = call(
        pack_lat,
        "pack_lat",
        [half, half],
        6,
        [wide, wide, wide, pltpu.VMEM((2, TX, 128), jnp.int32), pltpu.VMEM((2, TX, 128), F32), pltpu.SemaphoreType.DMA((2, 5))],
        in_specs=[pl.BlockSpec(memory_space=pltpu.HBM)] * 5,
        room=60,
    )(u, v, b, bl, s)
    before = shifted(to_up, "lat", 1, False)
    after = shifted(to_down, "lat", -1, False)
    vb = [sds((192, 256), BF), sds((576, 256), BF), sds((192, 320), BF), sds((192, 128)), sds((192, 128)), TOKEN]
    *weights, ready = call(build_weights, "weights", vb, 5, [pltpu.VMEM((8, 8, 384), F32)], in_specs=[VMEM] * 5)(
        w_in, b_in[None, :], w_mid, b_mid[None, :], w_out
    )

    def rows(n, i, three):
        return [pl.BlockSpec((4, n, TY), lambda _: (0, i, 0))] * three + [pl.BlockSpec((n, TY), lambda _: (i, 0))] * (three - 1)

    out = sds((15, 16, LANES), BF)
    hal, down, up = call(
        pack_lon,
        "pack_lon",
        [sds((FIELDS, TX, 128)), out, out],
        20,
        [pltpu.VMEM((16, LANES), F32)],
        in_specs=[VMEM, VMEM, VMEM] + rows(16, 0, 3) + rows(16, 3, 3) + rows(8, 2, 2) + rows(8, 5, 2),
        grid=(1,),
    )(ready, before, after, u, v, b, bl, s, u, v, b, bl, s, u, v, bl, u, v, bl)
    low = shifted(up, "lon", 1, True)
    high = shifted(down, "lon", -1, True)
    mid, mid_send = call(
        with_total(middle_sums, total),
        "middle_sums",
        [sds((6, 48, LANES)), sds((6, 48, LANES), BF)],
        5,
        [
            pltpu.VMEM((12, TX, LANES), F32),
            pltpu.VMEM((TX, LANES), F32),
            pltpu.VMEM((4, TX + 16, LANES), F32),
            pltpu.VMEM((TX + 16, LANES), F32),
        ],
        cost=micros(2),
    )(u, v, b, bl, hal)
    mid_in = lax.ppermute(mid_send, "grp", [(1, 0)])
    inner, ready = call(
        with_total(interior, total),
        "interior",
        [sds((8, FORCED, LANES)), TOKEN],
        9,
        [
            pltpu.VMEM((8, TX, LANES), F32),
            pltpu.VMEM((62 * 32, LANES), BF),
            pltpu.VMEM((62 * 32, LANES), BF),
            pltpu.VMEM((60 * 32, LANES), BF),
        ],
        cost=micros(7),
    )(u, v, bl, hal, *weights)
    rim, rim_send, two, edge = call(
        with_total(rim_sums, total),
        "rim_sums",
        [sds((6, 48, LANES)), sds((4, 48, LANES), BF), sds((2, ROWS, LANES)), sds((8, 64, LANES))],
        9,
        [pltpu.VMEM((13, 32, LANES), F32), pltpu.VMEM((4, 48, LANES), F32), pltpu.VMEM((48, LANES), F32)],
        cost=micros(2),
    )(ready, u, v, b, bl, s, hal, low, high)
    rim_in = lax.ppermute(rim_send, "grp", [(1, 0)])
    force = call(
        with_total(edges, total),
        "edges",
        sds((8, FORCED, LANES)),
        7,
        [pltpu.VMEM((52 * 32, LANES), BF), pltpu.VMEM((52 * 32, LANES), BF), pltpu.VMEM((55 * 32, LANES), BF)],
        cost=micros(6),
        aliases={6: 0},
    )(edge, *weights, inner)
    plane = pltpu.VMEM((ROWS, LANES), F32)
    tall = pltpu.VMEM((ROWS + 16, LANES), F32)
    fin, fin_send = call(
        with_total(substeps, total),
        "substeps",
        [sds((2, TX, TY)), sds((4, TX, TY), BF)],
        6,
        [tall, tall] + [plane] * 9,
        cost=micros(5),
    )(two, mid, rim, mid_in, rim_in, force)
    fin_in = lax.ppermute(fin_send, "grp", [(0, 1)])
    own = call(
        with_total(own_part, total),
        "own_part",
        sds((8, TX, TY)),
        8,
        [pltpu.VMEM((4, 96, LANES), F32), pltpu.VMEM((96, LANES), F32)],
        cost=micros(2),
    )(u, v, b, bl, hal, low, high, force)
    return tuple(
        call(finish, "finish", [sds((4, TX, TY)), sds((4, TX, TY)), sds((TX, TY))], 5, cost=micros(2))(
            bl, fin, fin_send, fin_in, own
        )
    )


def solution(mesh):
    tile = P("grp", "lon", "lat")
    flat = P("lon", "lat")
    return jax.shard_map(
        local,
        mesh=mesh,
        in_specs=(tile, tile, tile, tile, flat, flat, P(), P(), P(), P(), P()),
        out_specs=(tile, tile, flat),
        check_vma=False,
    )
```

```python
import jax
import jax.numpy as jnp
from jax import lax
from jax.experimental import pallas as pl
from jax.experimental.pallas import tpu as pltpu
from jax.sharding import PartitionSpec as P

NSUB = 8
TX, TY = 64, 512
LANES = 640
ROWS = 96
HALO = 16
RIM = 24
EDGE = 18
FORCED = 104
FIELDS = 14
F32 = jnp.float32
BF = jnp.bfloat16

coriolis_base = 0.6
coriolis_slope = 0.8
press_coef = 0.3
drag_coef = 0.5
step_dt = 0.2
closure_coef = 0.5
gravity = 1.0
sub_dt = 0.4
TOTAL_DEPTH = 15.0

TOKEN = jax.ShapeDtypeStruct((8, 128), jnp.float32)
VMEM = pl.BlockSpec(memory_space=pltpu.VMEM)


def sds(shape, dtype=F32):
    return jax.ShapeDtypeStruct(shape, dtype)


def wet_of(bl, level):
    return jnp.where(bl > level, 1.0, 0.0)


def latitudes(lat, shape):
    lane = lax.broadcasted_iota(jnp.int32, shape, len(shape) - 1)
    return lat * TY + jnp.where(lane < TY + 64, lane, lane - LANES)


def inside_of(lat, total, shape):
    y = latitudes(lat, shape)
    return jnp.where((y >= 0) & (y < total), 1.0, 0.0)


def pack_lat(sc, u, v, b, l, s, *refs):
    raw, to_down, to_up, made = refs[:5], refs[5], refs[6], refs[7:12]
    ub, vb, bb, lb, sb, sem = refs[12:18]
    held, spread, weight_sem = refs[18:23], refs[23], refs[24]
    base = 4 * sc[0]
    lane = lax.broadcasted_iota(jnp.int32, (TX, 128), 1)
    copies = []
    for side, at in enumerate((0, TY - 128)):
        for n, (src, dst) in enumerate(((u, ub), (v, vb), (b, bb))):
            copies.append(pltpu.make_async_copy(src.at[:, :, at : at + 128], dst.at[side], sem.at[side, n]))
        for n, (src, dst) in enumerate(((l, lb), (s, sb))):
            copies.append(pltpu.make_async_copy(src.at[:, at : at + 128], dst.at[side], sem.at[side, 3 + n]))
    more = [pltpu.make_async_copy(src, dst, weight_sem.at[n]) for n, (src, dst) in enumerate(zip(raw, held))]
    for copy in copies + more:
        copy.start()

    def fields(side):
        bl = lb[side].astype(F32)
        wets = [wet_of(bl, (base + k).astype(F32)) for k in range(4)]
        for a in (ub, vb, bb):
            for k in range(4):
                yield a[side, k] * wets[k]
        yield bl
        yield sb[side]

    for side, (out, origin) in enumerate(((to_down, 0), (to_up, 128 - EDGE))):
        for copy in copies[5 * side : 5 * side + 5]:
            copy.wait()
        for i, field in enumerate(fields(side)):
            tile, place = divmod(i, 7)
            if place == 0:
                acc = jnp.zeros((TX, 128), F32)
            moved = pltpu.roll(field, (EDGE * place - origin) % 128, 1)
            acc = jnp.where((lane >= EDGE * place) & (lane < EDGE * (place + 1)), moved, acc)
            if place == 6:
                out[tile] = acc.astype(BF)
    for copy in more:
        copy.wait()
    build_weights(*held, *made, spread)


def pack_lon(total, sc, summed, before, after, *refs):
    tops, bots, extra_t, extra_b = refs[0:5], refs[5:10], refs[10:13], refs[13:16]
    hal, to_down, to_up, work = refs[16:]
    base = 4 * sc[0]
    lane = lax.broadcasted_iota(jnp.int32, (TX, 128), 1)
    low_from = jnp.where(sc[1] > 0, 128 - EDGE, 128)
    high_to = jnp.where(sc[1] < total // TY - 1, EDGE, 0)
    for tile in range(2):
        low, high = before[tile].astype(F32), after[tile].astype(F32)
        for place in range(7):
            a = pltpu.roll(high, (-EDGE * place) % 128, 1)
            b = pltpu.roll(low, (128 - EDGE - EDGE * place) % 128, 1)
            hal[tile * 7 + place] = jnp.where(lane < high_to, a, jnp.where(lane >= low_from, b, 0.0))
    for out, (u, v, b, l, s), row in ((to_down, tops, 0), (to_up, bots, TX - 16)):
        bl = l[...].astype(F32)
        for k in range(4):
            wet = wet_of(bl, (base + k).astype(F32))
            for n, a in enumerate((u, v, b)):
                out[4 * n + k, :, :TY] = (a[k] * wet).astype(BF)
        out[12, :, :TY] = bl.astype(BF)
        out[13, :, :TY] = s[...].astype(BF)
        for i in range(FIELDS):
            out[i, :, TY:] = hal[i, row : row + 16, :].astype(BF)
    for out, (u, v, l), first, row in ((to_down, extra_t, 0, 16), (to_up, extra_b, 6, 46)):
        bl = l[first : first + 2, :].astype(F32)
        for k in range(4):
            wet = wet_of(bl, (base + k).astype(F32))
            for n, a in enumerate((u, v)):
                work[2 * (4 * n + k) : 2 * (4 * n + k) + 2, :TY] = a[k, first : first + 2, :] * wet
        for i in range(8):
            work[2 * i : 2 * i + 2, TY:] = hal[i, row : row + 2, :]
        out[14] = work[...].astype(BF)


def build_weights(w_in, b_in, w_mid, b_mid, w_out, w1, w2, w3, b1, b2, spread):
    def across(parts, rows, cols):
        rows_all = sum(p.shape[0] for p in parts)
        full = jnp.concatenate(parts + [jnp.zeros((128 - rows_all, 128), F32)], 0)
        return full.T[:rows, :]

    def wide(a):
        return jnp.concatenate([a, jnp.zeros((a.shape[0], 128 - a.shape[1]), F32)], 1)

    zero8 = jnp.zeros((8, 128), F32)
    parts = []
    for a in range(3):
        parts += [wide(w_in[3 * a + b].astype(F32)) for b in range(3)] + [zero8]
    first = across(parts, 32, 96)
    first = jnp.concatenate([first, jnp.zeros((32, 128), F32)], 1)
    for p in range(6):
        w1[32 * p : 32 * p + 32, :] = pltpu.roll(first, 32 * p, 1).astype(BF)
    for b in range(3):
        mid = across([wide(w_mid[3 * a + b].astype(F32)) for a in range(3)], 32, 96)
        mid = jnp.concatenate([mid, jnp.zeros((32, 128), F32)], 1)
        for p in range(6):
            w2[192 * b + 32 * p : 192 * b + 32 * p + 32, :] = pltpu.roll(mid, 32 * p, 1).astype(BF)
        last = jnp.concatenate([w_out[3 * a + b].astype(F32) for a in range(3)] + [jnp.zeros((8, 288), F32)], 1)
        for p in range(8):
            spread[:, p, :] = pltpu.roll(last, 32 * p, 1)
        w3[64 * b : 64 * b + 64, :] = spread[...].reshape(64, 384)[:, :320].astype(BF)
    eye = lax.broadcasted_iota(jnp.int32, (32, 32), 0) == lax.broadcasted_iota(jnp.int32, (32, 32), 1)
    for src, dst in ((b_in, b1), (b_mid, b2)):
        column = jnp.sum(jnp.where(eye, src[...], 0.0), 1, keepdims=True)
        for p in range(6):
            dst[32 * p : 32 * p + 32, :] = jnp.broadcast_to(column, (32, 128))


def load_slots(up, start, count, in0, at):
    for i in range(count):
        c = up[:, start + i, :]
        r = 32 * (at + i)
        in0[r : r + 16, :] = jnp.concatenate([pltpu.roll(c, 1, 1), c], 0).astype(BF)
        in0[r + 16 : r + 32, :] = jnp.concatenate([pltpu.roll(c, LANES - 1, 1), jnp.zeros_like(c)], 0).astype(BF)


def closure(in0, act1, act2, weights, inside, parts, store):
    w1, w2, w3, b1, b2 = weights
    bias1, bias2 = b1[:, :1], b2[:, :1]

    def combined(o, m):
        return pltpu.roll(o[:m], 1, 1) + o[m : 2 * m] + pltpu.roll(o[2 * m :], LANES - 1, 1)

    for s1, _, _, n1, _, _ in parts:
        for j in range(n1):
            r = 32 * (s1 + 6 * j)
            o = jnp.dot(w1[...], in0[r : r + 256, :], preferred_element_type=F32)
            act1[r : r + 192, :] = (jnp.maximum(o + bias1, 0.0) * inside).astype(BF)
    for s1, s2, shift, _, n2, _ in parts:
        for j in range(n2):
            r, to = 32 * (s1 + 6 * j), 32 * (s2 + shift + 6 * j)
            o = combined(jnp.dot(w2[...], act1[r : r + 256, :], preferred_element_type=F32), 192)
            act2[to : to + 192, :] = (jnp.maximum(o + bias2, 0.0) * inside).astype(BF)
    for part, (_, s2, _, _, _, n3) in enumerate(parts):
        for j in range(n3):
            r = 32 * (s2 + 8 * j)
            o = combined(jnp.dot(w3[...], act2[r : r + 320, :], preferred_element_type=F32), 64)
            store(part, j, (closure_coef * o).astype(BF).astype(F32).reshape(8, 8, LANES))


def interior(total, sc, u, v, bl, hal, w1, w2, w3, b1, b2, out, done, up, in0, act1, act2):
    done[...] = jnp.zeros_like(done)

    @pl.when(sc[0] == 0)
    def _():
        level = bl[...].astype(F32)
        for k in range(4):
            wet = wet_of(level, float(k))
            up[k, :, :TY] = u[k] * wet
            up[4 + k, :, :TY] = v[k] * wet
        for i in range(8):
            up[i, :, TY:] = hal[i]
        load_slots(up, 1, 62, in0, 0)
        act1[1920:1984, :] = jnp.zeros((64, LANES), BF)

        def store(part, j, f):
            out[:, 24 + 8 * j : 32 + 8 * j, :] = f

        closure(in0, act1, act2, (w1, w2, w3, b1, b2), inside_of(sc[1], total, (1, LANES)), [(0, 0, 0, 10, 10, 7)], store)


def edges(total, sc, edge, w1, w2, w3, b1, b2, inner, out, in0, act1, act2):
    @pl.when(sc[0] == 0)
    def _():
        for at, start in ((0, 6), (26, 33)):
            load_slots(edge, start, 26, in0, at)
            act1[32 * at + 768 : 32 * at + 832, :] = jnp.zeros((64, LANES), BF)
        act2[0:160, :] = jnp.zeros((160, LANES), BF)
        act2[29 * 32 + 768 :, :] = jnp.zeros((64, LANES), BF)

        def store(part, j, f):
            row = 80 * part + 8 * j
            out[:, row : row + 8, :] = f

        parts = [(0, 0, 5, 4, 4, 3), (26, 29, 0, 4, 4, 3)]
        closure(in0, act1, act2, (w1, w2, w3, b1, b2), inside_of(sc[1], total, (1, LANES)), parts, store)


def pressures(base, b_rows, pr, load, rows):
    for r in range(0, rows, 8):
        run = jnp.zeros((8, pr.shape[2]), F32)
        for k in range(4):
            weighted = b_rows(k, r) * (1.0 + 0.25 * (base + k).astype(F32))
            pr[k, r + 8 : r + 16, :] = run + 0.5 * weighted
            run = run + weighted
        load[r + 8 : r + 16, :] = run


def grads(ref, r):
    here = ref[r + 8 : r + 16, :]
    gx = (ref[r + 9 : r + 17, :] - ref[r + 7 : r + 15, :]) * 0.5
    gy = (pltpu.roll(here, here.shape[1] - 1, 1) - pltpu.roll(here, 1, 1)) * 0.5
    return gx, gy


def open_grads(ref, r):
    here = ref[r + 8 : r + 16, :]
    lane = lax.broadcasted_iota(jnp.int32, here.shape, 1)
    gx = (ref[r + 9 : r + 17, :] - ref[r + 7 : r + 15, :]) * 0.5
    right = jnp.where(lane == TY - 1, 0.0, pltpu.roll(here, TY - 1, 1))
    left = jnp.where(lane == 0, 0.0, pltpu.roll(here, 1, 1))
    return gx, (right - left) * 0.5


def coriolis_of(lat, total, shape):
    return coriolis_base + coriolis_slope * (latitudes(lat, shape).astype(F32) * (1.0 / total) - 0.5)


def sums_of(sc, coriolis, level, east, north, pr, load, r, grads=grads):
    base = 4 * sc[0]
    te = jnp.zeros(level.shape, F32)
    tn, us, vs = te, te, te
    for k in range(4):
        number = (base + k).astype(F32)
        thick = 1.0 + 0.25 * number
        weight = jnp.where(level > number, thick, 0.0)
        drag = jnp.where(level == number + 1.0, drag_coef, 0.0)
        e, n = east(k), north(k)
        gx, gy = grads(pr.at[k], r)
        te = te + weight * (coriolis * n - press_coef * gx - drag * e)
        tn = tn + weight * (-coriolis * e - press_coef * gy - drag * n)
        us = us + thick * e
        vs = vs + thick * n
    below = jnp.zeros(level.shape, F32)
    for k in range(4, 8):
        below = below + jnp.where(level > float(k), 1.0 + 0.25 * k, 0.0)
    gx, gy = grads(load, r)
    below = below * (press_coef * jnp.where(sc[0] == 0, 1.0, 0.0))
    return te - below * gx, tn - below * gy, us, vs, gx, gy


def closed(pr, load):
    for ref in [pr.at[k] for k in range(4)] + [load]:
        end = ref.shape[0]
        ref[0:8, :] = jnp.zeros((8, ref.shape[1]), F32)
        ref[end - 8 : end, :] = jnp.zeros((8, ref.shape[1]), F32)


def middle_sums(total, sc, u, v, b, bl, s, sums, send, done, pr, load):
    done[...] = jnp.zeros_like(done)
    base = 4 * sc[0]

    def wet(k, rr):
        return wet_of(bl[rr, :].astype(F32), (base + k).astype(F32))

    def b_rows(k, r):
        rr = slice(r, r + 8)
        return b[k, rr, :] * wet(k, rr)

    pressures(base, b_rows, pr, load, TX)
    closed(pr, load)
    coriolis = coriolis_of(sc[1], total, (8, LANES))[:, :TY]
    for q in range(0, TX, 16):
        halves = []
        for r in (q, q + 8):
            rr = slice(r, r + 8)
            level = bl[rr, :].astype(F32)
            found = sums_of(
                sc, coriolis, level, lambda k: u[k, rr, :] * wet(k, rr), lambda k: v[k, rr, :] * wet(k, rr), pr, load, r, open_grads
            )
            for i, a in enumerate(found):
                sums[i, rr, :] = a
            halves.append(found)
        for i in range(4):
            a = jnp.concatenate([halves[0][i], halves[1][i]], 0)
            send[i, q : q + 16, :] = a.astype(BF)


def seam_sums(total, sc, u, v, b, bl, hal, sums, ext, pr, load):
    base = 4 * sc[0]
    last, first = slice(TY - 128, TY), slice(0, 128)

    def three(a, outer, b):
        return jnp.concatenate([a, outer, b], 1)

    for r in range(0, TX, 8):
        rr = slice(r, r + 8)
        levels = [bl[rr, at].astype(F32) for at in (last, first)]
        ext[12, rr, :] = three(levels[0], hal[12, rr, :], levels[1])
        for k in range(4):
            wets = [wet_of(level, (base + k).astype(F32)) for level in levels]
            for n, a in enumerate((u, v, b)):
                ext[4 * n + k, rr, :] = three(a[k, rr, last] * wets[0], hal[4 * n + k, rr, :], a[k, rr, first] * wets[1])
    pressures(base, lambda k, r: ext[8 + k, r : r + 8, :], pr, load, TX)
    closed(pr, load)
    whole = coriolis_of(sc[1], total, (8, LANES))
    coriolis = three(whole[:, last], whole[:, TY:], whole[:, first])
    for r in range(0, TX, 8):
        rr = slice(r, r + 8)
        found = sums_of(sc, coriolis, ext[12, rr, :], lambda k: ext[k, rr, :], lambda k: ext[4 + k, rr, :], pr, load, r)
        for i, a in enumerate(found):
            sums[i, rr, :] = a


def rim_sums(total, sc, ready, u, v, b, bl, s, hal, low, high, seam, sums, send, two, edge, ext, pr, load):
    base = 4 * sc[0]
    tall = 32
    for side, halo in ((0, low), (1, high)):
        own = slice(0, 16) if side == 0 else slice(TX - 16, TX)
        hr, orr = (slice(0, 16), slice(16, 32)) if side == 0 else (slice(16, 32), slice(0, 16))
        level = bl[own, :].astype(F32)
        for i in range(13):
            ext[i, hr, :] = halo[i].astype(F32)
            ext[i, orr, TY:] = hal[i, own, :]
        for k in range(4):
            wet = wet_of(level, (base + k).astype(F32))
            for n, a in enumerate((u, v, b)):
                ext[4 * n + k, orr, :TY] = a[k, own, :] * wet
        ext[12, orr, :TY] = level
        pressures(base, lambda k, r: ext[8 + k, r : r + 8, :], pr, load, tall)
        for ref in [pr.at[k] for k in range(4)] + [load]:
            if side == 0:
                ref[0:8, :] = jnp.zeros((8, LANES), F32)
            else:
                ref[40:48, :] = jnp.zeros((8, LANES), F32)
        coriolis = coriolis_of(sc[1], total, (8, LANES))
        for j in range(3):
            r = 8 * j + 8 * side
            rr = slice(r, r + 8)
            found = sums_of(sc, coriolis, ext[12, rr, :], lambda k: ext[k, rr, :], lambda k: ext[4 + k, rr, :], pr, load, r)
            for i, a in enumerate(found):
                sums[i, RIM * side + 8 * j : RIM * side + 8 * j + 8, :] = a
        more = halo[14].astype(F32)
        for i in range(8):
            if side == 0:
                edge[i, 0:8, :] = jnp.zeros((8, LANES), F32)
                edge[i, 8:32, :] = ext[i, 0:24, :]
                edge[i, 6:8, :] = more[2 * i : 2 * i + 2, :]
            else:
                edge[i, 32:56, :] = ext[i, 8:32, :]
                edge[i, 56:64, :] = jnp.zeros((8, LANES), F32)
                edge[i, 56:58, :] = more[2 * i : 2 * i + 2, :]
        at = slice(0, 16) if side == 0 else slice(80, 96)
        two[0, at, :] = halo[12].astype(F32)
        two[1, at, :] = halo[13].astype(F32)
    two[0, 16:80, :TY] = bl[...].astype(F32)
    two[1, 16:80, :TY] = s[...]
    for i in range(2):
        two[i, 16:80, TY:] = hal[12 + i]
    lane = lax.broadcasted_iota(jnp.int32, (16, 128), 1)
    for i in range(4):
        for side in range(2):
            at = slice(0, 16) if side == 0 else slice(32, 48)
            packed = sums[i, at, TY:]
            for turn in range(2):
                base = 16 + 34 * turn
                own = slice(16 * (2 * turn + side), 16 * (2 * turn + side) + 16)
                outer, before, after = seam[i, own, 128:256], seam[i, own, 0:128], seam[i, own, 256:384]
                packed = jnp.where((lane >= base) & (lane < base + 16), pltpu.roll(outer, base, 1), packed)
                packed = jnp.where((lane >= base + 16) & (lane < base + 32), pltpu.roll(outer, base + 32, 1), packed)
                packed = jnp.where(lane == base + 32, pltpu.roll(before, base + 33, 1), packed)
                packed = jnp.where(lane == base + 33, pltpu.roll(after, base + 33, 1), packed)
            send[2 * i + side, :, :TY] = sums[i, at, :TY].astype(BF)
            send[2 * i + side, :, TY:] = packed.astype(BF)
    ends = [sums[i, row : row + 1, :] for i in range(4) for row in (16, 31)]
    send[8] = jnp.concatenate(ends + [jnp.zeros((8, LANES), F32)], 0).astype(BF)


def own_part(total, sc, u, v, b, bl, hal, low, high, force, out, pr, load):
    base = 4 * sc[0]
    upper = jnp.where(sc[0] == 0, step_dt, 0.0)

    def b_rows(k, r):
        if r == 0:
            return low[8 + k].astype(F32)[8:16]
        if r == TX + 8:
            return high[8 + k].astype(F32)[0:8]
        at = slice(r - 8, r)
        wet = wet_of(bl[at, :].astype(F32), (base + k).astype(F32))
        return jnp.concatenate([b[k, at, :] * wet, hal[8 + k, at, :]], 1)

    pressures(base, b_rows, pr, load, TX + 16)
    coriolis = coriolis_of(sc[1], total, (8, LANES))[:, :TY]
    for r in range(0, TX, 8):
        rr = slice(r, r + 8)
        lev = bl[rr, :].astype(F32)
        for k in range(4):
            number = (base + k).astype(F32)
            wet = wet_of(lev, number)
            drag = jnp.where(lev == number + 1.0, drag_coef, 0.0)
            east, north = u[k, rr, :], v[k, rr, :]
            gx, gy = grads(pr.at[k], r + 8)
            te = coriolis * north - press_coef * gx[:, :TY] - drag * east
            tn = -coriolis * east - press_coef * gy[:, :TY] - drag * north
            at = slice(r + 20, r + 28)
            fe = jnp.where(upper > 0.0, force[k, at, :TY], 0.0)
            fn = jnp.where(upper > 0.0, force[4 + k, at, :TY], 0.0)
            out[k, rr, :] = wet * (east + step_dt * (te + fe))
            out[4 + k, rr, :] = wet * (north + step_dt * (tn + fn))


def substeps(total, sc, two, mid, seam, rim, mid_in, rim_in, force, fin, send, lv, fx, fy, eb, nb, ae, an, es, ns, rel, c2):
    @pl.when(sc[0] == 0)
    def _():
        zero8 = jnp.zeros((8, LANES), F32)
        lane = lax.broadcasted_iota(jnp.int32, (8, 128), 1)

        def ended(i, at, outer):
            first = jnp.where(lane == 0, seam[i, at, 256:384], mid[i, at, 0:128])
            last = jnp.where(lane == 127, seam[i, at, 0:128], mid[i, at, TY - 128 :])
            pieces = [first, mid[i, at, 128 : TY - 128], last]
            return jnp.concatenate(pieces + [seam[i, at, 128:256]] if outer else pieces, 1)

        for ref in (lv, fx):
            ref[0:8, :] = zero8
            ref[ROWS + 8 : ROWS + 16, :] = zero8
        for r in range(0, ROWS, 8):
            rr = slice(r, r + 8)
            level = two[0, rr, :]
            depth = level + 0.125 * level * (level - 1.0)
            over = 1.0 / jnp.maximum(depth, 1.0)
            rel[rr, :] = depth * (1.0 / TOTAL_DEPTH)
            c2[rr, :] = jnp.where(level > 0.0, 0.5 * sub_dt * gravity, 0.0)
            middle = RIM <= r < ROWS - RIM
            at = r - RIM if middle else (r if r < RIM else r - 48)
            at = slice(at, at + 8)
            x = r - HALO
            found = []
            for i in range(4):
                own = ended(i, slice(x, x + 8), True) if middle else rim[i, at, :]
                if not 0 <= x < TX:
                    row = r % 16
                    found.append(own + rim_in[2 * i + (x > 0), :, :].astype(F32)[row : row + 8])
                    continue
                turn, half = x // 32, x % 16
                base = 16 + 34 * turn
                beyond = rim_in[2 * i + x // 16 % 2, :, TY:].astype(F32)[half : half + 8]
                theirs = mid_in[i, x - half : x - half + 16, :].astype(F32)[half : half + 8]
                outer = jnp.where(lane < 16, pltpu.roll(beyond, 128 - base, 1), pltpu.roll(beyond, 96 - base, 1))
                first = jnp.where(lane == 0, pltpu.roll(beyond, 95 - base, 1), theirs[:, 0:128])
                last = jnp.where(lane == 127, pltpu.roll(beyond, 95 - base, 1), theirs[:, TY - 128 :])
                theirs = jnp.concatenate([first, theirs[:, 128 : TY - 128], last, outer], 1)
                if x in (0, TX - 8):
                    end = rim_in[8].astype(F32)[2 * i + (x > 0) : 2 * i + (x > 0) + 1]
                    row = lax.broadcasted_iota(jnp.int32, (8, LANES), 0)
                    theirs = jnp.where(row == (0 if x == 0 else 7), end, theirs)
                found.append(own + theirs)
            for k in range(4):
                weight = jnp.where(level > float(k), 1.0 + 0.25 * k, 0.0)
                found[0] = found[0] + weight * force[k, r + 4 : r + 12, :]
                found[1] = found[1] + weight * force[4 + k, r + 4 : r + 12, :]
            ae[rr, :] = sub_dt * found[0] * over
            an[rr, :] = sub_dt * found[1] * over
            e, n = found[2] * over, found[3] * over
            es[rr, :], ns[rr, :] = e, n
            eb[rr, :], nb[rr, :] = e, n
            lv[r + 8 : r + 16, :] = two[1, rr, :]
        inside = inside_of(sc[1], total, (8, LANES))

        def step(first, carry):
            for r in range(first, ROWS - first, 8):
                rr = slice(r, r + 8)
                here = lv[r + 8 : r + 16, :]
                dx = lv[r + 9 : r + 17, :] - lv[r + 7 : r + 15, :]
                dy = pltpu.roll(here, LANES - 1, 1) - pltpu.roll(here, 1, 1)
                c = c2[rr, :]
                e = eb[rr, :] + (ae[rr, :] - c * dx)
                n = nb[rr, :] + (an[rr, :] - c * dy)
                eb[rr, :] = e
                nb[rr, :] = n
                fx[r + 8 : r + 16, :] = rel[rr, :] * e
                fy[rr, :] = rel[rr, :] * n
            for r in range(first, ROWS - first, 8):
                rr = slice(r, r + 8)
                dx = fx[r + 9 : r + 17, :] - fx[r + 7 : r + 15, :]
                f = fy[rr, :]
                dy = pltpu.roll(f, LANES - 1, 1) - pltpu.roll(f, 1, 1)
                lv[r + 8 : r + 16, :] = inside * (lv[r + 8 : r + 16, :] - (0.5 * sub_dt) * (dx + dy))
            return carry

        lax.fori_loop(0, NSUB // 2, lambda _, carry: step(0, carry), 0)
        lax.fori_loop(0, NSUB // 2, lambda _, carry: step(8, carry), 0)
        for q in range(0, TX, 16):
            r = q + HALO
            rr, at = slice(r, r + 16), slice(q, q + 16)
            fe = eb[rr, :TY] - es[rr, :TY] - (step_dt / sub_dt) * ae[rr, :TY]
            fn = nb[rr, :TY] - ns[rr, :TY] - (step_dt / sub_dt) * an[rr, :TY]
            fin[0, at, :], fin[1, at, :] = fe, fn
            slopes = []
            for i in (4, 5):
                pieces = []
                for p in (r, r + 8):
                    if RIM <= p < ROWS - RIM:
                        pieces.append(ended(i, slice(p - HALO, p - HALO + 8), False))
                    else:
                        p = p if p < RIM else p - 48
                        pieces.append(rim[i, p : p + 8, :TY])
                slopes.append(jnp.concatenate(pieces, 0))
            send[0, at, :] = (fe - (step_dt * press_coef) * slopes[0]).astype(BF)
            send[1, at, :] = (fn - (step_dt * press_coef) * slopes[1]).astype(BF)
            level = lv[r + 8 : r + 24, :TY]
            high = level.astype(BF)
            send[2, at, :] = high
            send[3, at, :] = (level - high.astype(F32)).astype(BF)


def finish(sc, bl, fin, mine, theirs, own, east_out, north_out, surface_out):
    base = 4 * sc[0]
    upper = jnp.where(sc[0] == 0, 1.0, 0.0) > 0.0
    for r in range(0, TX, 16):
        rr = slice(r, r + 16)
        level = bl[rr, :].astype(F32)
        fe = jnp.where(upper, fin[0, rr, :], theirs[0, rr, :].astype(F32))
        fn = jnp.where(upper, fin[1, rr, :], theirs[1, rr, :].astype(F32))
        for k in range(4):
            wet = wet_of(level, (base + k).astype(F32))
            east_out[k, rr, :] = own[k, rr, :] + wet * fe
            north_out[k, rr, :] = own[4 + k, rr, :] + wet * fn
        parts = [jnp.where(upper, mine[i, rr, :].astype(F32), theirs[i, rr, :].astype(F32)) for i in (2, 3)]
        surface_out[rr, :] = parts[0] + parts[1]


def call(kernel, name, out_shape, n_in, scratch=(), in_specs=None, cost=None, grid=(), aliases=None, room=28):
    single = not isinstance(out_shape, (list, tuple))

    def placed(*refs):
        kernel((lax.axis_index("grp"), lax.axis_index("lat")), *refs)

    return pl.pallas_call(
        placed,
        name=name,
        grid=grid,
        out_shape=out_shape,
        in_specs=in_specs or [VMEM] * n_in,
        out_specs=VMEM if single else [VMEM] * len(out_shape),
        scratch_shapes=list(scratch),
        compiler_params=pltpu.CompilerParams(vmem_limit_bytes=room * 2**20),
        cost_estimate=cost,
        input_output_aliases=aliases or {},
    )


def with_total(kernel, total):
    return lambda sc, *refs: kernel(total, sc, *refs)


def micros(us):
    return pl.CostEstimate(flops=int(us * 1e6), bytes_accessed=int(us * 3e6), transcendentals=0)


def shifted(x, axis, by):
    size = lax.axis_size(axis)
    return lax.ppermute(x, axis, [(i, (i + by) % size) for i in range(size)])


def local(u, v, b, wet_mask, bl, s, w_in, b_in, w_mid, b_mid, w_out):
    total = TY * lax.axis_size("lat")
    wide, half = pltpu.VMEM((2, 4, TX, 128), F32), sds((2, TX, 128), BF)
    made = [sds((192, 256), BF), sds((576, 256), BF), sds((192, 320), BF), sds((192, 128)), sds((192, 128))]
    to_down, to_up, *weights = call(
        pack_lat,
        "pack_lat",
        [half, half] + made,
        10,
        [
            wide,
            wide,
            wide,
            pltpu.VMEM((2, TX, 128), jnp.int32),
            pltpu.VMEM((2, TX, 128), F32),
            pltpu.SemaphoreType.DMA((2, 5)),
            pltpu.VMEM((9, 8, 32), BF),
            pltpu.VMEM((1, 32), F32),
            pltpu.VMEM((9, 32, 32), BF),
            pltpu.VMEM((1, 32), F32),
            pltpu.VMEM((9, 8, 32), BF),
            pltpu.VMEM((8, 8, 384), F32),
            pltpu.SemaphoreType.DMA((5,)),
        ],
        in_specs=[pl.BlockSpec(memory_space=pltpu.HBM)] * 10,
        room=60,
    )(u, v, b, bl, s, w_in, b_in[None, :], w_mid, b_mid[None, :], jnp.swapaxes(w_out, 1, 2))
    before = shifted(to_up, "lat", 1)
    after = shifted(to_down, "lat", -1)

    mid, mid_send, summed = call(
        with_total(middle_sums, total),
        "middle_sums",
        [sds((6, TX, TY)), sds((4, TX, TY), BF), TOKEN],
        5,
        [pltpu.VMEM((4, TX + 16, TY), F32), pltpu.VMEM((TX + 16, TY), F32)],
        cost=micros(1),
    )(u, v, b, bl, s)
    mid_in = shifted(mid_send, "grp", 1)

    def rows(n, i, three):
        return [pl.BlockSpec((4, n, TY), lambda _: (0, i, 0))] * three + [pl.BlockSpec((n, TY), lambda _: (i, 0))] * (three - 1)

    out = sds((15, 16, LANES), BF)
    hal, down, up = call(
        with_total(pack_lon, total),
        "pack_lon",
        [sds((FIELDS, TX, 128)), out, out],
        19,
        [pltpu.VMEM((16, LANES), F32)],
        in_specs=[VMEM, VMEM, VMEM] + rows(16, 0, 3) + rows(16, 3, 3) + rows(8, 2, 2) + rows(8, 5, 2),
        grid=(1,),
    )(summed, before, after, u, v, b, bl, s, u, v, b, bl, s, u, v, bl, u, v, bl)
    low = shifted(up, "lon", 1)
    high = shifted(down, "lon", -1)
    seam = call(
        with_total(seam_sums, total),
        "seam_sums",
        sds((6, TX, 384)),
        5,
        [pltpu.VMEM((13, TX, 384), F32), pltpu.VMEM((4, TX + 16, 384), F32), pltpu.VMEM((TX + 16, 384), F32)],
        cost=micros(1),
    )(u, v, b, bl, hal)
    inner, ready = call(
        with_total(interior, total),
        "interior",
        [sds((8, FORCED, LANES)), TOKEN],
        9,
        [
            pltpu.VMEM((8, TX, LANES), F32),
            pltpu.VMEM((62 * 32, LANES), BF),
            pltpu.VMEM((62 * 32, LANES), BF),
            pltpu.VMEM((60 * 32, LANES), BF),
        ],
        cost=micros(7),
    )(u, v, bl, hal, *weights)
    rim, rim_send, two, edge = call(
        with_total(rim_sums, total),
        "rim_sums",
        [sds((6, 48, LANES)), sds((9, 16, LANES), BF), sds((2, ROWS, LANES)), sds((8, 64, LANES))],
        10,
        [pltpu.VMEM((13, 32, LANES), F32), pltpu.VMEM((4, 48, LANES), F32), pltpu.VMEM((48, LANES), F32)],
        cost=micros(2),
    )(ready, u, v, b, bl, s, hal, low, high, seam)
    rim_in = shifted(rim_send, "grp", 1)
    force = call(
        with_total(edges, total),
        "edges",
        sds((8, FORCED, LANES)),
        7,
        [pltpu.VMEM((52 * 32, LANES), BF), pltpu.VMEM((52 * 32, LANES), BF), pltpu.VMEM((55 * 32, LANES), BF)],
        cost=micros(6),
        aliases={6: 0},
    )(edge, *weights, inner)
    plane = pltpu.VMEM((ROWS, LANES), F32)
    tall = pltpu.VMEM((ROWS + 16, LANES), F32)
    fin, fin_send = call(
        with_total(substeps, total),
        "substeps",
        [sds((2, TX, TY)), sds((4, TX, TY), BF)],
        7,
        [tall, tall] + [plane] * 9,
        cost=micros(5),
    )(two, mid, seam, rim, mid_in, rim_in, force)
    fin_in = shifted(fin_send, "grp", 1)
    own = call(
        with_total(own_part, total),
        "own_part",
        sds((8, TX, TY)),
        8,
        [pltpu.VMEM((4, 96, LANES), F32), pltpu.VMEM((96, LANES), F32)],
        cost=micros(2),
    )(u, v, b, bl, hal, low, high, force)
    return tuple(
        call(finish, "finish", [sds((4, TX, TY)), sds((4, TX, TY)), sds((TX, TY))], 5, cost=micros(2))(
            bl, fin, fin_send, fin_in, own
        )
    )


def solution(mesh):
    tile = P("grp", "lon", "lat")
    flat = P("lon", "lat")
    return jax.shard_map(
        local,
        mesh=mesh,
        in_specs=(tile, tile, tile, tile, flat, flat, P(), P(), P(), P(), P()),
        out_specs=(tile, tile, flat),
        check_vma=False,
    )
```

```python
import jax
import jax.numpy as jnp
from jax import lax
from jax.experimental import pallas as pl
from jax.experimental.pallas import tpu as pltpu
from jax.sharding import PartitionSpec as P

NSUB = 8
TX, TY = 64, 512
LANES = 640
ROWS = 96
HALO = 16
RIM = 24
EDGE = 18
FORCED = 104
FIELDS = 14
F32 = jnp.float32
BF = jnp.bfloat16

coriolis_base = 0.6
coriolis_slope = 0.8
press_coef = 0.3
drag_coef = 0.5
step_dt = 0.2
closure_coef = 0.5
gravity = 1.0
sub_dt = 0.4
TOTAL_DEPTH = 15.0

TOKEN = jax.ShapeDtypeStruct((8, 128), jnp.float32)
VMEM = pl.BlockSpec(memory_space=pltpu.VMEM)


def sds(shape, dtype=F32):
    return jax.ShapeDtypeStruct(shape, dtype)


def wet_of(bl, level):
    return jnp.where(bl > level, 1.0, 0.0)


def latitudes(lat, shape):
    lane = lax.broadcasted_iota(jnp.int32, shape, len(shape) - 1)
    return lat * TY + jnp.where(lane < TY + 64, lane, lane - LANES)


def inside_of(lat, total, shape):
    y = latitudes(lat, shape)
    return jnp.where((y >= 0) & (y < total), 1.0, 0.0)


def pack_lat(sc, u, v, b, l, s, *refs):
    raw, to_down, to_up, made = refs[:5], refs[5], refs[6], refs[7:12]
    ub, vb, bb, lb, sb, sem = refs[12:18]
    held, spread, weight_sem = refs[18:23], refs[23], refs[24]
    base = 4 * sc[0]
    lane = lax.broadcasted_iota(jnp.int32, (TX, 128), 1)
    copies = []
    for side, at in enumerate((0, TY - 128)):
        for n, (src, dst) in enumerate(((u, ub), (v, vb), (b, bb))):
            copies.append(pltpu.make_async_copy(src.at[:, :, at : at + 128], dst.at[side], sem.at[side, n]))
        for n, (src, dst) in enumerate(((l, lb), (s, sb))):
            copies.append(pltpu.make_async_copy(src.at[:, at : at + 128], dst.at[side], sem.at[side, 3 + n]))
    more = [pltpu.make_async_copy(src, dst, weight_sem.at[n]) for n, (src, dst) in enumerate(zip(raw, held))]
    for copy in copies + more:
        copy.start()

    def fields(side):
        bl = lb[side].astype(F32)
        wets = [wet_of(bl, (base + k).astype(F32)) for k in range(4)]
        for a in (ub, vb, bb):
            for k in range(4):
                yield a[side, k] * wets[k]
        yield bl
        yield sb[side]

    for side, (out, origin) in enumerate(((to_down, 0), (to_up, 128 - EDGE))):
        for copy in copies[5 * side : 5 * side + 5]:
            copy.wait()
        for i, field in enumerate(fields(side)):
            tile, place = divmod(i, 7)
            if place == 0:
                acc = jnp.zeros((TX, 128), F32)
            moved = pltpu.roll(field, (EDGE * place - origin) % 128, 1)
            acc = jnp.where((lane >= EDGE * place) & (lane < EDGE * (place + 1)), moved, acc)
            if place == 6:
                out[tile] = acc.astype(BF)
    for copy in more:
        copy.wait()
    build_weights(*held, *made, spread)


def bring(sc, bl, s, done):
    done[...] = bl[0:8, 0:128].astype(F32) + s[0:8, 0:128]


def pack_lon(total, sc, near, before, after, *refs):
    tops, bots, extra_t, extra_b = refs[0:5], refs[5:10], refs[10:13], refs[13:16]
    hal, to_down, to_up, work = refs[16:]
    base = 4 * sc[0]
    lane = lax.broadcasted_iota(jnp.int32, (TX, 128), 1)
    low_from = jnp.where(sc[1] > 0, 128 - EDGE, 128)
    high_to = jnp.where(sc[1] < total // TY - 1, EDGE, 0)
    for tile in range(2):
        low, high = before[tile].astype(F32), after[tile].astype(F32)
        for place in range(7):
            a = pltpu.roll(high, (-EDGE * place) % 128, 1)
            b = pltpu.roll(low, (128 - EDGE - EDGE * place) % 128, 1)
            hal[tile * 7 + place] = jnp.where(lane < high_to, a, jnp.where(lane >= low_from, b, 0.0))
    for out, (u, v, b, l, s), row in ((to_down, tops, 0), (to_up, bots, TX - 16)):
        bl = l[...].astype(F32)
        for k in range(4):
            wet = wet_of(bl, (base + k).astype(F32))
            for n, a in enumerate((u, v, b)):
                out[4 * n + k, :, :TY] = (a[k] * wet).astype(BF)
        out[12, :, :TY] = bl.astype(BF)
        out[13, :, :TY] = s[...].astype(BF)
        for i in range(FIELDS):
            out[i, :, TY:] = hal[i, row : row + 16, :].astype(BF)
    for out, (u, v, l), first, row in ((to_down, extra_t, 0, 16), (to_up, extra_b, 6, 46)):
        bl = l[first : first + 2, :].astype(F32)
        for k in range(4):
            wet = wet_of(bl, (base + k).astype(F32))
            for n, a in enumerate((u, v)):
                work[2 * (4 * n + k) : 2 * (4 * n + k) + 2, :TY] = a[k, first : first + 2, :] * wet
        for i in range(8):
            work[2 * i : 2 * i + 2, TY:] = hal[i, row : row + 2, :]
        out[14] = work[...].astype(BF)


def build_weights(w_in, b_in, w_mid, b_mid, w_out, w1, w2, w3, b1, b2, spread):
    def across(parts, rows, cols):
        rows_all = sum(p.shape[0] for p in parts)
        full = jnp.concatenate(parts + [jnp.zeros((128 - rows_all, 128), F32)], 0)
        return full.T[:rows, :]

    def wide(a):
        return jnp.concatenate([a, jnp.zeros((a.shape[0], 128 - a.shape[1]), F32)], 1)

    zero8 = jnp.zeros((8, 128), F32)
    parts = []
    for a in range(3):
        parts += [wide(w_in[3 * a + b].astype(F32)) for b in range(3)] + [zero8]
    first = across(parts, 32, 96)
    first = jnp.concatenate([first, jnp.zeros((32, 128), F32)], 1)
    for p in range(6):
        w1[32 * p : 32 * p + 32, :] = pltpu.roll(first, 32 * p, 1).astype(BF)
    for b in range(3):
        mid = across([wide(w_mid[3 * a + b].astype(F32)) for a in range(3)], 32, 96)
        mid = jnp.concatenate([mid, jnp.zeros((32, 128), F32)], 1)
        for p in range(6):
            w2[192 * b + 32 * p : 192 * b + 32 * p + 32, :] = pltpu.roll(mid, 32 * p, 1).astype(BF)
        last = jnp.concatenate([w_out[3 * a + b].astype(F32) for a in range(3)] + [jnp.zeros((8, 288), F32)], 1)
        for p in range(8):
            spread[:, p, :] = pltpu.roll(last, 32 * p, 1)
        w3[64 * b : 64 * b + 64, :] = spread[...].reshape(64, 384)[:, :320].astype(BF)
    eye = lax.broadcasted_iota(jnp.int32, (32, 32), 0) == lax.broadcasted_iota(jnp.int32, (32, 32), 1)
    for src, dst in ((b_in, b1), (b_mid, b2)):
        column = jnp.sum(jnp.where(eye, src[...], 0.0), 1, keepdims=True)
        for p in range(6):
            dst[32 * p : 32 * p + 32, :] = jnp.broadcast_to(column, (32, 128))


def load_slots(up, start, count, in0, at):
    for i in range(count):
        c = up[:, start + i, :]
        r = 32 * (at + i)
        in0[r : r + 16, :] = jnp.concatenate([pltpu.roll(c, 1, 1), c], 0).astype(BF)
        in0[r + 16 : r + 32, :] = jnp.concatenate([pltpu.roll(c, LANES - 1, 1), jnp.zeros_like(c)], 0).astype(BF)


def closure(in0, act1, act2, weights, inside, parts, store):
    w1, w2, w3, b1, b2 = weights
    bias1, bias2 = b1[:, :1], b2[:, :1]

    def combined(o, m):
        return pltpu.roll(o[:m], 1, 1) + o[m : 2 * m] + pltpu.roll(o[2 * m :], LANES - 1, 1)

    for s1, _, _, n1, _, _ in parts:
        for j in range(n1):
            r = 32 * (s1 + 6 * j)
            o = jnp.dot(w1[...], in0[r : r + 256, :], preferred_element_type=F32)
            act1[r : r + 192, :] = (jnp.maximum(o + bias1, 0.0) * inside).astype(BF)
    for s1, s2, shift, _, n2, _ in parts:
        for j in range(n2):
            r, to = 32 * (s1 + 6 * j), 32 * (s2 + shift + 6 * j)
            o = combined(jnp.dot(w2[...], act1[r : r + 256, :], preferred_element_type=F32), 192)
            act2[to : to + 192, :] = (jnp.maximum(o + bias2, 0.0) * inside).astype(BF)
    for part, (_, s2, _, _, _, n3) in enumerate(parts):
        for j in range(n3):
            r = 32 * (s2 + 8 * j)
            o = combined(jnp.dot(w3[...], act2[r : r + 320, :], preferred_element_type=F32), 64)
            store(part, j, (closure_coef * o).astype(BF).astype(F32).reshape(8, 8, LANES))


def interior(total, sc, u, v, bl, hal, w1, w2, w3, b1, b2, out, done, up, in0, act1, act2):
    done[...] = jnp.zeros_like(done)

    @pl.when(sc[0] == 0)
    def _():
        level = bl[...].astype(F32)
        for k in range(4):
            wet = wet_of(level, float(k))
            up[k, :, :TY] = u[k] * wet
            up[4 + k, :, :TY] = v[k] * wet
        for i in range(8):
            up[i, :, TY:] = hal[i]
        load_slots(up, 1, 62, in0, 0)
        act1[1920:1984, :] = jnp.zeros((64, LANES), BF)

        def store(part, j, f):
            out[:, 24 + 8 * j : 32 + 8 * j, :] = f

        closure(in0, act1, act2, (w1, w2, w3, b1, b2), inside_of(sc[1], total, (1, LANES)), [(0, 0, 0, 10, 10, 7)], store)


def edges(total, sc, edge, two, w1, w2, w3, b1, b2, inner, out, send, in0, act1, act2):
    @pl.when(sc[0] == 0)
    def _():
        for at, start in ((0, 6), (26, 33)):
            load_slots(edge, start, 26, in0, at)
            act1[32 * at + 768 : 32 * at + 832, :] = jnp.zeros((64, LANES), BF)
        act2[0:160, :] = jnp.zeros((160, LANES), BF)
        act2[29 * 32 + 768 :, :] = jnp.zeros((64, LANES), BF)

        def store(part, j, f):
            row = 80 * part + 8 * j
            out[:, row : row + 8, :] = f

        parts = [(0, 0, 5, 4, 4, 3), (26, 29, 0, 4, 4, 3)]
        closure(in0, act1, act2, (w1, w2, w3, b1, b2), inside_of(sc[1], total, (1, LANES)), parts, store)
        for i in range(0, 48, 16):
            halves = []
            for p in (i, i + 8):
                r = p if p < RIM else p + 48
                level = two[0, r : r + 8, :]
                rows = slice(r + 4, r + 12)
                halves.append(forced(sc, level, out, rows, [slice(0, LANES)], ~inner_rows(r - HALO, level.shape)))
            for n in range(2):
                send[n, i : i + 16, :] = jnp.concatenate([halves[0][n], halves[1][n]], 0).astype(BF)

    @pl.when(sc[0] != 0)
    def _():
        send[...] = jnp.zeros_like(send)


def pressures(base, b_rows, pr, load, rows):
    for r in range(0, rows, 8):
        run = jnp.zeros((8, pr.shape[2]), F32)
        for k in range(4):
            weighted = b_rows(k, r) * (1.0 + 0.25 * (base + k).astype(F32))
            pr[k, r + 8 : r + 16, :] = run + 0.5 * weighted
            run = run + weighted
        load[r + 8 : r + 16, :] = run


def grads(ref, r):
    here = ref[r + 8 : r + 16, :]
    gx = (ref[r + 9 : r + 17, :] - ref[r + 7 : r + 15, :]) * 0.5
    gy = (pltpu.roll(here, here.shape[1] - 1, 1) - pltpu.roll(here, 1, 1)) * 0.5
    return gx, gy


def open_grads(ref, r):
    here = ref[r + 8 : r + 16, :]
    lane = lax.broadcasted_iota(jnp.int32, here.shape, 1)
    gx = (ref[r + 9 : r + 17, :] - ref[r + 7 : r + 15, :]) * 0.5
    right = jnp.where(lane == TY - 1, 0.0, pltpu.roll(here, TY - 1, 1))
    left = jnp.where(lane == 0, 0.0, pltpu.roll(here, 1, 1))
    return gx, (right - left) * 0.5


def coriolis_of(lat, total, shape):
    return coriolis_base + coriolis_slope * (latitudes(lat, shape).astype(F32) * (1.0 / total) - 0.5)


def sums_of(sc, coriolis, level, east, north, pr, load, r, grads=grads):
    base = 4 * sc[0]
    te = jnp.zeros(level.shape, F32)
    tn, us, vs = te, te, te
    for k in range(4):
        number = (base + k).astype(F32)
        thick = 1.0 + 0.25 * number
        weight = jnp.where(level > number, thick, 0.0)
        drag = jnp.where(level == number + 1.0, drag_coef, 0.0)
        e, n = east(k), north(k)
        gx, gy = grads(pr.at[k], r)
        te = te + weight * (coriolis * n - press_coef * gx - drag * e)
        tn = tn + weight * (-coriolis * e - press_coef * gy - drag * n)
        us = us + thick * e
        vs = vs + thick * n
    below = jnp.zeros(level.shape, F32)
    for k in range(4, 8):
        below = below + jnp.where(level > float(k), 1.0 + 0.25 * k, 0.0)
    gx, gy = grads(load, r)
    below = below * (press_coef * jnp.where(sc[0] == 0, 1.0, 0.0))
    return te - below * gx, tn - below * gy, us, vs, gx, gy


def closed(pr, load):
    for ref in [pr.at[k] for k in range(4)] + [load]:
        end = ref.shape[0]
        ref[0:8, :] = jnp.zeros((8, ref.shape[1]), F32)
        ref[end - 8 : end, :] = jnp.zeros((8, ref.shape[1]), F32)


def forced(sc, level, force, rows, pieces, keep):
    te = jnp.zeros(level.shape, F32)
    tn = te
    for k in range(4):
        weight = jnp.where(level > float(k), 1.0 + 0.25 * k, 0.0)
        fe = [force[k, rows, at] for at in pieces]
        fn = [force[4 + k, rows, at] for at in pieces]
        te = te + weight * (fe[0] if len(fe) == 1 else jnp.concatenate(fe, 1))
        tn = tn + weight * (fn[0] if len(fn) == 1 else jnp.concatenate(fn, 1))
    keep = keep & (jnp.zeros(level.shape, jnp.int32) + sc[0] == 0)
    return jnp.where(keep, te, 0.0), jnp.where(keep, tn, 0.0)


def inner_rows(r, shape):
    x = r + lax.broadcasted_iota(jnp.int32, shape, 0)
    return (x >= 4) & (x < 60)


def middle_sums(total, sc, first, u, v, b, bl, s, force, sums, send, done, pr, load):
    done[...] = jnp.zeros_like(done)
    base = 4 * sc[0]

    def wet(k, rr):
        return wet_of(bl[rr, :].astype(F32), (base + k).astype(F32))

    def b_rows(k, r):
        rr = slice(r, r + 8)
        return b[k, rr, :] * wet(k, rr)

    pressures(base, b_rows, pr, load, TX)
    closed(pr, load)
    coriolis = coriolis_of(sc[1], total, (8, LANES))[:, :TY]
    for q in range(0, TX, 16):
        halves = []
        for r in (q, q + 8):
            rr = slice(r, r + 8)
            level = bl[rr, :].astype(F32)
            found = sums_of(
                sc, coriolis, level, lambda k: u[k, rr, :] * wet(k, rr), lambda k: v[k, rr, :] * wet(k, rr), pr, load, r, open_grads
            )
            extra = forced(sc, level, force, slice(r + 20, r + 28), [slice(0, TY)], inner_rows(r, level.shape))
            found = (found[0] + extra[0], found[1] + extra[1]) + found[2:]
            for i, a in enumerate(found):
                sums[i, rr, :] = a
            halves.append(found)
        for i in range(4):
            a = jnp.concatenate([halves[0][i], halves[1][i]], 0)
            send[i, q : q + 16, :] = a.astype(BF)
        send[4, q : q + 16, :] = load[q + 8 : q + 24, :].astype(BF)


def seam_sums(total, sc, u, v, b, bl, hal, force, sums, ext, pr, load):
    base = 4 * sc[0]
    last, first = slice(TY - 128, TY), slice(0, 128)

    def three(a, outer, b):
        return jnp.concatenate([a, outer, b], 1)

    for r in range(0, TX, 8):
        rr = slice(r, r + 8)
        levels = [bl[rr, at].astype(F32) for at in (last, first)]
        ext[12, rr, :] = three(levels[0], hal[12, rr, :], levels[1])
        for k in range(4):
            wets = [wet_of(level, (base + k).astype(F32)) for level in levels]
            for n, a in enumerate((u, v, b)):
                ext[4 * n + k, rr, :] = three(a[k, rr, last] * wets[0], hal[4 * n + k, rr, :], a[k, rr, first] * wets[1])
    pressures(base, lambda k, r: ext[8 + k, r : r + 8, :], pr, load, TX)
    closed(pr, load)
    whole = coriolis_of(sc[1], total, (8, LANES))
    coriolis = three(whole[:, last], whole[:, TY:], whole[:, first])
    for r in range(0, TX, 8):
        rr = slice(r, r + 8)
        found = sums_of(sc, coriolis, ext[12, rr, :], lambda k: ext[k, rr, :], lambda k: ext[4 + k, rr, :], pr, load, r)
        pieces = [last, slice(TY, LANES), first]
        extra = forced(sc, ext[12, rr, :], force, slice(r + 20, r + 28), pieces, inner_rows(r, (8, 384)))
        found = (found[0] + extra[0], found[1] + extra[1]) + found[2:] + (load[r + 8 : r + 16, :],)
        for i, a in enumerate(found):
            sums[i, rr, :] = a


def rim_sums(total, sc, ready, u, v, b, bl, s, hal, low, high, seam, sums, send, two, edge, ext, pr, load):
    base = 4 * sc[0]
    tall = 32
    loads = []
    for side, halo in ((0, low), (1, high)):
        own = slice(0, 16) if side == 0 else slice(TX - 16, TX)
        hr, orr = (slice(0, 16), slice(16, 32)) if side == 0 else (slice(16, 32), slice(0, 16))
        level = bl[own, :].astype(F32)
        for i in range(13):
            ext[i, hr, :] = halo[i].astype(F32)
            ext[i, orr, TY:] = hal[i, own, :]
        for k in range(4):
            wet = wet_of(level, (base + k).astype(F32))
            for n, a in enumerate((u, v, b)):
                ext[4 * n + k, orr, :TY] = a[k, own, :] * wet
        ext[12, orr, :TY] = level
        pressures(base, lambda k, r: ext[8 + k, r : r + 8, :], pr, load, tall)
        for ref in [pr.at[k] for k in range(4)] + [load]:
            if side == 0:
                ref[0:8, :] = jnp.zeros((8, LANES), F32)
            else:
                ref[40:48, :] = jnp.zeros((8, LANES), F32)
        loads.append(load[23:24, :] if side == 0 else load[24:25, :])
        coriolis = coriolis_of(sc[1], total, (8, LANES))
        for j in range(3):
            r = 8 * j + 8 * side
            rr = slice(r, r + 8)
            found = sums_of(sc, coriolis, ext[12, rr, :], lambda k: ext[k, rr, :], lambda k: ext[4 + k, rr, :], pr, load, r)
            for i, a in enumerate(found):
                sums[i, RIM * side + 8 * j : RIM * side + 8 * j + 8, :] = a
        more = halo[14].astype(F32)
        for i in range(8):
            if side == 0:
                edge[i, 0:8, :] = jnp.zeros((8, LANES), F32)
                edge[i, 8:32, :] = ext[i, 0:24, :]
                edge[i, 6:8, :] = more[2 * i : 2 * i + 2, :]
            else:
                edge[i, 32:56, :] = ext[i, 8:32, :]
                edge[i, 56:64, :] = jnp.zeros((8, LANES), F32)
                edge[i, 56:58, :] = more[2 * i : 2 * i + 2, :]
        at = slice(0, 16) if side == 0 else slice(80, 96)
        two[0, at, :] = halo[12].astype(F32)
        two[1, at, :] = halo[13].astype(F32)
    two[0, 16:80, :TY] = bl[...].astype(F32)
    two[1, 16:80, :TY] = s[...]
    for i in range(2):
        two[i, 16:80, TY:] = hal[12 + i]
    lane = lax.broadcasted_iota(jnp.int32, (16, 128), 1)
    for i in range(4):
        for side in range(2):
            at = slice(0, 16) if side == 0 else slice(32, 48)
            packed = sums[i, at, TY:]
            for turn in range(2):
                base = 16 + 34 * turn
                own = slice(16 * (2 * turn + side), 16 * (2 * turn + side) + 16)
                outer, before, after = seam[i, own, 128:256], seam[i, own, 0:128], seam[i, own, 256:384]
                packed = jnp.where((lane >= base) & (lane < base + 16), pltpu.roll(outer, base, 1), packed)
                packed = jnp.where((lane >= base + 16) & (lane < base + 32), pltpu.roll(outer, base + 32, 1), packed)
                packed = jnp.where(lane == base + 32, pltpu.roll(before, base + 33, 1), packed)
                packed = jnp.where(lane == base + 33, pltpu.roll(after, base + 33, 1), packed)
                if i == 0:
                    load_at = seam[6, own, 128:256]
                    packed = jnp.where(lane == 84 + 2 * turn, pltpu.roll(load_at, 84 + 2 * turn, 1), packed)
                    packed = jnp.where(lane == 85 + 2 * turn, pltpu.roll(load_at, 86 + 2 * turn, 1), packed)
            send[2 * i + side, :, :TY] = sums[i, at, :TY].astype(BF)
            send[2 * i + side, :, TY:] = packed.astype(BF)
    ends = [sums[i, row : row + 1, :] for i in range(4) for row in (16, 31)]
    send[8] = jnp.concatenate(ends + loads + [jnp.zeros((6, LANES), F32)], 0).astype(BF)


def own_part(total, sc, u, v, b, bl, hal, low, high, force, mid_in, rim_in, out, pr, load):
    base = 4 * sc[0]
    upper = jnp.where(sc[0] == 0, step_dt, 0.0)

    def b_rows(k, r):
        if r == 0:
            return low[8 + k].astype(F32)[8:16]
        if r == TX + 8:
            return high[8 + k].astype(F32)[0:8]
        at = slice(r - 8, r)
        wet = wet_of(bl[at, :].astype(F32), (base + k).astype(F32))
        return jnp.concatenate([b[k, at, :] * wet, hal[8 + k, at, :]], 1)

    pressures(base, b_rows, pr, load, TX + 16)
    lane = lax.broadcasted_iota(jnp.int32, (16, 128), 1)
    for x in range(0, TX, 16):
        turn = x // 32
        beyond = rim_in[x // 16 % 2, :, TY:].astype(F32)
        outer = jnp.where(lane < 64, pltpu.roll(beyond, 44 - 2 * turn, 1), pltpu.roll(beyond, 42 - 2 * turn, 1))
        above = jnp.concatenate([mid_in[4, x : x + 16, :].astype(F32), outer], 1)
        above = jnp.where(upper > 0.0, 0.0, above)
        for k in range(4):
            pr[k, x + 16 : x + 32, :] = pr[k, x + 16 : x + 32, :] + above
    ends = rim_in[8].astype(F32)
    for at, row in ((8, 15), (9, TX + 16)):
        above = jnp.where(upper > 0.0, 0.0, ends[at : at + 1, :])
        for k in range(4):
            pr[k, row : row + 1, :] = pr[k, row : row + 1, :] + above
    coriolis = coriolis_of(sc[1], total, (8, LANES))[:, :TY]
    for r in range(0, TX, 8):
        rr = slice(r, r + 8)
        lev = bl[rr, :].astype(F32)
        for k in range(4):
            number = (base + k).astype(F32)
            wet = wet_of(lev, number)
            drag = jnp.where(lev == number + 1.0, drag_coef, 0.0)
            east, north = u[k, rr, :], v[k, rr, :]
            gx, gy = grads(pr.at[k], r + 8)
            te = coriolis * north - press_coef * gx[:, :TY] - drag * east
            tn = -coriolis * east - press_coef * gy[:, :TY] - drag * north
            at = slice(r + 20, r + 28)
            fe = jnp.where(upper > 0.0, force[k, at, :TY], 0.0)
            fn = jnp.where(upper > 0.0, force[4 + k, at, :TY], 0.0)
            out[k, rr, :] = wet * (east + step_dt * (te + fe))
            out[4 + k, rr, :] = wet * (north + step_dt * (tn + fn))


def substeps(total, sc, two, mid, seam, rim, mid_in, rim_in, force, force_in, own, east_out, north_out, surface_out, lv, fx, fy, eb, nb, ae, an, es, ns, rel, c2):
    zero8 = jnp.zeros((8, LANES), F32)
    lower = jnp.zeros((8, LANES), jnp.int32) + sc[0] > 0
    lane = lax.broadcasted_iota(jnp.int32, (8, 128), 1)

    def ended(i, at, outer):
        first = jnp.where(lane == 0, seam[i, at, 256:384], mid[i, at, 0:128])
        last = jnp.where(lane == 127, seam[i, at, 0:128], mid[i, at, TY - 128 :])
        pieces = [first, mid[i, at, 128 : TY - 128], last]
        return jnp.concatenate(pieces + [seam[i, at, 128:256]] if outer else pieces, 1)

    for ref in (lv, fx):
        ref[0:8, :] = zero8
        ref[ROWS + 8 : ROWS + 16, :] = zero8
    for r in range(0, ROWS, 8):
        rr = slice(r, r + 8)
        level = two[0, rr, :]
        depth = level + 0.125 * level * (level - 1.0)
        over = 1.0 / jnp.maximum(depth, 1.0)
        rel[rr, :] = depth * (1.0 / TOTAL_DEPTH)
        c2[rr, :] = jnp.where(level > 0.0, 0.5 * sub_dt * gravity, 0.0)
        middle = RIM <= r < ROWS - RIM
        at = r - RIM if middle else (r if r < RIM else r - 48)
        at = slice(at, at + 8)
        x = r - HALO
        found = []
        for i in range(4):
            here = ended(i, slice(x, x + 8), True) if middle else rim[i, at, :]
            if not 0 <= x < TX:
                row = r % 16
                found.append(here + rim_in[2 * i + (x > 0), :, :].astype(F32)[row : row + 8])
                continue
            turn, half = x // 32, x % 16
            base = 16 + 34 * turn
            beyond = rim_in[2 * i + x // 16 % 2, :, TY:].astype(F32)[half : half + 8]
            theirs = mid_in[i, x - half : x - half + 16, :].astype(F32)[half : half + 8]
            outer = jnp.where(lane < 16, pltpu.roll(beyond, 128 - base, 1), pltpu.roll(beyond, 96 - base, 1))
            first = jnp.where(lane == 0, pltpu.roll(beyond, 95 - base, 1), theirs[:, 0:128])
            last = jnp.where(lane == 127, pltpu.roll(beyond, 95 - base, 1), theirs[:, TY - 128 :])
            theirs = jnp.concatenate([first, theirs[:, 128 : TY - 128], last, outer], 1)
            if x in (0, TX - 8):
                end = rim_in[8].astype(F32)[2 * i + (x > 0) : 2 * i + (x > 0) + 1]
                row = lax.broadcasted_iota(jnp.int32, (8, LANES), 0)
                theirs = jnp.where(row == (0 if x == 0 else 7), end, theirs)
            found.append(here + theirs)
        if not middle:
            everywhere = level == level
            mine = forced(sc, level, force, slice(r + 4, r + 12), [slice(0, LANES)], everywhere)
            pair, half = at.start // 16 * 16, at.start % 16
            for n in range(2):
                theirs = force_in[n, pair : pair + 16, :].astype(F32)[half : half + 8]
                found[n] = found[n] + jnp.where(lower, theirs, mine[n])
        ae[rr, :] = sub_dt * found[0] * over
        an[rr, :] = sub_dt * found[1] * over
        e, n = found[2] * over, found[3] * over
        es[rr, :], ns[rr, :] = e, n
        eb[rr, :], nb[rr, :] = e, n
        lv[r + 8 : r + 16, :] = two[1, rr, :]
    inside = inside_of(sc[1], total, (8, LANES))

    def step(first, carry):
        for r in range(first, ROWS - first, 8):
            rr = slice(r, r + 8)
            here = lv[r + 8 : r + 16, :]
            dx = lv[r + 9 : r + 17, :] - lv[r + 7 : r + 15, :]
            dy = pltpu.roll(here, LANES - 1, 1) - pltpu.roll(here, 1, 1)
            c = c2[rr, :]
            e = eb[rr, :] + (ae[rr, :] - c * dx)
            n = nb[rr, :] + (an[rr, :] - c * dy)
            eb[rr, :] = e
            nb[rr, :] = n
            fx[r + 8 : r + 16, :] = rel[rr, :] * e
            fy[rr, :] = rel[rr, :] * n
        for r in range(first, ROWS - first, 8):
            rr = slice(r, r + 8)
            dx = fx[r + 9 : r + 17, :] - fx[r + 7 : r + 15, :]
            f = fy[rr, :]
            dy = pltpu.roll(f, LANES - 1, 1) - pltpu.roll(f, 1, 1)
            lv[r + 8 : r + 16, :] = inside * (lv[r + 8 : r + 16, :] - (0.5 * sub_dt) * (dx + dy))
        return carry

    lax.fori_loop(0, NSUB // 2, lambda _, carry: step(0, carry), 0)
    lax.fori_loop(0, NSUB // 2, lambda _, carry: step(8, carry), 0)
    base = 4 * sc[0]
    for q in range(0, TX, 8):
        rr, at = slice(q + HALO, q + HALO + 8), slice(q, q + 8)
        level = two[0, rr, :TY]
        fe = eb[rr, :TY] - es[rr, :TY] - (step_dt / sub_dt) * ae[rr, :TY]
        fn = nb[rr, :TY] - ns[rr, :TY] - (step_dt / sub_dt) * an[rr, :TY]
        for k in range(4):
            wet = wet_of(level, (base + k).astype(F32))
            east_out[k, at, :] = own[k, at, :] + wet * fe
            north_out[k, at, :] = own[4 + k, at, :] + wet * fn
        surface_out[at, :] = lv[q + HALO + 8 : q + HALO + 16, :TY]


def call(kernel, name, out_shape, n_in, scratch=(), in_specs=None, cost=None, grid=(), aliases=None, room=28):
    single = not isinstance(out_shape, (list, tuple))

    def placed(*refs):
        kernel((lax.axis_index("grp"), lax.axis_index("lat")), *refs)

    return pl.pallas_call(
        placed,
        name=name,
        grid=grid,
        out_shape=out_shape,
        in_specs=in_specs or [VMEM] * n_in,
        out_specs=VMEM if single else [VMEM] * len(out_shape),
        scratch_shapes=list(scratch),
        compiler_params=pltpu.CompilerParams(vmem_limit_bytes=room * 2**20),
        cost_estimate=cost,
        input_output_aliases=aliases or {},
    )


def with_total(kernel, total):
    return lambda sc, *refs: kernel(total, sc, *refs)


def micros(us):
    return pl.CostEstimate(flops=int(us * 1e6), bytes_accessed=int(us * 3e6), transcendentals=0)


def shifted(x, axis, by):
    size = lax.axis_size(axis)
    return lax.ppermute(x, axis, [(i, (i + by) % size) for i in range(size)])


def local(u, v, b, wet_mask, bl, s, w_in, b_in, w_mid, b_mid, w_out):
    total = TY * lax.axis_size("lat")
    wide, half = pltpu.VMEM((2, 4, TX, 128), F32), sds((2, TX, 128), BF)
    made = [sds((192, 256), BF), sds((576, 256), BF), sds((192, 320), BF), sds((192, 128)), sds((192, 128))]
    to_down, to_up, *weights = call(
        pack_lat,
        "pack_lat",
        [half, half] + made,
        10,
        [
            wide,
            wide,
            wide,
            pltpu.VMEM((2, TX, 128), jnp.int32),
            pltpu.VMEM((2, TX, 128), F32),
            pltpu.SemaphoreType.DMA((2, 5)),
            pltpu.VMEM((9, 8, 32), BF),
            pltpu.VMEM((1, 32), F32),
            pltpu.VMEM((9, 32, 32), BF),
            pltpu.VMEM((1, 32), F32),
            pltpu.VMEM((9, 8, 32), BF),
            pltpu.VMEM((8, 8, 384), F32),
            pltpu.SemaphoreType.DMA((5,)),
        ],
        in_specs=[pl.BlockSpec(memory_space=pltpu.HBM)] * 10,
        room=60,
    )(u, v, b, bl, s, w_in, b_in[None, :], w_mid, b_mid[None, :], jnp.swapaxes(w_out, 1, 2))
    before = shifted(to_up, "lat", 1)
    after = shifted(to_down, "lat", -1)

    near = call(bring, "bring", TOKEN, 2, cost=micros(1))(bl, s)

    def rows(n, i, three):
        return [pl.BlockSpec((4, n, TY), lambda _: (0, i, 0))] * three + [pl.BlockSpec((n, TY), lambda _: (i, 0))] * (three - 1)

    out = sds((15, 16, LANES), BF)
    hal, down, up = call(
        with_total(pack_lon, total),
        "pack_lon",
        [sds((FIELDS, TX, 128)), out, out],
        19,
        [pltpu.VMEM((16, LANES), F32)],
        in_specs=[VMEM, VMEM, VMEM] + rows(16, 0, 3) + rows(16, 3, 3) + rows(8, 2, 2) + rows(8, 5, 2),
        grid=(1,),
    )(near, before, after, u, v, b, bl, s, u, v, b, bl, s, u, v, bl, u, v, bl)
    low = shifted(up, "lon", 1)
    high = shifted(down, "lon", -1)
    inner, ready = call(
        with_total(interior, total),
        "interior",
        [sds((8, FORCED, LANES)), TOKEN],
        9,
        [
            pltpu.VMEM((8, TX, LANES), F32),
            pltpu.VMEM((62 * 32, LANES), BF),
            pltpu.VMEM((62 * 32, LANES), BF),
            pltpu.VMEM((60 * 32, LANES), BF),
        ],
        cost=micros(7),
    )(u, v, bl, hal, *weights)
    mid, mid_send, summed = call(
        with_total(middle_sums, total),
        "middle_sums",
        [sds((6, TX, TY)), sds((5, TX, TY), BF), TOKEN],
        7,
        [pltpu.VMEM((4, TX + 16, TY), F32), pltpu.VMEM((TX + 16, TY), F32)],
        cost=micros(1),
    )(ready, u, v, b, bl, s, inner)
    mid_in = shifted(mid_send, "grp", 1)
    seam = call(
        with_total(seam_sums, total),
        "seam_sums",
        sds((7, TX, 384)),
        6,
        [pltpu.VMEM((13, TX, 384), F32), pltpu.VMEM((4, TX + 16, 384), F32), pltpu.VMEM((TX + 16, 384), F32)],
        cost=micros(1),
    )(u, v, b, bl, hal, inner)
    rim, rim_send, two, edge = call(
        with_total(rim_sums, total),
        "rim_sums",
        [sds((6, 48, LANES)), sds((9, 16, LANES), BF), sds((2, ROWS, LANES)), sds((8, 64, LANES))],
        10,
        [pltpu.VMEM((13, 32, LANES), F32), pltpu.VMEM((4, 48, LANES), F32), pltpu.VMEM((48, LANES), F32)],
        cost=micros(2),
    )(summed, u, v, b, bl, s, hal, low, high, seam)
    rim_in = shifted(rim_send, "grp", 1)
    force, force_send = call(
        with_total(edges, total),
        "edges",
        [sds((8, FORCED, LANES)), sds((2, 48, LANES), BF)],
        8,
        [pltpu.VMEM((52 * 32, LANES), BF), pltpu.VMEM((52 * 32, LANES), BF), pltpu.VMEM((55 * 32, LANES), BF)],
        cost=micros(6),
        aliases={7: 0},
    )(edge, two, *weights, inner)
    force_in = shifted(force_send, "grp", 1)
    own = call(
        with_total(own_part, total),
        "own_part",
        sds((8, TX, TY)),
        10,
        [pltpu.VMEM((4, 96, LANES), F32), pltpu.VMEM((96, LANES), F32)],
        cost=micros(2),
    )(u, v, b, bl, hal, low, high, force, mid_in, rim_in)
    plane = pltpu.VMEM((ROWS, LANES), F32)
    tall = pltpu.VMEM((ROWS + 16, LANES), F32)
    return tuple(
        call(
            with_total(substeps, total),
            "substeps",
            [sds((4, TX, TY)), sds((4, TX, TY)), sds((TX, TY))],
            9,
            [tall, tall] + [plane] * 9,
            cost=micros(5),
        )(two, mid, seam, rim, mid_in, rim_in, force, force_in, own)
    )


def solution(mesh):
    tile = P("grp", "lon", "lat")
    flat = P("lon", "lat")
    return jax.shard_map(
        local,
        mesh=mesh,
        in_specs=(tile, tile, tile, tile, flat, flat, P(), P(), P(), P(), P()),
        out_specs=(tile, tile, flat),
        check_vma=False,
    )
```

```python
import jax
import jax.numpy as jnp
from jax import lax
from jax.experimental import pallas as pl
from jax.experimental.pallas import tpu as pltpu
from jax.sharding import PartitionSpec as P

NSUB = 8
TX, TY = 64, 512
LANES = 640
ROWS = 96
HALO = 16
RIM = 24
EDGE = 18
FORCED = 104
FIELDS = 14
F32 = jnp.float32
BF = jnp.bfloat16

coriolis_base = 0.6
coriolis_slope = 0.8
press_coef = 0.3
drag_coef = 0.5
step_dt = 0.2
closure_coef = 0.5
gravity = 1.0
sub_dt = 0.4
TOTAL_DEPTH = 15.0

TOKEN = jax.ShapeDtypeStruct((8, 128), jnp.float32)
VMEM = pl.BlockSpec(memory_space=pltpu.VMEM)


def placed(n, *spots):
    return [(src, n, block, at) for src, (block, at) in zip((0, 128 - n), spots)]


SPOTS = (
    [placed(EDGE, (1 + i // 3, 36 * (i % 3)), (1 + i // 3, 36 * (i % 3) + 18)) for i in range(8)]
    + [placed(16, (0, 32 * k), (0, 32 * k + 16)) for k in range(4)]
    + [placed(16, (3, 72), (3, 88)), placed(16, (2, 108), (3, 104)), placed(4, (1, 108), (1, 112))]
)


def outer_lanes(halo, i):
    lane = lax.broadcasted_iota(jnp.int32, (16, 128), 1)
    found = jnp.zeros((16, 128), F32)
    for src, n, block, at in SPOTS[i]:
        moved = pltpu.roll(halo[15, :, 128 * block : 128 * block + 128].astype(F32), (src - at) % 128, 1)
        found = jnp.where((lane >= src) & (lane < src + n), moved, found)
    return found


def sent_rows(halo, i):
    return jnp.concatenate([halo[i].astype(F32), outer_lanes(halo, i)], 1)


def sds(shape, dtype=F32):
    return jax.ShapeDtypeStruct(shape, dtype)


def wet_of(bl, level):
    return jnp.where(bl > level, 1.0, 0.0)


def latitudes(lat, shape):
    lane = lax.broadcasted_iota(jnp.int32, shape, len(shape) - 1)
    return lat * TY + jnp.where(lane < TY + 64, lane, lane - LANES)


def inside_of(lat, total, shape):
    y = latitudes(lat, shape)
    return jnp.where((y >= 0) & (y < total), 1.0, 0.0)


def pack_lat(sc, u, v, b, l, s, *refs):
    raw, to_down, to_up, flat, made = refs[:5], refs[5], refs[6], refs[7], refs[8:13]
    ub, vb, bb, lb, sb, sem = refs[13:19]
    held, spread, weight_sem = refs[19:24], refs[24], refs[25]
    base = 4 * sc[0]
    lane = lax.broadcasted_iota(jnp.int32, (TX, 128), 1)
    copies = []
    for side, at in enumerate((0, TY - 128)):
        for n, (src, dst) in enumerate(((u, ub), (v, vb), (b, bb))):
            copies.append(pltpu.make_async_copy(src.at[:, :, at : at + 128], dst.at[side], sem.at[side, n]))
    copies = [pltpu.make_async_copy(l, lb, sem.at[0, 3]), pltpu.make_async_copy(s, sb, sem.at[0, 4])] + copies
    more = [pltpu.make_async_copy(src, dst, weight_sem.at[n]) for n, (src, dst) in enumerate(zip(raw, held))]
    for copy in copies + more:
        copy.start()

    def fields(side):
        at = slice(0, 128) if side == 0 else slice(TY - 128, TY)
        bl = lb[:, at].astype(F32)
        wets = [wet_of(bl, (base + k).astype(F32)) for k in range(4)]
        for a in (ub, vb, bb):
            for k in range(4):
                yield a[side, k] * wets[k]
        yield bl
        yield sb[:, at]

    for side, (out, origin) in enumerate(((to_down, 0), (to_up, 128 - EDGE))):
        for copy in copies[:5] if side == 0 else copies[5:]:
            copy.wait()
        for i, field in enumerate(fields(side)):
            tile, place = divmod(i, 7)
            if place == 0:
                acc = jnp.zeros((TX, 128), F32)
            moved = pltpu.roll(field, (EDGE * place - origin) % 128, 1)
            acc = jnp.where((lane >= EDGE * place) & (lane < EDGE * (place + 1)), moved, acc)
            if place == 6:
                out[tile] = acc.astype(BF)
    flat[0] = lb[...].astype(F32)
    flat[1] = sb[...]
    for copy in more:
        copy.wait()
    build_weights(*held, *made, spread)


def bring(sc, flat, done):
    done[...] = flat[0, 0:8, 0:128] + flat[1, 0:8, 0:128]


def pack_lon(total, sc, near, before, after, u, v, b, flat, hal, to_down, to_up, work):
    bl, s = flat.at[0], flat.at[1]
    base = 4 * sc[0]
    lane = lax.broadcasted_iota(jnp.int32, (TX, 128), 1)
    low_from = jnp.where(sc[1] > 0, 128 - EDGE, 128)
    high_to = jnp.where(sc[1] < total // TY - 1, EDGE, 0)
    for tile in range(2):
        low, high = before[tile].astype(F32), after[tile].astype(F32)
        for place in range(7):
            beyond = pltpu.roll(high, (-EDGE * place) % 128, 1)
            short = pltpu.roll(low, (128 - EDGE - EDGE * place) % 128, 1)
            hal[tile * 7 + place] = jnp.where(lane < high_to, beyond, jnp.where(lane >= low_from, short, 0.0))
    for out, row in ((to_down, 0), (to_up, TX - 16)):
        rr = slice(row, row + 16)
        level = bl[rr, :]
        for k in range(4):
            wet = wet_of(level, (base + k).astype(F32))
            for n, a in enumerate((u, v, b)):
                out[4 * n + k] = (a[k, rr, :] * wet).astype(BF)
        out[12] = level.astype(BF)
        out[13] = s[rr, :].astype(BF)
    for out, row in ((to_down, 16), (to_up, 46)):
        rr = slice(row, row + 2)
        level = bl[rr, :]
        for k in range(4):
            wet = wet_of(level, (base + k).astype(F32))
            for n, a in enumerate((u, v)):
                work[2 * (4 * n + k) : 2 * (4 * n + k) + 2, :TY] = a[k, rr, :] * wet
        for i in range(8):
            work[2 * i : 2 * i + 2, TY:] = hal[i, row : row + 2, :]
        out[14] = work[:, :TY].astype(BF)
        near = 0 if row == 16 else TX - 16
        column = lax.broadcasted_iota(jnp.int32, (16, 128), 1)
        blocks = [jnp.zeros((16, 128), F32)] * 4
        for i in range(FIELDS + 1):
            field = hal[i, near : near + 16, :] if i < FIELDS else work[:, TY:]
            for src, n, block, at in SPOTS[i]:
                moved = pltpu.roll(field, (at - src) % 128, 1)
                blocks[block] = jnp.where((column >= at) & (column < at + n), moved, blocks[block])
        out[15] = jnp.concatenate(blocks, 1).astype(BF)


def build_weights(w_in, b_in, w_mid, b_mid, w_out, w1, w2, w3, b1, b2, spread):
    def across(parts, rows, cols):
        rows_all = sum(p.shape[0] for p in parts)
        full = jnp.concatenate(parts + [jnp.zeros((128 - rows_all, 128), F32)], 0)
        return full.T[:rows, :]

    def wide(a):
        return jnp.concatenate([a, jnp.zeros((a.shape[0], 128 - a.shape[1]), F32)], 1)

    zero8 = jnp.zeros((8, 128), F32)
    parts = []
    for a in range(3):
        parts += [wide(w_in[3 * a + b].astype(F32)) for b in range(3)] + [zero8]
    first = across(parts, 32, 96)
    first = jnp.concatenate([first, jnp.zeros((32, 128), F32)], 1)
    for p in range(6):
        w1[32 * p : 32 * p + 32, :] = pltpu.roll(first, 32 * p, 1).astype(BF)
    for b in range(3):
        mid = across([wide(w_mid[3 * a + b].astype(F32)) for a in range(3)], 32, 96)
        mid = jnp.concatenate([mid, jnp.zeros((32, 128), F32)], 1)
        for p in range(6):
            w2[192 * b + 32 * p : 192 * b + 32 * p + 32, :] = pltpu.roll(mid, 32 * p, 1).astype(BF)
        last = jnp.concatenate([w_out[3 * a + b].astype(F32) for a in range(3)] + [jnp.zeros((8, 288), F32)], 1)
        for p in range(8):
            spread[:, p, :] = pltpu.roll(last, 32 * p, 1)
        w3[64 * b : 64 * b + 64, :] = spread[...].reshape(64, 384)[:, :320].astype(BF)
    eye = lax.broadcasted_iota(jnp.int32, (32, 32), 0) == lax.broadcasted_iota(jnp.int32, (32, 32), 1)
    for src, dst in ((b_in, b1), (b_mid, b2)):
        column = jnp.sum(jnp.where(eye, src[...], 0.0), 1, keepdims=True)
        for p in range(6):
            dst[32 * p : 32 * p + 32, :] = jnp.broadcast_to(column, (32, 128))


def load_slots(up, start, count, in0, at):
    for i in range(count):
        c = up[:, start + i, :]
        r = 32 * (at + i)
        in0[r : r + 16, :] = jnp.concatenate([pltpu.roll(c, 1, 1), c], 0).astype(BF)
        in0[r + 16 : r + 32, :] = jnp.concatenate([pltpu.roll(c, LANES - 1, 1), jnp.zeros_like(c)], 0).astype(BF)


def closure(in0, act1, act2, weights, inside, parts, store):
    w1, w2, w3, b1, b2 = weights
    bias1, bias2 = b1[:, :1], b2[:, :1]

    def combined(o, m):
        return pltpu.roll(o[:m], 1, 1) + o[m : 2 * m] + pltpu.roll(o[2 * m :], LANES - 1, 1)

    for s1, _, _, n1, _, _ in parts:
        for j in range(n1):
            r = 32 * (s1 + 6 * j)
            o = jnp.dot(w1[...], in0[r : r + 256, :], preferred_element_type=F32)
            act1[r : r + 192, :] = (jnp.maximum(o + bias1, 0.0) * inside).astype(BF)
    for s1, s2, shift, _, n2, _ in parts:
        for j in range(n2):
            r, to = 32 * (s1 + 6 * j), 32 * (s2 + shift + 6 * j)
            o = combined(jnp.dot(w2[...], act1[r : r + 256, :], preferred_element_type=F32), 192)
            act2[to : to + 192, :] = (jnp.maximum(o + bias2, 0.0) * inside).astype(BF)
    for part, (_, s2, _, _, _, n3) in enumerate(parts):
        for j in range(n3):
            r = 32 * (s2 + 8 * j)
            o = combined(jnp.dot(w3[...], act2[r : r + 320, :], preferred_element_type=F32), 64)
            store(part, j, (closure_coef * o).astype(BF).astype(F32).reshape(8, 8, LANES))


def interior(total, sc, u, v, flat, hal, w1, w2, w3, b1, b2, out, done, up, in0, act1, act2):
    done[...] = jnp.zeros_like(done)

    @pl.when(sc[0] == 0)
    def _():
        level = flat[0]
        for k in range(4):
            wet = wet_of(level, float(k))
            up[k, :, :TY] = u[k] * wet
            up[4 + k, :, :TY] = v[k] * wet
        for i in range(8):
            up[i, :, TY:] = hal[i]
        load_slots(up, 1, 62, in0, 0)
        act1[1920:1984, :] = jnp.zeros((64, LANES), BF)

        def store(part, j, f):
            out[:, 24 + 8 * j : 32 + 8 * j, :] = f

        closure(in0, act1, act2, (w1, w2, w3, b1, b2), inside_of(sc[1], total, (1, LANES)), [(0, 0, 0, 10, 10, 7)], store)


def edges(total, sc, edge, two, w1, w2, w3, b1, b2, inner, out, send, in0, act1, act2):
    @pl.when(sc[0] == 0)
    def _():
        for at, start in ((0, 6), (26, 33)):
            load_slots(edge, start, 26, in0, at)
            act1[32 * at + 768 : 32 * at + 832, :] = jnp.zeros((64, LANES), BF)
        act2[0:160, :] = jnp.zeros((160, LANES), BF)
        act2[29 * 32 + 768 :, :] = jnp.zeros((64, LANES), BF)

        def store(part, j, f):
            row = 80 * part + 8 * j
            out[:, row : row + 8, :] = f

        parts = [(0, 0, 5, 4, 4, 3), (26, 29, 0, 4, 4, 3)]
        closure(in0, act1, act2, (w1, w2, w3, b1, b2), inside_of(sc[1], total, (1, LANES)), parts, store)
        def extra(r):
            level = two[0, r : r + 8, :]
            return forced(sc, level, out, slice(r + 4, r + 12), [slice(0, LANES)], ~inner_rows(r - HALO, level.shape))

        for side, r in enumerate((0, 80)):
            halves = extra(r), extra(r + 8)
            for n in range(2):
                send[2 * n + side] = jnp.concatenate([halves[0][n], halves[1][n]], 0).astype(BF)
        halves = extra(16), extra(72)
        send[4] = jnp.concatenate([halves[0][n] + halves[1][n] for n in range(2)], 0).astype(BF)

    @pl.when(sc[0] != 0)
    def _():
        send[...] = jnp.zeros_like(send)


def pressures(base, b_rows, pr, load, rows):
    for r in range(0, rows, 8):
        run = jnp.zeros((8, pr.shape[2]), F32)
        for k in range(4):
            weighted = b_rows(k, r) * (1.0 + 0.25 * (base + k).astype(F32))
            pr[k, r + 8 : r + 16, :] = run + 0.5 * weighted
            run = run + weighted
        load[r + 8 : r + 16, :] = run


def grads(ref, r):
    here = ref[r + 8 : r + 16, :]
    gx = (ref[r + 9 : r + 17, :] - ref[r + 7 : r + 15, :]) * 0.5
    gy = (pltpu.roll(here, here.shape[1] - 1, 1) - pltpu.roll(here, 1, 1)) * 0.5
    return gx, gy


def open_grads(ref, r):
    here = ref[r + 8 : r + 16, :]
    lane = lax.broadcasted_iota(jnp.int32, here.shape, 1)
    gx = (ref[r + 9 : r + 17, :] - ref[r + 7 : r + 15, :]) * 0.5
    right = jnp.where(lane == TY - 1, 0.0, pltpu.roll(here, TY - 1, 1))
    left = jnp.where(lane == 0, 0.0, pltpu.roll(here, 1, 1))
    return gx, (right - left) * 0.5


def coriolis_of(lat, total, shape):
    return coriolis_base + coriolis_slope * (latitudes(lat, shape).astype(F32) * (1.0 / total) - 0.5)


def sums_of(sc, coriolis, level, east, north, pr, load, r, grads=grads):
    base = 4 * sc[0]
    te = jnp.zeros(level.shape, F32)
    tn, us, vs = te, te, te
    for k in range(4):
        number = (base + k).astype(F32)
        thick = 1.0 + 0.25 * number
        weight = jnp.where(level > number, thick, 0.0)
        drag = jnp.where(level == number + 1.0, drag_coef, 0.0)
        e, n = east(k), north(k)
        gx, gy = grads(pr.at[k], r)
        te = te + weight * (coriolis * n - press_coef * gx - drag * e)
        tn = tn + weight * (-coriolis * e - press_coef * gy - drag * n)
        us = us + thick * e
        vs = vs + thick * n
    below = jnp.zeros(level.shape, F32)
    for k in range(4, 8):
        below = below + jnp.where(level > float(k), 1.0 + 0.25 * k, 0.0)
    gx, gy = grads(load, r)
    below = below * (press_coef * jnp.where(sc[0] == 0, 1.0, 0.0))
    return te - below * gx, tn - below * gy, us, vs, gx, gy


def closed(pr, load):
    for ref in [pr.at[k] for k in range(4)] + [load]:
        end = ref.shape[0]
        ref[0:8, :] = jnp.zeros((8, ref.shape[1]), F32)
        ref[end - 8 : end, :] = jnp.zeros((8, ref.shape[1]), F32)


def forced(sc, level, force, rows, pieces, keep):
    te = jnp.zeros(level.shape, F32)
    tn = te
    for k in range(4):
        weight = jnp.where(level > float(k), 1.0 + 0.25 * k, 0.0)
        fe = [force[k, rows, at] for at in pieces]
        fn = [force[4 + k, rows, at] for at in pieces]
        te = te + weight * (fe[0] if len(fe) == 1 else jnp.concatenate(fe, 1))
        tn = tn + weight * (fn[0] if len(fn) == 1 else jnp.concatenate(fn, 1))
    keep = keep & (jnp.zeros(level.shape, jnp.int32) + sc[0] == 0)
    return jnp.where(keep, te, 0.0), jnp.where(keep, tn, 0.0)


def inner_rows(r, shape):
    x = r + lax.broadcasted_iota(jnp.int32, shape, 0)
    return (x >= 4) & (x < 60)


def middle_sums(total, sc, first, u, v, b, flat, force, sums, send, done, pr, load):
    done[...] = jnp.zeros_like(done)
    base = 4 * sc[0]
    bl, s = flat.at[0], flat.at[1]

    def wet(k, rr):
        return wet_of(bl[rr, :].astype(F32), (base + k).astype(F32))

    def b_rows(k, r):
        rr = slice(r, r + 8)
        return b[k, rr, :] * wet(k, rr)

    pressures(base, b_rows, pr, load, TX)
    closed(pr, load)
    coriolis = coriolis_of(sc[1], total, (8, LANES))[:, :TY]
    for q in range(0, TX, 16):
        halves = []
        for r in (q, q + 8):
            rr = slice(r, r + 8)
            level = bl[rr, :].astype(F32)
            found = sums_of(
                sc, coriolis, level, lambda k: u[k, rr, :] * wet(k, rr), lambda k: v[k, rr, :] * wet(k, rr), pr, load, r, open_grads
            )
            extra = forced(sc, level, force, slice(r + 20, r + 28), [slice(0, TY)], inner_rows(r, level.shape))
            found = (found[0] + extra[0], found[1] + extra[1]) + found[2:]
            for i, a in enumerate(found):
                sums[i, rr, :] = a
            halves.append(found)
        for i in range(4):
            a = jnp.concatenate([halves[0][i], halves[1][i]], 0)
            send[i, q : q + 16, :] = a.astype(BF)
        send[4, q : q + 16, :] = load[q + 8 : q + 24, :].astype(BF)


def seam_sums(total, sc, u, v, b, flat, hal, force, sums, ext, pr, load):
    base = 4 * sc[0]
    bl, s = flat.at[0], flat.at[1]
    last, first = slice(TY - 128, TY), slice(0, 128)

    def three(a, outer, b):
        return jnp.concatenate([a, outer, b], 1)

    for r in range(0, TX, 8):
        rr = slice(r, r + 8)
        levels = [bl[rr, at].astype(F32) for at in (last, first)]
        ext[12, rr, :] = three(levels[0], hal[12, rr, :], levels[1])
        for k in range(4):
            wets = [wet_of(level, (base + k).astype(F32)) for level in levels]
            for n, a in enumerate((u, v, b)):
                ext[4 * n + k, rr, :] = three(a[k, rr, last] * wets[0], hal[4 * n + k, rr, :], a[k, rr, first] * wets[1])
    pressures(base, lambda k, r: ext[8 + k, r : r + 8, :], pr, load, TX)
    closed(pr, load)
    whole = coriolis_of(sc[1], total, (8, LANES))
    coriolis = three(whole[:, last], whole[:, TY:], whole[:, first])
    for r in range(0, TX, 8):
        rr = slice(r, r + 8)
        found = sums_of(sc, coriolis, ext[12, rr, :], lambda k: ext[k, rr, :], lambda k: ext[4 + k, rr, :], pr, load, r)
        pieces = [last, slice(TY, LANES), first]
        extra = forced(sc, ext[12, rr, :], force, slice(r + 20, r + 28), pieces, inner_rows(r, (8, 384)))
        found = (found[0] + extra[0], found[1] + extra[1]) + found[2:] + (load[r + 8 : r + 16, :],)
        for i, a in enumerate(found):
            sums[i, rr, :] = a


def rim_sums(total, sc, ready, u, v, b, flat, hal, low, high, seam, sums, send, two, edge, ext, pr, load):
    base = 4 * sc[0]
    bl, s = flat.at[0], flat.at[1]
    tall = 32
    loads = []
    for side, halo in ((0, low), (1, high)):
        own = slice(0, 16) if side == 0 else slice(TX - 16, TX)
        hr, orr = (slice(0, 16), slice(16, 32)) if side == 0 else (slice(16, 32), slice(0, 16))
        level = bl[own, :].astype(F32)
        for i in range(13):
            ext[i, hr, :] = sent_rows(halo, i)
            ext[i, orr, TY:] = hal[i, own, :]
        for k in range(4):
            wet = wet_of(level, (base + k).astype(F32))
            for n, a in enumerate((u, v, b)):
                ext[4 * n + k, orr, :TY] = a[k, own, :] * wet
        ext[12, orr, :TY] = level
        pressures(base, lambda k, r: ext[8 + k, r : r + 8, :], pr, load, tall)
        for ref in [pr.at[k] for k in range(4)] + [load]:
            if side == 0:
                ref[0:8, :] = jnp.zeros((8, LANES), F32)
            else:
                ref[40:48, :] = jnp.zeros((8, LANES), F32)
        loads.append(load[23:24, :] if side == 0 else load[24:25, :])
        coriolis = coriolis_of(sc[1], total, (8, LANES))
        for j in range(3):
            r = 8 * j + 8 * side
            rr = slice(r, r + 8)
            found = sums_of(sc, coriolis, ext[12, rr, :], lambda k: ext[k, rr, :], lambda k: ext[4 + k, rr, :], pr, load, r)
            for i, a in enumerate(found):
                sums[i, RIM * side + 8 * j : RIM * side + 8 * j + 8, :] = a
        more = sent_rows(halo, 14)
        for i in range(8):
            if side == 0:
                edge[i, 0:8, :] = jnp.zeros((8, LANES), F32)
                edge[i, 8:32, :] = ext[i, 0:24, :]
                edge[i, 6:8, :] = more[2 * i : 2 * i + 2, :]
            else:
                edge[i, 32:56, :] = ext[i, 8:32, :]
                edge[i, 56:64, :] = jnp.zeros((8, LANES), F32)
                edge[i, 56:58, :] = more[2 * i : 2 * i + 2, :]
        at = slice(0, 16) if side == 0 else slice(80, 96)
        two[0, at, :] = sent_rows(halo, 12)
        two[1, at, :] = sent_rows(halo, 13)
    two[0, 16:80, :TY] = bl[...].astype(F32)
    two[1, 16:80, :TY] = s[...]
    for i in range(2):
        two[i, 16:80, TY:] = hal[12 + i]
    lane = lax.broadcasted_iota(jnp.int32, (16, 128), 1)
    for i in range(4):
        for side in range(2):
            at = slice(0, 16) if side == 0 else slice(32, 48)
            packed = sums[i, at, TY:]
            for turn in range(2):
                base = 16 + 34 * turn
                own = slice(16 * (2 * turn + side), 16 * (2 * turn + side) + 16)
                outer, before, after = seam[i, own, 128:256], seam[i, own, 0:128], seam[i, own, 256:384]
                packed = jnp.where((lane >= base) & (lane < base + 16), pltpu.roll(outer, base, 1), packed)
                packed = jnp.where((lane >= base + 16) & (lane < base + 32), pltpu.roll(outer, base + 32, 1), packed)
                packed = jnp.where(lane == base + 32, pltpu.roll(before, base + 33, 1), packed)
                packed = jnp.where(lane == base + 33, pltpu.roll(after, base + 33, 1), packed)
                if i == 0:
                    load_at = seam[6, own, 128:256]
                    packed = jnp.where(lane == 84 + 2 * turn, pltpu.roll(load_at, 84 + 2 * turn, 1), packed)
                    packed = jnp.where(lane == 85 + 2 * turn, pltpu.roll(load_at, 86 + 2 * turn, 1), packed)
            send[2 * i + side, :, :TY] = sums[i, at, :TY].astype(BF)
            send[2 * i + side, :, TY:] = packed.astype(BF)
    ends = [sums[i, row : row + 1, :] for i in range(4) for row in (16, 31)]
    send[8] = jnp.concatenate(ends + loads + [jnp.zeros((6, LANES), F32)], 0).astype(BF)


def own_part(total, sc, u, v, b, flat, hal, low, high, force, out, done, pr, load):
    done[...] = jnp.zeros_like(done)
    base = 4 * sc[0]
    bl, s = flat.at[0], flat.at[1]
    upper = jnp.where(sc[0] == 0, step_dt, 0.0)

    def b_rows(k, r):
        if r == 0:
            return sent_rows(low, 8 + k)[8:16]
        if r == TX + 8:
            return sent_rows(high, 8 + k)[0:8]
        at = slice(r - 8, r)
        wet = wet_of(bl[at, :].astype(F32), (base + k).astype(F32))
        return jnp.concatenate([b[k, at, :] * wet, hal[8 + k, at, :]], 1)

    pressures(base, b_rows, pr, load, TX + 16)
    coriolis = coriolis_of(sc[1], total, (8, LANES))[:, :TY]
    for r in range(0, TX, 8):
        rr = slice(r, r + 8)
        lev = bl[rr, :].astype(F32)
        for k in range(4):
            number = (base + k).astype(F32)
            wet = wet_of(lev, number)
            drag = jnp.where(lev == number + 1.0, drag_coef, 0.0)
            east, north = u[k, rr, :], v[k, rr, :]
            gx, gy = grads(pr.at[k], r + 8)
            te = coriolis * north - press_coef * gx[:, :TY] - drag * east
            tn = -coriolis * east - press_coef * gy[:, :TY] - drag * north
            at = slice(r + 20, r + 28)
            fe = jnp.where(upper > 0.0, force[k, at, :TY], 0.0)
            fn = jnp.where(upper > 0.0, force[4 + k, at, :TY], 0.0)
            out[k, rr, :] = wet * (east + step_dt * (te + fe))
            out[4 + k, rr, :] = wet * (north + step_dt * (tn + fn))


def prepare(total, sc, ready, two, mid, seam, rim, mid_in, rim_in, force, ae, an, es, ns, rel, c2, off, above):
    zero8 = jnp.zeros((8, LANES), F32)
    lane = lax.broadcasted_iota(jnp.int32, (8, 128), 1)

    def ended(i, at, outer):
        first = jnp.where(lane == 0, seam[i, at, 256:384], mid[i, at, 0:128])
        last = jnp.where(lane == 127, seam[i, at, 0:128], mid[i, at, TY - 128 :])
        pieces = [first, mid[i, at, 128 : TY - 128], last]
        return jnp.concatenate(pieces + [seam[i, at, 128:256]] if outer else pieces, 1)

    for r in range(0, ROWS, 8):
        rr = slice(r, r + 8)
        level = two[0, rr, :]
        depth = level + 0.125 * level * (level - 1.0)
        over = 1.0 / jnp.maximum(depth, 1.0)
        rel[rr, :] = depth * (1.0 / TOTAL_DEPTH)
        c2[rr, :] = jnp.where(level > 0.0, 0.5 * sub_dt * gravity, 0.0)
        middle = RIM <= r < ROWS - RIM
        at = r - RIM if middle else (r if r < RIM else r - 48)
        at = slice(at, at + 8)
        x = r - HALO
        found = []
        for i in range(4):
            here = ended(i, slice(x, x + 8), True) if middle else rim[i, at, :]
            if not 0 <= x < TX:
                row = r % 16
                found.append(here + rim_in[2 * i + (x > 0), :, :].astype(F32)[row : row + 8])
                continue
            turn, half = x // 32, x % 16
            base = 16 + 34 * turn
            beyond = rim_in[2 * i + x // 16 % 2, :, TY:].astype(F32)[half : half + 8]
            theirs = mid_in[i, x - half : x - half + 16, :].astype(F32)[half : half + 8]
            outer = jnp.where(lane < 16, pltpu.roll(beyond, 128 - base, 1), pltpu.roll(beyond, 96 - base, 1))
            first = jnp.where(lane == 0, pltpu.roll(beyond, 95 - base, 1), theirs[:, 0:128])
            last = jnp.where(lane == 127, pltpu.roll(beyond, 95 - base, 1), theirs[:, TY - 128 :])
            theirs = jnp.concatenate([first, theirs[:, 128 : TY - 128], last, outer], 1)
            if x in (0, TX - 8):
                end = rim_in[8].astype(F32)[2 * i + (x > 0) : 2 * i + (x > 0) + 1]
                row = lax.broadcasted_iota(jnp.int32, (8, LANES), 0)
                theirs = jnp.where(row == (0 if x == 0 else 7), end, theirs)
            found.append(here + theirs)
        if not middle:
            everywhere = level == level
            mine = forced(sc, level, force, slice(r + 4, r + 12), [slice(0, LANES)], everywhere)
            found[:2] = [found[n] + mine[n] for n in range(2)]
        ae[rr, :] = sub_dt * found[0] * over
        an[rr, :] = sub_dt * found[1] * over
        e, n = found[2] * over, found[3] * over
        es[rr, :], ns[rr, :] = e, n

    @pl.when(sc[0] == 0)
    def _():
        off[0] = es[HALO : HALO + TX, :TY]
        off[1] = ns[HALO : HALO + TX, :TY]

    @pl.when(sc[0] != 0)
    def _():
        lane = lax.broadcasted_iota(jnp.int32, (16, 128), 1)
        for x in range(0, TX, 16):
            turn = x // 32
            beyond = rim_in[x // 16 % 2, :, TY:].astype(F32)
            outer = jnp.where(lane < 64, pltpu.roll(beyond, 44 - 2 * turn, 1), pltpu.roll(beyond, 42 - 2 * turn, 1))
            above[x + 8 : x + 24, :TY] = mid_in[4, x : x + 16, :].astype(F32)
            above[x + 8 : x + 24, TY:] = outer
        ends = rim_in[8].astype(F32)
        above[7:8, :], above[TX + 8 : TX + 9, :] = ends[8:9, :], ends[9:10, :]
        for r in range(0, TX, 8):
            gx, gy = grads(above, r)
            at = slice(r + HALO, r + HALO + 8)
            off[0, r : r + 8, :] = es[at, :TY] + (step_dt * press_coef) * gx[:, :TY]
            off[1, r : r + 8, :] = ns[at, :TY] + (step_dt * press_coef) * gy[:, :TY]


def substeps(total, sc, two, ae_in, an_in, es, ns, rel, c2, off, force_in, own, east_out, north_out, surface_out, lv, fx, fy, eb, nb, ae, an):
    zero8 = jnp.zeros((8, LANES), F32)
    for ref in (lv, fx):
        ref[0:8, :] = zero8
        ref[ROWS + 8 : ROWS + 16, :] = zero8
    share = jnp.where(sc[0] > 0, sub_dt, 0.0)
    for r in range(0, ROWS, 8):
        rr = slice(r, r + 8)
        eb[rr, :], nb[rr, :] = es[rr, :], ns[rr, :]
        lv[r + 8 : r + 16, :] = two[1, rr, :]
        if RIM <= r < ROWS - RIM:
            ae[rr, :], an[rr, :] = ae_in[rr, :], an_in[rr, :]
            continue
        level = two[0, rr, :]
        over = share / jnp.maximum(level + 0.125 * level * (level - 1.0), 1.0)
        row = lax.broadcasted_iota(jnp.int32, (8, LANES), 0)
        for n, (old, new) in enumerate(((ae_in, ae), (an_in, an))):
            if HALO <= r < ROWS - HALO:
                theirs = force_in[4].astype(F32)[8 * n : 8 * n + 8]
                theirs = jnp.where((row < 4) if r < RIM else (row >= 4), theirs, 0.0)
            else:
                half = r % 16
                theirs = force_in[2 * n + (r > RIM), :, :].astype(F32)[half : half + 8]
            new[rr, :] = old[rr, :] + over * theirs
    inside = inside_of(sc[1], total, (8, LANES))

    def step(first, carry):
        for r in range(first, ROWS - first, 8):
            rr = slice(r, r + 8)
            here = lv[r + 8 : r + 16, :]
            dx = lv[r + 9 : r + 17, :] - lv[r + 7 : r + 15, :]
            dy = pltpu.roll(here, LANES - 1, 1) - pltpu.roll(here, 1, 1)
            c = c2[rr, :]
            e = eb[rr, :] + (ae[rr, :] - c * dx)
            n = nb[rr, :] + (an[rr, :] - c * dy)
            eb[rr, :] = e
            nb[rr, :] = n
            fx[r + 8 : r + 16, :] = rel[rr, :] * e
            fy[rr, :] = rel[rr, :] * n
        for r in range(first, ROWS - first, 8):
            rr = slice(r, r + 8)
            dx = fx[r + 9 : r + 17, :] - fx[r + 7 : r + 15, :]
            f = fy[rr, :]
            dy = pltpu.roll(f, LANES - 1, 1) - pltpu.roll(f, 1, 1)
            lv[r + 8 : r + 16, :] = inside * (lv[r + 8 : r + 16, :] - (0.5 * sub_dt) * (dx + dy))
        return carry

    lax.fori_loop(0, NSUB // 2, lambda _, carry: step(0, carry), 0)
    lax.fori_loop(0, NSUB // 2, lambda _, carry: step(8, carry), 0)
    base = 4 * sc[0]
    for q in range(0, TX, 8):
        rr, at = slice(q + HALO, q + HALO + 8), slice(q, q + 8)
        level = two[0, rr, :TY]
        fe = eb[rr, :TY] - off[0, at, :] - (step_dt / sub_dt) * ae[rr, :TY]
        fn = nb[rr, :TY] - off[1, at, :] - (step_dt / sub_dt) * an[rr, :TY]
        for k in range(4):
            wet = wet_of(level, (base + k).astype(F32))
            east_out[k, at, :] = own[k, at, :] + wet * fe
            north_out[k, at, :] = own[4 + k, at, :] + wet * fn
        surface_out[at, :] = lv[q + HALO + 8 : q + HALO + 16, :TY]


def call(kernel, name, out_shape, n_in, scratch=(), in_specs=None, cost=None, grid=(), aliases=None, room=20):
    single = not isinstance(out_shape, (list, tuple))

    def body(*refs):
        kernel((lax.axis_index("grp"), lax.axis_index("lat")), *refs)

    return pl.pallas_call(
        body,
        name=name,
        grid=grid,
        out_shape=out_shape,
        in_specs=in_specs or [VMEM] * n_in,
        out_specs=VMEM if single else [VMEM] * len(out_shape),
        scratch_shapes=list(scratch),
        compiler_params=pltpu.CompilerParams(vmem_limit_bytes=room * 2**20),
        cost_estimate=cost,
        input_output_aliases=aliases or {},
    )


def with_total(kernel, total):
    return lambda sc, *refs: kernel(total, sc, *refs)


def micros(us):
    return pl.CostEstimate(flops=int(us * 1e6), bytes_accessed=int(us * 3e6), transcendentals=0)


def shifted(x, axis, by):
    size = lax.axis_size(axis)
    return lax.ppermute(x, axis, [(i, (i + by) % size) for i in range(size)])


def local(u, v, b, wet_mask, bl, s, w_in, b_in, w_mid, b_mid, w_out):
    total = TY * lax.axis_size("lat")
    wide, half = pltpu.VMEM((2, 4, TX, 128), F32), sds((2, TX, 128), BF)
    made = [sds((192, 256), BF), sds((576, 256), BF), sds((192, 320), BF), sds((192, 128)), sds((192, 128))]
    to_down, to_up, flat, *weights = call(
        pack_lat,
        "pack_lat",
        [half, half, sds((2, TX, TY))] + made,
        10,
        [
            wide,
            wide,
            wide,
            pltpu.VMEM((TX, TY), jnp.int32),
            pltpu.VMEM((TX, TY), F32),
            pltpu.SemaphoreType.DMA((2, 5)),
            pltpu.VMEM((9, 8, 32), BF),
            pltpu.VMEM((1, 32), F32),
            pltpu.VMEM((9, 32, 32), BF),
            pltpu.VMEM((1, 32), F32),
            pltpu.VMEM((9, 8, 32), BF),
            pltpu.VMEM((8, 8, 384), F32),
            pltpu.SemaphoreType.DMA((5,)),
        ],
        in_specs=[pl.BlockSpec(memory_space=pltpu.HBM)] * 10,
        room=60,
    )(u, v, b, bl, s, w_in, b_in[None, :], w_mid, b_mid[None, :], jnp.swapaxes(w_out, 1, 2))
    before = shifted(to_up, "lat", 1)
    after = shifted(to_down, "lat", -1)

    near = call(bring, "bring", TOKEN, 1, cost=micros(1))(flat)

    out = sds((16, 16, TY), BF)
    hal, down, up = call(
        with_total(pack_lon, total),
        "pack_lon",
        [sds((FIELDS, TX, 128)), out, out],
        7,
        [pltpu.VMEM((16, LANES), F32)],
    )(near, before, after, u, v, b, flat)
    low = shifted(up, "lon", 1)
    high = shifted(down, "lon", -1)
    inner, ready = call(
        with_total(interior, total),
        "interior",
        [sds((8, FORCED, LANES)), TOKEN],
        9,
        [
            pltpu.VMEM((8, TX, LANES), F32),
            pltpu.VMEM((62 * 32, LANES), BF),
            pltpu.VMEM((62 * 32, LANES), BF),
            pltpu.VMEM((60 * 32, LANES), BF),
        ],
        cost=micros(7),
    )(u, v, flat, hal, *weights)
    mid, mid_send, summed = call(
        with_total(middle_sums, total),
        "middle_sums",
        [sds((6, TX, TY)), sds((5, TX, TY), BF), TOKEN],
        6,
        [pltpu.VMEM((4, TX + 16, TY), F32), pltpu.VMEM((TX + 16, TY), F32)],
        cost=micros(1),
    )(ready, u, v, b, flat, inner)
    mid_in = shifted(mid_send, "grp", 1)
    seam = call(
        with_total(seam_sums, total),
        "seam_sums",
        sds((7, TX, 384)),
        6,
        [pltpu.VMEM((13, TX, 384), F32), pltpu.VMEM((4, TX + 16, 384), F32), pltpu.VMEM((TX + 16, 384), F32)],
        cost=micros(1),
    )(u, v, b, flat, hal, inner)
    rim, rim_send, two, edge = call(
        with_total(rim_sums, total),
        "rim_sums",
        [sds((6, 48, LANES)), sds((9, 16, LANES), BF), sds((2, ROWS, LANES)), sds((8, 64, LANES))],
        9,
        [pltpu.VMEM((13, 32, LANES), F32), pltpu.VMEM((4, 48, LANES), F32), pltpu.VMEM((48, LANES), F32)],
        cost=micros(2),
    )(summed, u, v, b, flat, hal, low, high, seam)
    rim_in = shifted(rim_send, "grp", 1)
    force, force_send = call(
        with_total(edges, total),
        "edges",
        [sds((8, FORCED, LANES)), sds((5, 16, LANES), BF)],
        8,
        [pltpu.VMEM((52 * 32, LANES), BF), pltpu.VMEM((52 * 32, LANES), BF), pltpu.VMEM((55 * 32, LANES), BF)],
        cost=micros(6),
        aliases={7: 0},
    )(edge, two, *weights, inner)
    force_in = shifted(force_send, "grp", 1)
    own, owned = call(
        with_total(own_part, total),
        "own_part",
        [sds((8, TX, TY)), TOKEN],
        8,
        [pltpu.VMEM((4, 96, LANES), F32), pltpu.VMEM((96, LANES), F32)],
        cost=micros(2),
    )(u, v, b, flat, hal, low, high, force)
    start = call(
        with_total(prepare, total),
        "prepare",
        [sds((ROWS, LANES))] * 6 + [sds((2, TX, TY))],
        8,
        [pltpu.VMEM((TX + 16, LANES), F32)],
        cost=micros(1),
    )(owned, two, mid, seam, rim, mid_in, rim_in, force)
    plane = pltpu.VMEM((ROWS, LANES), F32)
    tall = pltpu.VMEM((ROWS + 16, LANES), F32)
    return tuple(
        call(
            with_total(substeps, total),
            "substeps",
            [sds((4, TX, TY)), sds((4, TX, TY)), sds((TX, TY))],
            10,
            [tall, tall] + [plane] * 5,
            cost=micros(5),
        )(two, *start, force_in, own)
    )


def solution(mesh):
    tile = P("grp", "lon", "lat")
    flat = P("lon", "lat")
    return jax.shard_map(
        local,
        mesh=mesh,
        in_specs=(tile, tile, tile, tile, flat, flat, P(), P(), P(), P(), P()),
        out_specs=(tile, tile, flat),
        check_vma=False,
    )
```

```python
import jax
import jax.numpy as jnp
from jax import lax
from jax.experimental import pallas as pl
from jax.experimental.pallas import tpu as pltpu
from jax.sharding import PartitionSpec as P

NSUB = 8
TX, TY = 64, 512
LANES = 640
ROWS = 96
HALO = 16
RIM = 24
EDGE = 18
FORCED = 104
FIELDS = 14
F32 = jnp.float32
BF = jnp.bfloat16

coriolis_base = 0.6
coriolis_slope = 0.8
press_coef = 0.3
drag_coef = 0.5
step_dt = 0.2
closure_coef = 0.5
gravity = 1.0
sub_dt = 0.4
TOTAL_DEPTH = 15.0

TOKEN = jax.ShapeDtypeStruct((8, 128), jnp.float32)
VMEM = pl.BlockSpec(memory_space=pltpu.VMEM)


def placed(n, *spots):
    return [(src, n, block, at) for src, (block, at) in zip((0, 128 - n), spots)]


SPOTS = (
    [placed(EDGE, (1 + i // 3, 36 * (i % 3)), (1 + i // 3, 36 * (i % 3) + 18)) for i in range(8)]
    + [placed(16, (0, 32 * k), (0, 32 * k + 16)) for k in range(4)]
    + [placed(16, (3, 72), (3, 88)), placed(16, (2, 108), (3, 104)), placed(4, (1, 108), (1, 112))]
)


def outer_lanes(halo, i):
    lane = lax.broadcasted_iota(jnp.int32, (16, 128), 1)
    found = jnp.zeros((16, 128), F32)
    for src, n, block, at in SPOTS[i]:
        moved = pltpu.roll(halo[15, :, 128 * block : 128 * block + 128].astype(F32), (src - at) % 128, 1)
        found = jnp.where((lane >= src) & (lane < src + n), moved, found)
    return found


def sent_rows(halo, i):
    return jnp.concatenate([halo[i].astype(F32), outer_lanes(halo, i)], 1)


def sds(shape, dtype=F32):
    return jax.ShapeDtypeStruct(shape, dtype)


def wet_of(bl, level):
    return jnp.where(bl > level, 1.0, 0.0)


def latitudes(lat, shape):
    lane = lax.broadcasted_iota(jnp.int32, shape, len(shape) - 1)
    return lat * TY + jnp.where(lane < TY + 64, lane, lane - LANES)


def inside_of(lat, total, shape):
    y = latitudes(lat, shape)
    return jnp.where((y >= 0) & (y < total), 1.0, 0.0)


def pack_lat(sc, u, v, b, l, s, *refs):
    raw, to_down, to_up, flat, made = refs[:5], refs[5], refs[6], refs[7], refs[8:13]
    ub, vb, bb, lb, sb, sem = refs[13:19]
    held, spread, weight_sem = refs[19:24], refs[24], refs[25]
    base = 4 * sc[0]
    lane = lax.broadcasted_iota(jnp.int32, (TX, 128), 1)
    copies = []
    for side, at in enumerate((0, TY - 128)):
        for n, (src, dst) in enumerate(((u, ub), (v, vb), (b, bb))):
            copies.append(pltpu.make_async_copy(src.at[:, :, at : at + 128], dst.at[side], sem.at[side, n]))
    copies = [pltpu.make_async_copy(l, lb, sem.at[0, 3]), pltpu.make_async_copy(s, sb, sem.at[0, 4])] + copies
    more = [pltpu.make_async_copy(src, dst, weight_sem.at[n]) for n, (src, dst) in enumerate(zip(raw, held))]
    for copy in copies + more:
        copy.start()

    def fields(side):
        at = slice(0, 128) if side == 0 else slice(TY - 128, TY)
        bl = lb[:, at].astype(F32)
        wets = [wet_of(bl, (base + k).astype(F32)) for k in range(4)]
        for a in (ub, vb, bb):
            for k in range(4):
                yield a[side, k] * wets[k]
        yield bl
        yield sb[:, at]

    for side, (out, origin) in enumerate(((to_down, 0), (to_up, 128 - EDGE))):
        for copy in copies[:5] if side == 0 else copies[5:]:
            copy.wait()
        for i, field in enumerate(fields(side)):
            tile, place = divmod(i, 7)
            if place == 0:
                acc = jnp.zeros((TX, 128), F32)
            moved = pltpu.roll(field, (EDGE * place - origin) % 128, 1)
            acc = jnp.where((lane >= EDGE * place) & (lane < EDGE * (place + 1)), moved, acc)
            if place == 6:
                out[tile] = acc.astype(BF)
    flat[0] = lb[...].astype(F32)
    flat[1] = sb[...]
    for copy in more:
        copy.wait()
    build_weights(*held, *made, spread)


def bring(sc, flat, done):
    done[...] = flat[0, 0:8, 0:128] + flat[1, 0:8, 0:128]


def pack_lon(total, sc, near, before, after, u, v, b, flat, hal, to_down, to_up, work):
    bl, s = flat.at[0], flat.at[1]
    base = 4 * sc[0]
    lane = lax.broadcasted_iota(jnp.int32, (TX, 128), 1)
    low_from = jnp.where(sc[1] > 0, 128 - EDGE, 128)
    high_to = jnp.where(sc[1] < total // TY - 1, EDGE, 0)
    for tile in range(2):
        low, high = before[tile].astype(F32), after[tile].astype(F32)
        for place in range(7):
            beyond = pltpu.roll(high, (-EDGE * place) % 128, 1)
            short = pltpu.roll(low, (128 - EDGE - EDGE * place) % 128, 1)
            hal[tile * 7 + place] = jnp.where(lane < high_to, beyond, jnp.where(lane >= low_from, short, 0.0))
    for out, row in ((to_down, 0), (to_up, TX - 16)):
        rr = slice(row, row + 16)
        level = bl[rr, :]
        for k in range(4):
            wet = wet_of(level, (base + k).astype(F32))
            for n, a in enumerate((u, v, b)):
                out[4 * n + k] = (a[k, rr, :] * wet).astype(BF)
        out[12] = level.astype(BF)
        out[13] = s[rr, :].astype(BF)
    for out, row in ((to_down, 16), (to_up, 46)):
        rr = slice(row, row + 2)
        level = bl[rr, :]
        for k in range(4):
            wet = wet_of(level, (base + k).astype(F32))
            for n, a in enumerate((u, v)):
                work[2 * (4 * n + k) : 2 * (4 * n + k) + 2, :TY] = a[k, rr, :] * wet
        for i in range(8):
            work[2 * i : 2 * i + 2, TY:] = hal[i, row : row + 2, :]
        out[14] = work[:, :TY].astype(BF)
        near = 0 if row == 16 else TX - 16
        column = lax.broadcasted_iota(jnp.int32, (16, 128), 1)
        blocks = [jnp.zeros((16, 128), F32)] * 4
        for i in range(FIELDS + 1):
            field = hal[i, near : near + 16, :] if i < FIELDS else work[:, TY:]
            for src, n, block, at in SPOTS[i]:
                moved = pltpu.roll(field, (at - src) % 128, 1)
                blocks[block] = jnp.where((column >= at) & (column < at + n), moved, blocks[block])
        out[15] = jnp.concatenate(blocks, 1).astype(BF)


def build_weights(w_in, b_in, w_mid, b_mid, w_out, w1, w2, w3, b1, b2, spread):
    def across(parts, rows, cols):
        rows_all = sum(p.shape[0] for p in parts)
        full = jnp.concatenate(parts + [jnp.zeros((128 - rows_all, 128), F32)], 0)
        return full.T[:rows, :]

    def wide(a):
        return jnp.concatenate([a, jnp.zeros((a.shape[0], 128 - a.shape[1]), F32)], 1)

    zero8 = jnp.zeros((8, 128), F32)
    parts = []
    for a in range(3):
        parts += [wide(w_in[3 * a + b].astype(F32)) for b in range(3)] + [zero8]
    first = across(parts, 32, 96)
    first = jnp.concatenate([first, jnp.zeros((32, 128), F32)], 1)
    for p in range(6):
        w1[32 * p : 32 * p + 32, :] = pltpu.roll(first, 32 * p, 1).astype(BF)
    for b in range(3):
        mid = across([wide(w_mid[3 * a + b].astype(F32)) for a in range(3)], 32, 96)
        mid = jnp.concatenate([mid, jnp.zeros((32, 128), F32)], 1)
        for p in range(6):
            w2[192 * b + 32 * p : 192 * b + 32 * p + 32, :] = pltpu.roll(mid, 32 * p, 1).astype(BF)
        last = jnp.concatenate([w_out[3 * a + b].astype(F32) for a in range(3)] + [jnp.zeros((8, 288), F32)], 1)
        for p in range(8):
            spread[:, p, :] = pltpu.roll(last, 32 * p, 1)
        w3[64 * b : 64 * b + 64, :] = spread[...].reshape(64, 384)[:, :320].astype(BF)
    eye = lax.broadcasted_iota(jnp.int32, (32, 32), 0) == lax.broadcasted_iota(jnp.int32, (32, 32), 1)
    for src, dst in ((b_in, b1), (b_mid, b2)):
        column = jnp.sum(jnp.where(eye, src[...], 0.0), 1, keepdims=True)
        for p in range(6):
            dst[32 * p : 32 * p + 32, :] = jnp.broadcast_to(column, (32, 128))


def load_slots(up, start, count, in0, at):
    for i in range(count):
        c = up[:, start + i, :]
        r = 32 * (at + i)
        in0[r : r + 16, :] = jnp.concatenate([pltpu.roll(c, 1, 1), c], 0).astype(BF)
        in0[r + 16 : r + 32, :] = jnp.concatenate([pltpu.roll(c, LANES - 1, 1), jnp.zeros_like(c)], 0).astype(BF)


def closure(in0, act1, act2, weights, inside, parts, store):
    w1, w2, w3, b1, b2 = weights
    bias1, bias2 = b1[:, :1], b2[:, :1]

    def combined(o, m):
        return pltpu.roll(o[:m], 1, 1) + o[m : 2 * m] + pltpu.roll(o[2 * m :], LANES - 1, 1)

    for s1, _, _, n1, _, _ in parts:
        for j in range(n1):
            r = 32 * (s1 + 6 * j)
            o = jnp.dot(w1[...], in0[r : r + 256, :], preferred_element_type=F32)
            act1[r : r + 192, :] = (jnp.maximum(o + bias1, 0.0) * inside).astype(BF)
    for s1, s2, shift, _, n2, _ in parts:
        for j in range(n2):
            r, to = 32 * (s1 + 6 * j), 32 * (s2 + shift + 6 * j)
            o = combined(jnp.dot(w2[...], act1[r : r + 256, :], preferred_element_type=F32), 192)
            act2[to : to + 192, :] = (jnp.maximum(o + bias2, 0.0) * inside).astype(BF)
    for part, (_, s2, _, _, _, n3) in enumerate(parts):
        for j in range(n3):
            r = 32 * (s2 + 8 * j)
            o = combined(jnp.dot(w3[...], act2[r : r + 320, :], preferred_element_type=F32), 64)
            store(part, j, (closure_coef * o).astype(BF).astype(F32).reshape(8, 8, LANES))


def interior(total, sc, u, v, flat, hal, w1, w2, w3, b1, b2, out, done, up, in0, act1, act2):
    done[...] = jnp.zeros_like(done)

    @pl.when(sc[0] == 0)
    def _():
        level = flat[0]
        for k in range(4):
            wet = wet_of(level, float(k))
            up[k, :, :TY] = u[k] * wet
            up[4 + k, :, :TY] = v[k] * wet
        for i in range(8):
            up[i, :, TY:] = hal[i]
        load_slots(up, 1, 62, in0, 0)
        act1[1920:1984, :] = jnp.zeros((64, LANES), BF)

        def store(part, j, f):
            out[:, 24 + 8 * j : 32 + 8 * j, :] = f

        closure(in0, act1, act2, (w1, w2, w3, b1, b2), inside_of(sc[1], total, (1, LANES)), [(0, 0, 0, 10, 10, 7)], store)


def edges(total, sc, edge, two, w1, w2, w3, b1, b2, inner, out, send, in0, act1, act2):
    @pl.when(sc[0] == 0)
    def _():
        for at, start in ((0, 6), (26, 33)):
            load_slots(edge, start, 26, in0, at)
            act1[32 * at + 768 : 32 * at + 832, :] = jnp.zeros((64, LANES), BF)
        act2[0:160, :] = jnp.zeros((160, LANES), BF)
        act2[29 * 32 + 768 :, :] = jnp.zeros((64, LANES), BF)

        def store(part, j, f):
            row = 80 * part + 8 * j
            out[:, row : row + 8, :] = f

        parts = [(0, 0, 5, 4, 4, 3), (26, 29, 0, 4, 4, 3)]
        closure(in0, act1, act2, (w1, w2, w3, b1, b2), inside_of(sc[1], total, (1, LANES)), parts, store)
        def extra(r):
            level = two[0, r : r + 8, :]
            return forced(sc, level, out, slice(r + 4, r + 12), [slice(0, LANES)], ~inner_rows(r - HALO, level.shape))

        for side, r in enumerate((0, 80)):
            halves = extra(r), extra(r + 8)
            for n in range(2):
                send[2 * n + side] = jnp.concatenate([halves[0][n], halves[1][n]], 0).astype(BF)
        halves = extra(16), extra(72)
        send[4] = jnp.concatenate([halves[0][n] + halves[1][n] for n in range(2)], 0).astype(BF)

    @pl.when(sc[0] != 0)
    def _():
        send[...] = jnp.zeros_like(send)


def pressures(base, b_rows, pr, load, rows):
    for r in range(0, rows, 8):
        run = jnp.zeros((8, pr.shape[2]), F32)
        for k in range(4):
            weighted = b_rows(k, r) * (1.0 + 0.25 * (base + k).astype(F32))
            pr[k, r + 8 : r + 16, :] = run + 0.5 * weighted
            run = run + weighted
        load[r + 8 : r + 16, :] = run


def grads(ref, r):
    here = ref[r + 8 : r + 16, :]
    gx = (ref[r + 9 : r + 17, :] - ref[r + 7 : r + 15, :]) * 0.5
    gy = (pltpu.roll(here, here.shape[1] - 1, 1) - pltpu.roll(here, 1, 1)) * 0.5
    return gx, gy


def open_grads(ref, r):
    here = ref[r + 8 : r + 16, :]
    lane = lax.broadcasted_iota(jnp.int32, here.shape, 1)
    gx = (ref[r + 9 : r + 17, :] - ref[r + 7 : r + 15, :]) * 0.5
    right = jnp.where(lane == TY - 1, 0.0, pltpu.roll(here, TY - 1, 1))
    left = jnp.where(lane == 0, 0.0, pltpu.roll(here, 1, 1))
    return gx, (right - left) * 0.5


def coriolis_of(lat, total, shape):
    return coriolis_base + coriolis_slope * (latitudes(lat, shape).astype(F32) * (1.0 / total) - 0.5)


def sums_of(sc, coriolis, level, east, north, pr, load, r, grads=grads):
    base = 4 * sc[0]
    te = jnp.zeros(level.shape, F32)
    tn, us, vs = te, te, te
    for k in range(4):
        number = (base + k).astype(F32)
        thick = 1.0 + 0.25 * number
        weight = jnp.where(level > number, thick, 0.0)
        drag = jnp.where(level == number + 1.0, drag_coef, 0.0)
        e, n = east(k), north(k)
        gx, gy = grads(pr.at[k], r)
        te = te + weight * (coriolis * n - press_coef * gx - drag * e)
        tn = tn + weight * (-coriolis * e - press_coef * gy - drag * n)
        us = us + thick * e
        vs = vs + thick * n
    below = jnp.zeros(level.shape, F32)
    for k in range(4, 8):
        below = below + jnp.where(level > float(k), 1.0 + 0.25 * k, 0.0)
    gx, gy = grads(load, r)
    below = below * (press_coef * jnp.where(sc[0] == 0, 1.0, 0.0))
    return te - below * gx, tn - below * gy, us, vs, gx, gy


def closed(pr, load):
    for ref in [pr.at[k] for k in range(4)] + [load]:
        end = ref.shape[0]
        ref[0:8, :] = jnp.zeros((8, ref.shape[1]), F32)
        ref[end - 8 : end, :] = jnp.zeros((8, ref.shape[1]), F32)


def forced(sc, level, force, rows, pieces, keep):
    te = jnp.zeros(level.shape, F32)
    tn = te
    for k in range(4):
        weight = jnp.where(level > float(k), 1.0 + 0.25 * k, 0.0)
        fe = [force[k, rows, at] for at in pieces]
        fn = [force[4 + k, rows, at] for at in pieces]
        te = te + weight * (fe[0] if len(fe) == 1 else jnp.concatenate(fe, 1))
        tn = tn + weight * (fn[0] if len(fn) == 1 else jnp.concatenate(fn, 1))
    keep = keep & (jnp.zeros(level.shape, jnp.int32) + sc[0] == 0)
    return jnp.where(keep, te, 0.0), jnp.where(keep, tn, 0.0)


def inner_rows(r, shape):
    x = r + lax.broadcasted_iota(jnp.int32, shape, 0)
    return (x >= 4) & (x < 60)


def middle_sums(total, sc, first, u, v, b, flat, force, sums, send, done, pr, load):
    done[...] = jnp.zeros_like(done)
    base = 4 * sc[0]
    bl, s = flat.at[0], flat.at[1]

    def wet(k, rr):
        return wet_of(bl[rr, :].astype(F32), (base + k).astype(F32))

    def b_rows(k, r):
        rr = slice(r, r + 8)
        return b[k, rr, :] * wet(k, rr)

    pressures(base, b_rows, pr, load, TX)
    closed(pr, load)
    coriolis = coriolis_of(sc[1], total, (8, LANES))[:, :TY]
    for q in range(0, TX, 16):
        halves = []
        for r in (q, q + 8):
            rr = slice(r, r + 8)
            level = bl[rr, :].astype(F32)
            found = sums_of(
                sc, coriolis, level, lambda k: u[k, rr, :] * wet(k, rr), lambda k: v[k, rr, :] * wet(k, rr), pr, load, r, open_grads
            )
            extra = forced(sc, level, force, slice(r + 20, r + 28), [slice(0, TY)], inner_rows(r, level.shape))
            found = (found[0] + extra[0], found[1] + extra[1]) + found[2:]
            for i, a in enumerate(found):
                sums[i, rr, :] = a
            halves.append(found)
        for i in range(4):
            a = jnp.concatenate([halves[0][i], halves[1][i]], 0)
            send[i, q : q + 16, :] = a.astype(BF)
        send[4, q : q + 16, :] = load[q + 8 : q + 24, :].astype(BF)


def seam_sums(total, sc, u, v, b, flat, hal, force, sums, ext, pr, load):
    base = 4 * sc[0]
    bl, s = flat.at[0], flat.at[1]
    last, first = slice(TY - 128, TY), slice(0, 128)

    def three(a, outer, b):
        return jnp.concatenate([a, outer, b], 1)

    for r in range(0, TX, 8):
        rr = slice(r, r + 8)
        levels = [bl[rr, at].astype(F32) for at in (last, first)]
        ext[12, rr, :] = three(levels[0], hal[12, rr, :], levels[1])
        for k in range(4):
            wets = [wet_of(level, (base + k).astype(F32)) for level in levels]
            for n, a in enumerate((u, v, b)):
                ext[4 * n + k, rr, :] = three(a[k, rr, last] * wets[0], hal[4 * n + k, rr, :], a[k, rr, first] * wets[1])
    pressures(base, lambda k, r: ext[8 + k, r : r + 8, :], pr, load, TX)
    closed(pr, load)
    whole = coriolis_of(sc[1], total, (8, LANES))
    coriolis = three(whole[:, last], whole[:, TY:], whole[:, first])
    for r in range(0, TX, 8):
        rr = slice(r, r + 8)
        found = sums_of(sc, coriolis, ext[12, rr, :], lambda k: ext[k, rr, :], lambda k: ext[4 + k, rr, :], pr, load, r)
        pieces = [last, slice(TY, LANES), first]
        extra = forced(sc, ext[12, rr, :], force, slice(r + 20, r + 28), pieces, inner_rows(r, (8, 384)))
        found = (found[0] + extra[0], found[1] + extra[1]) + found[2:] + (load[r + 8 : r + 16, :],)
        for i, a in enumerate(found):
            sums[i, rr, :] = a


def rim_sums(total, sc, ready, u, v, b, flat, hal, low, high, seam, sums, send, two, edge, ext, pr, load):
    base = 4 * sc[0]
    bl, s = flat.at[0], flat.at[1]
    tall = 32
    loads = []
    for side, halo in ((0, low), (1, high)):
        own = slice(0, 16) if side == 0 else slice(TX - 16, TX)
        hr, orr = (slice(0, 16), slice(16, 32)) if side == 0 else (slice(16, 32), slice(0, 16))
        level = bl[own, :].astype(F32)
        for i in range(13):
            ext[i, hr, :] = sent_rows(halo, i)
            ext[i, orr, TY:] = hal[i, own, :]
        for k in range(4):
            wet = wet_of(level, (base + k).astype(F32))
            for n, a in enumerate((u, v, b)):
                ext[4 * n + k, orr, :TY] = a[k, own, :] * wet
        ext[12, orr, :TY] = level
        pressures(base, lambda k, r: ext[8 + k, r : r + 8, :], pr, load, tall)
        for ref in [pr.at[k] for k in range(4)] + [load]:
            if side == 0:
                ref[0:8, :] = jnp.zeros((8, LANES), F32)
            else:
                ref[40:48, :] = jnp.zeros((8, LANES), F32)
        loads.append(load[23:24, :] if side == 0 else load[24:25, :])
        coriolis = coriolis_of(sc[1], total, (8, LANES))
        for j in range(3):
            r = 8 * j + 8 * side
            rr = slice(r, r + 8)
            found = sums_of(sc, coriolis, ext[12, rr, :], lambda k: ext[k, rr, :], lambda k: ext[4 + k, rr, :], pr, load, r)
            for i, a in enumerate(found):
                sums[i, RIM * side + 8 * j : RIM * side + 8 * j + 8, :] = a
        more = sent_rows(halo, 14)
        for i in range(8):
            if side == 0:
                edge[i, 0:8, :] = jnp.zeros((8, LANES), F32)
                edge[i, 8:32, :] = ext[i, 0:24, :]
                edge[i, 6:8, :] = more[2 * i : 2 * i + 2, :]
            else:
                edge[i, 32:56, :] = ext[i, 8:32, :]
                edge[i, 56:64, :] = jnp.zeros((8, LANES), F32)
                edge[i, 56:58, :] = more[2 * i : 2 * i + 2, :]
        at = slice(0, 16) if side == 0 else slice(80, 96)
        two[0, at, :] = sent_rows(halo, 12)
        two[1, at, :] = sent_rows(halo, 13)
    two[0, 16:80, :TY] = bl[...].astype(F32)
    two[1, 16:80, :TY] = s[...]
    for i in range(2):
        two[i, 16:80, TY:] = hal[12 + i]
    lane = lax.broadcasted_iota(jnp.int32, (16, 128), 1)
    for i in range(4):
        for side in range(2):
            at = slice(0, 16) if side == 0 else slice(32, 48)
            packed = sums[i, at, TY:]
            for turn in range(2):
                base = 16 + 34 * turn
                own = slice(16 * (2 * turn + side), 16 * (2 * turn + side) + 16)
                outer, before, after = seam[i, own, 128:256], seam[i, own, 0:128], seam[i, own, 256:384]
                packed = jnp.where((lane >= base) & (lane < base + 16), pltpu.roll(outer, base, 1), packed)
                packed = jnp.where((lane >= base + 16) & (lane < base + 32), pltpu.roll(outer, base + 32, 1), packed)
                packed = jnp.where(lane == base + 32, pltpu.roll(before, base + 33, 1), packed)
                packed = jnp.where(lane == base + 33, pltpu.roll(after, base + 33, 1), packed)
                if i == 0:
                    load_at = seam[6, own, 128:256]
                    packed = jnp.where(lane == 84 + 2 * turn, pltpu.roll(load_at, 84 + 2 * turn, 1), packed)
                    packed = jnp.where(lane == 85 + 2 * turn, pltpu.roll(load_at, 86 + 2 * turn, 1), packed)
            send[2 * i + side, :, :TY] = sums[i, at, :TY].astype(BF)
            send[2 * i + side, :, TY:] = packed.astype(BF)
    ends = [sums[i, row : row + 1, :] for i in range(4) for row in (16, 31)]
    send[8] = jnp.concatenate(ends + loads + [jnp.zeros((6, LANES), F32)], 0).astype(BF)


def own_part(total, sc, u, v, b, flat, hal, low, high, force, out, done, pr, load):
    done[...] = jnp.zeros_like(done)
    base = 4 * sc[0]
    bl, s = flat.at[0], flat.at[1]
    upper = jnp.where(sc[0] == 0, step_dt, 0.0)

    def b_rows(k, r):
        if r == 0:
            return sent_rows(low, 8 + k)[8:16]
        if r == TX + 8:
            return sent_rows(high, 8 + k)[0:8]
        at = slice(r - 8, r)
        wet = wet_of(bl[at, :].astype(F32), (base + k).astype(F32))
        return jnp.concatenate([b[k, at, :] * wet, hal[8 + k, at, :]], 1)

    pressures(base, b_rows, pr, load, TX + 16)
    coriolis = coriolis_of(sc[1], total, (8, LANES))[:, :TY]
    for r in range(0, TX, 8):
        rr = slice(r, r + 8)
        lev = bl[rr, :].astype(F32)
        for k in range(4):
            number = (base + k).astype(F32)
            wet = wet_of(lev, number)
            drag = jnp.where(lev == number + 1.0, drag_coef, 0.0)
            east, north = u[k, rr, :], v[k, rr, :]
            gx, gy = grads(pr.at[k], r + 8)
            te = coriolis * north - press_coef * gx[:, :TY] - drag * east
            tn = -coriolis * east - press_coef * gy[:, :TY] - drag * north
            at = slice(r + 20, r + 28)
            fe = jnp.where(upper > 0.0, force[k, at, :TY], 0.0)
            fn = jnp.where(upper > 0.0, force[4 + k, at, :TY], 0.0)
            out[k, rr, :] = wet * (east + step_dt * (te + fe))
            out[4 + k, rr, :] = wet * (north + step_dt * (tn + fn))


def prepare(total, sc, ready, two, mid, seam, rim, mid_in, rim_in, force, ae, an, es, ns, rel, c2, off, above):
    zero8 = jnp.zeros((8, LANES), F32)
    lane = lax.broadcasted_iota(jnp.int32, (8, 128), 1)

    def ended(i, at, outer):
        first = jnp.where(lane == 0, seam[i, at, 256:384], mid[i, at, 0:128])
        last = jnp.where(lane == 127, seam[i, at, 0:128], mid[i, at, TY - 128 :])
        pieces = [first, mid[i, at, 128 : TY - 128], last]
        return jnp.concatenate(pieces + [seam[i, at, 128:256]] if outer else pieces, 1)

    for r in range(0, ROWS, 8):
        rr = slice(r, r + 8)
        level = two[0, rr, :]
        depth = level + 0.125 * level * (level - 1.0)
        over = 1.0 / jnp.maximum(depth, 1.0)
        rel[rr, :] = depth * (1.0 / TOTAL_DEPTH)
        c2[rr, :] = jnp.where(level > 0.0, 0.5 * sub_dt * gravity, 0.0)
        middle = RIM <= r < ROWS - RIM
        at = r - RIM if middle else (r if r < RIM else r - 48)
        at = slice(at, at + 8)
        x = r - HALO
        found = []
        for i in range(4):
            here = ended(i, slice(x, x + 8), True) if middle else rim[i, at, :]
            if not 0 <= x < TX:
                row = r % 16
                found.append(here + rim_in[2 * i + (x > 0), :, :].astype(F32)[row : row + 8])
                continue
            turn, half = x // 32, x % 16
            base = 16 + 34 * turn
            beyond = rim_in[2 * i + x // 16 % 2, :, TY:].astype(F32)[half : half + 8]
            theirs = mid_in[i, x - half : x - half + 16, :].astype(F32)[half : half + 8]
            outer = jnp.where(lane < 16, pltpu.roll(beyond, 128 - base, 1), pltpu.roll(beyond, 96 - base, 1))
            first = jnp.where(lane == 0, pltpu.roll(beyond, 95 - base, 1), theirs[:, 0:128])
            last = jnp.where(lane == 127, pltpu.roll(beyond, 95 - base, 1), theirs[:, TY - 128 :])
            theirs = jnp.concatenate([first, theirs[:, 128 : TY - 128], last, outer], 1)
            if x in (0, TX - 8):
                end = rim_in[8].astype(F32)[2 * i + (x > 0) : 2 * i + (x > 0) + 1]
                row = lax.broadcasted_iota(jnp.int32, (8, LANES), 0)
                theirs = jnp.where(row == (0 if x == 0 else 7), end, theirs)
            found.append(here + theirs)
        if not middle:
            everywhere = level == level
            mine = forced(sc, level, force, slice(r + 4, r + 12), [slice(0, LANES)], everywhere)
            found[:2] = [found[n] + mine[n] for n in range(2)]
        ae[rr, :] = sub_dt * found[0] * over
        an[rr, :] = sub_dt * found[1] * over
        e, n = found[2] * over, found[3] * over
        es[rr, :], ns[rr, :] = e, n

    @pl.when(sc[0] == 0)
    def _():
        off[0] = es[HALO : HALO + TX, :TY]
        off[1] = ns[HALO : HALO + TX, :TY]

    @pl.when(sc[0] != 0)
    def _():
        lane = lax.broadcasted_iota(jnp.int32, (16, 128), 1)
        for x in range(0, TX, 16):
            turn = x // 32
            beyond = rim_in[x // 16 % 2, :, TY:].astype(F32)
            outer = jnp.where(lane < 64, pltpu.roll(beyond, 44 - 2 * turn, 1), pltpu.roll(beyond, 42 - 2 * turn, 1))
            above[x + 8 : x + 24, :TY] = mid_in[4, x : x + 16, :].astype(F32)
            above[x + 8 : x + 24, TY:] = outer
        ends = rim_in[8].astype(F32)
        above[7:8, :], above[TX + 8 : TX + 9, :] = ends[8:9, :], ends[9:10, :]
        for r in range(0, TX, 8):
            gx, gy = grads(above, r)
            at = slice(r + HALO, r + HALO + 8)
            off[0, r : r + 8, :] = es[at, :TY] + (step_dt * press_coef) * gx[:, :TY]
            off[1, r : r + 8, :] = ns[at, :TY] + (step_dt * press_coef) * gy[:, :TY]


def substeps(total, sc, two, ae_in, an_in, es, ns, rel, c2, off, force_in, own, east_out, north_out, surface_out, lv, fx, fy, eb, nb, ae, an):
    zero8 = jnp.zeros((8, LANES), F32)
    for ref in (lv, fx):
        ref[0:8, :] = zero8
        ref[ROWS + 8 : ROWS + 16, :] = zero8
    share = jnp.where(sc[0] > 0, sub_dt, 0.0)
    for r in range(0, ROWS, 8):
        rr = slice(r, r + 8)
        eb[rr, :], nb[rr, :] = es[rr, :], ns[rr, :]
        lv[r + 8 : r + 16, :] = two[1, rr, :]
        if RIM <= r < ROWS - RIM:
            ae[rr, :], an[rr, :] = ae_in[rr, :], an_in[rr, :]
            continue
        level = two[0, rr, :]
        over = share / jnp.maximum(level + 0.125 * level * (level - 1.0), 1.0)
        row = lax.broadcasted_iota(jnp.int32, (8, LANES), 0)
        for n, (old, new) in enumerate(((ae_in, ae), (an_in, an))):
            if HALO <= r < ROWS - HALO:
                theirs = force_in[4].astype(F32)[8 * n : 8 * n + 8]
                theirs = jnp.where((row < 4) if r < RIM else (row >= 4), theirs, 0.0)
            else:
                half = r % 16
                theirs = force_in[2 * n + (r > RIM), :, :].astype(F32)[half : half + 8]
            new[rr, :] = old[rr, :] + over * theirs
    inside = inside_of(sc[1], total, (8, LANES))

    def step(first, carry):
        for r in range(first, ROWS - first, 8):
            rr = slice(r, r + 8)
            here = lv[r + 8 : r + 16, :]
            dx = lv[r + 9 : r + 17, :] - lv[r + 7 : r + 15, :]
            dy = pltpu.roll(here, LANES - 1, 1) - pltpu.roll(here, 1, 1)
            c = c2[rr, :]
            e = eb[rr, :] + (ae[rr, :] - c * dx)
            n = nb[rr, :] + (an[rr, :] - c * dy)
            eb[rr, :] = e
            nb[rr, :] = n
            fx[r + 8 : r + 16, :] = rel[rr, :] * e
            fy[rr, :] = rel[rr, :] * n
        for r in range(first, ROWS - first, 8):
            rr = slice(r, r + 8)
            dx = fx[r + 9 : r + 17, :] - fx[r + 7 : r + 15, :]
            f = fy[rr, :]
            dy = pltpu.roll(f, LANES - 1, 1) - pltpu.roll(f, 1, 1)
            lv[r + 8 : r + 16, :] = inside * (lv[r + 8 : r + 16, :] - (0.5 * sub_dt) * (dx + dy))
        return carry

    lax.fori_loop(0, NSUB // 2, lambda _, carry: step(0, carry), 0, unroll=4)
    lax.fori_loop(0, NSUB // 2, lambda _, carry: step(8, carry), 0, unroll=4)
    base = 4 * sc[0]
    for q in range(0, TX, 8):
        rr, at = slice(q + HALO, q + HALO + 8), slice(q, q + 8)
        level = two[0, rr, :TY]
        fe = eb[rr, :TY] - off[0, at, :] - (step_dt / sub_dt) * ae[rr, :TY]
        fn = nb[rr, :TY] - off[1, at, :] - (step_dt / sub_dt) * an[rr, :TY]
        for k in range(4):
            wet = wet_of(level, (base + k).astype(F32))
            east_out[k, at, :] = own[k, at, :] + wet * fe
            north_out[k, at, :] = own[4 + k, at, :] + wet * fn
        surface_out[at, :] = lv[q + HALO + 8 : q + HALO + 16, :TY]


def call(kernel, name, out_shape, n_in, scratch=(), in_specs=None, cost=None, grid=(), aliases=None, room=20):
    single = not isinstance(out_shape, (list, tuple))

    def body(*refs):
        kernel((lax.axis_index("grp"), lax.axis_index("lat")), *refs)

    return pl.pallas_call(
        body,
        name=name,
        grid=grid,
        out_shape=out_shape,
        in_specs=in_specs or [VMEM] * n_in,
        out_specs=VMEM if single else [VMEM] * len(out_shape),
        scratch_shapes=list(scratch),
        compiler_params=pltpu.CompilerParams(vmem_limit_bytes=room * 2**20),
        cost_estimate=cost,
        input_output_aliases=aliases or {},
    )


def with_total(kernel, total):
    return lambda sc, *refs: kernel(total, sc, *refs)


def micros(us):
    return pl.CostEstimate(flops=int(us * 1e6), bytes_accessed=int(us * 3e6), transcendentals=0)


def shifted(x, axis, by):
    size = lax.axis_size(axis)
    return lax.ppermute(x, axis, [(i, (i + by) % size) for i in range(size)])


def local(u, v, b, wet_mask, bl, s, w_in, b_in, w_mid, b_mid, w_out):
    total = TY * lax.axis_size("lat")
    wide, half = pltpu.VMEM((2, 4, TX, 128), F32), sds((2, TX, 128), BF)
    made = [sds((192, 256), BF), sds((576, 256), BF), sds((192, 320), BF), sds((192, 128)), sds((192, 128))]
    to_down, to_up, flat, *weights = call(
        pack_lat,
        "pack_lat",
        [half, half, sds((2, TX, TY))] + made,
        10,
        [
            wide,
            wide,
            wide,
            pltpu.VMEM((TX, TY), jnp.int32),
            pltpu.VMEM((TX, TY), F32),
            pltpu.SemaphoreType.DMA((2, 5)),
            pltpu.VMEM((9, 8, 32), BF),
            pltpu.VMEM((1, 32), F32),
            pltpu.VMEM((9, 32, 32), BF),
            pltpu.VMEM((1, 32), F32),
            pltpu.VMEM((9, 8, 32), BF),
            pltpu.VMEM((8, 8, 384), F32),
            pltpu.SemaphoreType.DMA((5,)),
        ],
        in_specs=[pl.BlockSpec(memory_space=pltpu.HBM)] * 10,
        room=60,
    )(u, v, b, bl, s, w_in, b_in[None, :], w_mid, b_mid[None, :], jnp.swapaxes(w_out, 1, 2))
    before = shifted(to_up, "lat", 1)
    after = shifted(to_down, "lat", -1)

    near = call(bring, "bring", TOKEN, 1, cost=micros(1))(flat)

    out = sds((16, 16, TY), BF)
    hal, down, up = call(
        with_total(pack_lon, total),
        "pack_lon",
        [sds((FIELDS, TX, 128)), out, out],
        7,
        [pltpu.VMEM((16, LANES), F32)],
    )(near, before, after, u, v, b, flat)
    low = shifted(up, "lon", 1)
    high = shifted(down, "lon", -1)
    inner, ready = call(
        with_total(interior, total),
        "interior",
        [sds((8, FORCED, LANES)), TOKEN],
        9,
        [
            pltpu.VMEM((8, TX, LANES), F32),
            pltpu.VMEM((62 * 32, LANES), BF),
            pltpu.VMEM((62 * 32, LANES), BF),
            pltpu.VMEM((60 * 32, LANES), BF),
        ],
        cost=micros(7),
    )(u, v, flat, hal, *weights)
    mid, mid_send, summed = call(
        with_total(middle_sums, total),
        "middle_sums",
        [sds((6, TX, TY)), sds((5, TX, TY), BF), TOKEN],
        6,
        [pltpu.VMEM((4, TX + 16, TY), F32), pltpu.VMEM((TX + 16, TY), F32)],
        cost=micros(1),
    )(ready, u, v, b, flat, inner)
    mid_in = shifted(mid_send, "grp", 1)
    seam = call(
        with_total(seam_sums, total),
        "seam_sums",
        sds((7, TX, 384)),
        6,
        [pltpu.VMEM((13, TX, 384), F32), pltpu.VMEM((4, TX + 16, 384), F32), pltpu.VMEM((TX + 16, 384), F32)],
        cost=micros(1),
    )(u, v, b, flat, hal, inner)
    rim, rim_send, two, edge = call(
        with_total(rim_sums, total),
        "rim_sums",
        [sds((6, 48, LANES)), sds((9, 16, LANES), BF), sds((2, ROWS, LANES)), sds((8, 64, LANES))],
        9,
        [pltpu.VMEM((13, 32, LANES), F32), pltpu.VMEM((4, 48, LANES), F32), pltpu.VMEM((48, LANES), F32)],
        cost=micros(2),
    )(summed, u, v, b, flat, hal, low, high, seam)
    rim_in = shifted(rim_send, "grp", 1)
    force, force_send = call(
        with_total(edges, total),
        "edges",
        [sds((8, FORCED, LANES)), sds((5, 16, LANES), BF)],
        8,
        [pltpu.VMEM((52 * 32, LANES), BF), pltpu.VMEM((52 * 32, LANES), BF), pltpu.VMEM((55 * 32, LANES), BF)],
        cost=micros(6),
        aliases={7: 0},
    )(edge, two, *weights, inner)
    force_in = shifted(force_send, "grp", 1)
    own, owned = call(
        with_total(own_part, total),
        "own_part",
        [sds((8, TX, TY)), TOKEN],
        8,
        [pltpu.VMEM((4, 96, LANES), F32), pltpu.VMEM((96, LANES), F32)],
        cost=micros(2),
    )(u, v, b, flat, hal, low, high, force)
    start = call(
        with_total(prepare, total),
        "prepare",
        [sds((ROWS, LANES))] * 6 + [sds((2, TX, TY))],
        8,
        [pltpu.VMEM((TX + 16, LANES), F32)],
        cost=micros(1),
    )(owned, two, mid, seam, rim, mid_in, rim_in, force)
    plane = pltpu.VMEM((ROWS, LANES), F32)
    tall = pltpu.VMEM((ROWS + 16, LANES), F32)
    return tuple(
        call(
            with_total(substeps, total),
            "substeps",
            [sds((4, TX, TY)), sds((4, TX, TY)), sds((TX, TY))],
            10,
            [tall, tall] + [plane] * 5,
            cost=micros(5),
        )(two, *start, force_in, own)
    )


def solution(mesh):
    tile = P("grp", "lon", "lat")
    flat = P("lon", "lat")
    return jax.shard_map(
        local,
        mesh=mesh,
        in_specs=(tile, tile, tile, tile, flat, flat, P(), P(), P(), P(), P()),
        out_specs=(tile, tile, flat),
        check_vma=False,
    )
```

```python
import jax
import jax.numpy as jnp
from jax import lax
from jax.experimental import pallas as pl
from jax.experimental.pallas import tpu as pltpu
from jax.sharding import PartitionSpec as P

NSUB = 8
TX, TY = 64, 512
LANES = 640
ROWS = 96
HALO = 16
RIM = 24
EDGE = 18
FORCED = 104
FIELDS = 14
F32 = jnp.float32
BF = jnp.bfloat16

coriolis_base = 0.6
coriolis_slope = 0.8
press_coef = 0.3
drag_coef = 0.5
step_dt = 0.2
closure_coef = 0.5
gravity = 1.0
sub_dt = 0.4
TOTAL_DEPTH = 15.0

TOKEN = jax.ShapeDtypeStruct((8, 128), jnp.float32)
VMEM = pl.BlockSpec(memory_space=pltpu.VMEM)


def placed(n, *spots):
    return [(src, n, block, at) for src, (block, at) in zip((0, 128 - n), spots)]


SPOTS = (
    [placed(EDGE, (1 + i // 3, 36 * (i % 3)), (1 + i // 3, 36 * (i % 3) + 18)) for i in range(8)]
    + [placed(16, (0, 32 * k), (0, 32 * k + 16)) for k in range(4)]
    + [placed(16, (3, 72), (3, 88)), placed(16, (2, 108), (3, 104)), placed(4, (1, 108), (1, 112))]
)


def outer_lanes(halo, i):
    lane = lax.broadcasted_iota(jnp.int32, (16, 128), 1)
    found = jnp.zeros((16, 128), F32)
    for src, n, block, at in SPOTS[i]:
        moved = pltpu.roll(halo[15, :, 128 * block : 128 * block + 128].astype(F32), (src - at) % 128, 1)
        found = jnp.where((lane >= src) & (lane < src + n), moved, found)
    return found


def sent_rows(halo, i):
    return jnp.concatenate([halo[i].astype(F32), outer_lanes(halo, i)], 1)


def sds(shape, dtype=F32):
    return jax.ShapeDtypeStruct(shape, dtype)


def wet_of(bl, level):
    return jnp.where(bl > level, 1.0, 0.0)


def latitudes(lat, shape):
    lane = lax.broadcasted_iota(jnp.int32, shape, len(shape) - 1)
    return lat * TY + jnp.where(lane < TY + 64, lane, lane - LANES)


def inside_of(lat, total, shape):
    y = latitudes(lat, shape)
    return jnp.where((y >= 0) & (y < total), 1.0, 0.0)


def pack_lat(sc, u, v, b, l, s, *refs):
    raw, to_down, to_up, flat, made = refs[:5], refs[5], refs[6], refs[7], refs[8:13]
    ub, vb, bb, lb, sb, sem = refs[13:19]
    held, spread, weight_sem = refs[19:24], refs[24], refs[25]
    base = 4 * sc[0]
    lane = lax.broadcasted_iota(jnp.int32, (TX, 128), 1)
    copies = []
    for side, at in enumerate((0, TY - 128)):
        for n, (src, dst) in enumerate(((u, ub), (v, vb), (b, bb))):
            copies.append(pltpu.make_async_copy(src.at[:, :, at : at + 128], dst.at[side], sem.at[side, n]))
    copies = [pltpu.make_async_copy(l, lb, sem.at[0, 3]), pltpu.make_async_copy(s, sb, sem.at[0, 4])] + copies
    more = [pltpu.make_async_copy(src, dst, weight_sem.at[n]) for n, (src, dst) in enumerate(zip(raw, held))]
    for copy in copies + more:
        copy.start()

    def fields(side):
        at = slice(0, 128) if side == 0 else slice(TY - 128, TY)
        bl = lb[:, at].astype(F32)
        wets = [wet_of(bl, (base + k).astype(F32)) for k in range(4)]
        for a in (ub, vb, bb):
            for k in range(4):
                yield a[side, k] * wets[k]
        yield bl
        yield sb[:, at]

    for side, (out, origin) in enumerate(((to_down, 0), (to_up, 128 - EDGE))):
        for copy in copies[:5] if side == 0 else copies[5:]:
            copy.wait()
        for i, field in enumerate(fields(side)):
            tile, place = divmod(i, 7)
            if place == 0:
                acc = jnp.zeros((TX, 128), F32)
            moved = pltpu.roll(field, (EDGE * place - origin) % 128, 1)
            acc = jnp.where((lane >= EDGE * place) & (lane < EDGE * (place + 1)), moved, acc)
            if place == 6:
                out[tile] = acc.astype(BF)
    flat[0] = lb[...].astype(F32)
    flat[1] = sb[...]
    for copy in more:
        copy.wait()
    build_weights(*held, *made, spread)


def bring(sc, flat, done):
    done[...] = flat[0, 0:8, 0:128] + flat[1, 0:8, 0:128]


def pack_lon(total, sc, near, before, after, u, v, b, flat, hal, to_down, to_up, work):
    bl, s = flat.at[0], flat.at[1]
    base = 4 * sc[0]
    lane = lax.broadcasted_iota(jnp.int32, (TX, 128), 1)
    low_from = jnp.where(sc[1] > 0, 128 - EDGE, 128)
    high_to = jnp.where(sc[1] < total // TY - 1, EDGE, 0)
    for tile in range(2):
        low, high = before[tile].astype(F32), after[tile].astype(F32)
        for place in range(7):
            beyond = pltpu.roll(high, (-EDGE * place) % 128, 1)
            short = pltpu.roll(low, (128 - EDGE - EDGE * place) % 128, 1)
            hal[tile * 7 + place] = jnp.where(lane < high_to, beyond, jnp.where(lane >= low_from, short, 0.0))
    for out, row in ((to_down, 0), (to_up, TX - 16)):
        rr = slice(row, row + 16)
        level = bl[rr, :]
        for k in range(4):
            wet = wet_of(level, (base + k).astype(F32))
            for n, a in enumerate((u, v, b)):
                out[4 * n + k] = (a[k, rr, :] * wet).astype(BF)
        out[12] = level.astype(BF)
        out[13] = s[rr, :].astype(BF)
    for out, row in ((to_down, 16), (to_up, 46)):
        rr = slice(row, row + 2)
        level = bl[rr, :]
        for k in range(4):
            wet = wet_of(level, (base + k).astype(F32))
            for n, a in enumerate((u, v)):
                work[2 * (4 * n + k) : 2 * (4 * n + k) + 2, :TY] = a[k, rr, :] * wet
        for i in range(8):
            work[2 * i : 2 * i + 2, TY:] = hal[i, row : row + 2, :]
        out[14] = work[:, :TY].astype(BF)
        near = 0 if row == 16 else TX - 16
        column = lax.broadcasted_iota(jnp.int32, (16, 128), 1)
        blocks = [jnp.zeros((16, 128), F32)] * 4
        for i in range(FIELDS + 1):
            field = hal[i, near : near + 16, :] if i < FIELDS else work[:, TY:]
            for src, n, block, at in SPOTS[i]:
                moved = pltpu.roll(field, (at - src) % 128, 1)
                blocks[block] = jnp.where((column >= at) & (column < at + n), moved, blocks[block])
        out[15] = jnp.concatenate(blocks, 1).astype(BF)


def build_weights(w_in, b_in, w_mid, b_mid, w_out, w1, w2, w3, b1, b2, spread):
    def across(parts, rows, cols):
        rows_all = sum(p.shape[0] for p in parts)
        full = jnp.concatenate(parts + [jnp.zeros((128 - rows_all, 128), F32)], 0)
        return full.T[:rows, :]

    def wide(a):
        return jnp.concatenate([a, jnp.zeros((a.shape[0], 128 - a.shape[1]), F32)], 1)

    zero8 = jnp.zeros((8, 128), F32)
    parts = []
    for a in range(3):
        parts += [wide(w_in[3 * a + b].astype(F32)) for b in range(3)] + [zero8]
    first = across(parts, 32, 96)
    first = jnp.concatenate([first, jnp.zeros((32, 128), F32)], 1)
    for p in range(6):
        w1[32 * p : 32 * p + 32, :] = pltpu.roll(first, 32 * p, 1).astype(BF)
    for b in range(3):
        mid = across([wide(w_mid[3 * a + b].astype(F32)) for a in range(3)], 32, 96)
        mid = jnp.concatenate([mid, jnp.zeros((32, 128), F32)], 1)
        for p in range(6):
            w2[192 * b + 32 * p : 192 * b + 32 * p + 32, :] = pltpu.roll(mid, 32 * p, 1).astype(BF)
        last = jnp.concatenate([w_out[3 * a + b].astype(F32) for a in range(3)] + [jnp.zeros((8, 288), F32)], 1)
        for p in range(8):
            spread[:, p, :] = pltpu.roll(last, 32 * p, 1)
        w3[64 * b : 64 * b + 64, :] = spread[...].reshape(64, 384)[:, :320].astype(BF)
    eye = lax.broadcasted_iota(jnp.int32, (32, 32), 0) == lax.broadcasted_iota(jnp.int32, (32, 32), 1)
    for src, dst in ((b_in, b1), (b_mid, b2)):
        column = jnp.sum(jnp.where(eye, src[...], 0.0), 1, keepdims=True)
        dst[...] = jnp.broadcast_to(column, (32, 128))


def load_slots(up, start, count, in0, at):
    for i in range(count):
        c = up[:, start + i, :]
        r = 32 * (at + i)
        in0[r : r + 16, :] = jnp.concatenate([pltpu.roll(c, 1, 1), c], 0).astype(BF)
        in0[r + 16 : r + 32, :] = jnp.concatenate([pltpu.roll(c, LANES - 1, 1), jnp.zeros_like(c)], 0).astype(BF)


def closure(in0, act1, act2, weights, inside, parts, store):
    w1, w2, w3, b1, b2 = weights
    bias1, bias2 = (jnp.concatenate([b[:, :1]] * 6, 0) for b in (b1, b2))

    def combined(o, m):
        return pltpu.roll(o[:m], 1, 1) + o[m : 2 * m] + pltpu.roll(o[2 * m :], LANES - 1, 1)

    for s1, _, _, n1, _, _ in parts:
        for j in range(n1):
            r = 32 * (s1 + 6 * j)
            o = jnp.dot(w1[...], in0[r : r + 256, :], preferred_element_type=F32)
            act1[r : r + 192, :] = (jnp.maximum(o + bias1, 0.0) * inside).astype(BF)
    for s1, s2, shift, _, n2, _ in parts:
        for j in range(n2):
            r, to = 32 * (s1 + 6 * j), 32 * (s2 + shift + 6 * j)
            o = combined(jnp.dot(w2[...], act1[r : r + 256, :], preferred_element_type=F32), 192)
            act2[to : to + 192, :] = (jnp.maximum(o + bias2, 0.0) * inside).astype(BF)
    for part, (_, s2, _, _, _, n3) in enumerate(parts):
        for j in range(n3):
            r = 32 * (s2 + 8 * j)
            o = combined(jnp.dot(w3[...], act2[r : r + 320, :], preferred_element_type=F32), 64)
            store(part, j, (closure_coef * o).astype(BF).astype(F32).reshape(8, 8, LANES))


def interior(total, sc, u, v, flat, hal, w1, w2, w3, b1, b2, out, done, up, in0, act1, act2):
    done[...] = jnp.zeros_like(done)

    @pl.when(sc[0] == 0)
    def _():
        level = flat[0]
        for k in range(4):
            wet = wet_of(level, float(k))
            up[k, :, :TY] = u[k] * wet
            up[4 + k, :, :TY] = v[k] * wet
        for i in range(8):
            up[i, :, TY:] = hal[i]
        load_slots(up, 1, 62, in0, 0)
        act1[1920:1984, :] = jnp.zeros((64, LANES), BF)

        def store(part, j, f):
            out[:, 24 + 8 * j : 32 + 8 * j, :] = f

        closure(in0, act1, act2, (w1, w2, w3, b1, b2), inside_of(sc[1], total, (1, LANES)), [(0, 0, 0, 10, 10, 7)], store)


def edges(total, sc, edge, two, w1, w2, w3, b1, b2, inner, out, send, in0, act1, act2):
    @pl.when(sc[0] == 0)
    def _():
        for at, start in ((0, 6), (26, 33)):
            load_slots(edge, start, 26, in0, at)
            act1[32 * at + 768 : 32 * at + 832, :] = jnp.zeros((64, LANES), BF)
        act2[0:160, :] = jnp.zeros((160, LANES), BF)
        act2[29 * 32 + 768 :, :] = jnp.zeros((64, LANES), BF)

        def store(part, j, f):
            row = 80 * part + 8 * j
            out[:, row : row + 8, :] = f

        parts = [(0, 0, 5, 4, 4, 3), (26, 29, 0, 4, 4, 3)]
        closure(in0, act1, act2, (w1, w2, w3, b1, b2), inside_of(sc[1], total, (1, LANES)), parts, store)
        def extra(r):
            level = two[0, r : r + 8, :]
            return forced(sc, level, out, slice(r + 4, r + 12), [slice(0, LANES)], ~inner_rows(r - HALO, level.shape))

        for side, r in enumerate((0, 80)):
            halves = extra(r), extra(r + 8)
            for n in range(2):
                send[2 * n + side] = jnp.concatenate([halves[0][n], halves[1][n]], 0).astype(BF)
        halves = extra(16), extra(72)
        send[4] = jnp.concatenate([halves[0][n] + halves[1][n] for n in range(2)], 0).astype(BF)

    @pl.when(sc[0] != 0)
    def _():
        send[...] = jnp.zeros_like(send)


def pressures(base, b_rows, pr, load, rows):
    for r in range(0, rows, 8):
        run = jnp.zeros((8, pr.shape[2]), F32)
        for k in range(4):
            weighted = b_rows(k, r) * (1.0 + 0.25 * (base + k).astype(F32))
            pr[k, r + 8 : r + 16, :] = run + 0.5 * weighted
            run = run + weighted
        load[r + 8 : r + 16, :] = run


def grads(ref, r):
    here = ref[r + 8 : r + 16, :]
    gx = (ref[r + 9 : r + 17, :] - ref[r + 7 : r + 15, :]) * 0.5
    gy = (pltpu.roll(here, here.shape[1] - 1, 1) - pltpu.roll(here, 1, 1)) * 0.5
    return gx, gy


def open_grads(ref, r):
    here = ref[r + 8 : r + 16, :]
    lane = lax.broadcasted_iota(jnp.int32, here.shape, 1)
    gx = (ref[r + 9 : r + 17, :] - ref[r + 7 : r + 15, :]) * 0.5
    right = jnp.where(lane == TY - 1, 0.0, pltpu.roll(here, TY - 1, 1))
    left = jnp.where(lane == 0, 0.0, pltpu.roll(here, 1, 1))
    return gx, (right - left) * 0.5


def coriolis_of(lat, total, shape):
    return coriolis_base + coriolis_slope * (latitudes(lat, shape).astype(F32) * (1.0 / total) - 0.5)


def sums_of(sc, coriolis, level, east, north, pr, load, r, grads=grads):
    base = 4 * sc[0]
    te = jnp.zeros(level.shape, F32)
    tn, us, vs = te, te, te
    for k in range(4):
        number = (base + k).astype(F32)
        thick = 1.0 + 0.25 * number
        weight = jnp.where(level > number, thick, 0.0)
        drag = jnp.where(level == number + 1.0, drag_coef, 0.0)
        e, n = east(k), north(k)
        gx, gy = grads(pr.at[k], r)
        te = te + weight * (coriolis * n - press_coef * gx - drag * e)
        tn = tn + weight * (-coriolis * e - press_coef * gy - drag * n)
        us = us + thick * e
        vs = vs + thick * n
    below = jnp.zeros(level.shape, F32)
    for k in range(4, 8):
        below = below + jnp.where(level > float(k), 1.0 + 0.25 * k, 0.0)
    gx, gy = grads(load, r)
    below = below * (press_coef * jnp.where(sc[0] == 0, 1.0, 0.0))
    return te - below * gx, tn - below * gy, us, vs, gx, gy


def closed(pr, load):
    for ref in [pr.at[k] for k in range(4)] + [load]:
        end = ref.shape[0]
        ref[0:8, :] = jnp.zeros((8, ref.shape[1]), F32)
        ref[end - 8 : end, :] = jnp.zeros((8, ref.shape[1]), F32)


def forced(sc, level, force, rows, pieces, keep):
    te = jnp.zeros(level.shape, F32)
    tn = te
    for k in range(4):
        weight = jnp.where(level > float(k), 1.0 + 0.25 * k, 0.0)
        fe = [force[k, rows, at] for at in pieces]
        fn = [force[4 + k, rows, at] for at in pieces]
        te = te + weight * (fe[0] if len(fe) == 1 else jnp.concatenate(fe, 1))
        tn = tn + weight * (fn[0] if len(fn) == 1 else jnp.concatenate(fn, 1))
    keep = keep & (jnp.zeros(level.shape, jnp.int32) + sc[0] == 0)
    return jnp.where(keep, te, 0.0), jnp.where(keep, tn, 0.0)


def inner_rows(r, shape):
    x = r + lax.broadcasted_iota(jnp.int32, shape, 0)
    return (x >= 4) & (x < 60)


def middle_sums(total, sc, first, u, v, b, flat, force, sums, send, done, pr, load):
    done[...] = jnp.zeros_like(done)
    base = 4 * sc[0]
    bl, s = flat.at[0], flat.at[1]

    def wet(k, rr):
        return wet_of(bl[rr, :].astype(F32), (base + k).astype(F32))

    def b_rows(k, r):
        rr = slice(r, r + 8)
        return b[k, rr, :] * wet(k, rr)

    pressures(base, b_rows, pr, load, TX)
    closed(pr, load)
    coriolis = coriolis_of(sc[1], total, (8, LANES))[:, :TY]
    for q in range(0, TX, 16):
        halves = []
        for r in (q, q + 8):
            rr = slice(r, r + 8)
            level = bl[rr, :].astype(F32)
            found = sums_of(
                sc, coriolis, level, lambda k: u[k, rr, :] * wet(k, rr), lambda k: v[k, rr, :] * wet(k, rr), pr, load, r, open_grads
            )
            extra = forced(sc, level, force, slice(r + 20, r + 28), [slice(0, TY)], inner_rows(r, level.shape))
            found = (found[0] + extra[0], found[1] + extra[1]) + found[2:]
            for i, a in enumerate(found):
                sums[i, rr, :] = a
            halves.append(found)
        for i in range(4):
            a = jnp.concatenate([halves[0][i], halves[1][i]], 0)
            send[i, q : q + 16, :] = a.astype(BF)
        send[4, q : q + 16, :] = load[q + 8 : q + 24, :].astype(BF)


def seam_sums(total, sc, u, v, b, flat, hal, force, sums, ext, pr, load):
    base = 4 * sc[0]
    bl, s = flat.at[0], flat.at[1]
    last, first = slice(TY - 128, TY), slice(0, 128)

    def three(a, outer, b):
        return jnp.concatenate([a, outer, b], 1)

    for r in range(0, TX, 8):
        rr = slice(r, r + 8)
        levels = [bl[rr, at].astype(F32) for at in (last, first)]
        ext[12, rr, :] = three(levels[0], hal[12, rr, :], levels[1])
        for k in range(4):
            wets = [wet_of(level, (base + k).astype(F32)) for level in levels]
            for n, a in enumerate((u, v, b)):
                ext[4 * n + k, rr, :] = three(a[k, rr, last] * wets[0], hal[4 * n + k, rr, :], a[k, rr, first] * wets[1])
    pressures(base, lambda k, r: ext[8 + k, r : r + 8, :], pr, load, TX)
    closed(pr, load)
    whole = coriolis_of(sc[1], total, (8, LANES))
    coriolis = three(whole[:, last], whole[:, TY:], whole[:, first])
    for r in range(0, TX, 8):
        rr = slice(r, r + 8)
        found = sums_of(sc, coriolis, ext[12, rr, :], lambda k: ext[k, rr, :], lambda k: ext[4 + k, rr, :], pr, load, r)
        pieces = [last, slice(TY, LANES), first]
        extra = forced(sc, ext[12, rr, :], force, slice(r + 20, r + 28), pieces, inner_rows(r, (8, 384)))
        found = (found[0] + extra[0], found[1] + extra[1]) + found[2:] + (load[r + 8 : r + 16, :],)
        for i, a in enumerate(found):
            sums[i, rr, :] = a


def rim_sums(total, sc, ready, u, v, b, flat, hal, low, high, seam, sums, send, two, edge, ext, pr, load):
    base = 4 * sc[0]
    bl, s = flat.at[0], flat.at[1]
    tall = 32
    loads = []
    for side, halo in ((0, low), (1, high)):
        own = slice(0, 16) if side == 0 else slice(TX - 16, TX)
        hr, orr = (slice(0, 16), slice(16, 32)) if side == 0 else (slice(16, 32), slice(0, 16))
        level = bl[own, :].astype(F32)
        for i in range(13):
            ext[i, hr, :] = sent_rows(halo, i)
            ext[i, orr, TY:] = hal[i, own, :]
        for k in range(4):
            wet = wet_of(level, (base + k).astype(F32))
            for n, a in enumerate((u, v, b)):
                ext[4 * n + k, orr, :TY] = a[k, own, :] * wet
        ext[12, orr, :TY] = level
        pressures(base, lambda k, r: ext[8 + k, r : r + 8, :], pr, load, tall)
        for ref in [pr.at[k] for k in range(4)] + [load]:
            if side == 0:
                ref[0:8, :] = jnp.zeros((8, LANES), F32)
            else:
                ref[40:48, :] = jnp.zeros((8, LANES), F32)
        loads.append(load[23:24, :] if side == 0 else load[24:25, :])
        coriolis = coriolis_of(sc[1], total, (8, LANES))
        for j in range(3):
            r = 8 * j + 8 * side
            rr = slice(r, r + 8)
            found = sums_of(sc, coriolis, ext[12, rr, :], lambda k: ext[k, rr, :], lambda k: ext[4 + k, rr, :], pr, load, r)
            for i, a in enumerate(found):
                sums[i, RIM * side + 8 * j : RIM * side + 8 * j + 8, :] = a
        more = sent_rows(halo, 14)
        for i in range(8):
            if side == 0:
                edge[i, 0:8, :] = jnp.zeros((8, LANES), F32)
                edge[i, 8:32, :] = ext[i, 0:24, :]
                edge[i, 6:8, :] = more[2 * i : 2 * i + 2, :]
            else:
                edge[i, 32:56, :] = ext[i, 8:32, :]
                edge[i, 56:64, :] = jnp.zeros((8, LANES), F32)
                edge[i, 56:58, :] = more[2 * i : 2 * i + 2, :]
        at = slice(0, 16) if side == 0 else slice(80, 96)
        two[0, at, :] = sent_rows(halo, 12)
        two[1, at, :] = sent_rows(halo, 13)
    two[0, 16:80, :TY] = bl[...].astype(F32)
    two[1, 16:80, :TY] = s[...]
    for i in range(2):
        two[i, 16:80, TY:] = hal[12 + i]
    lane = lax.broadcasted_iota(jnp.int32, (16, 128), 1)
    for i in range(4):
        for side in range(2):
            at = slice(0, 16) if side == 0 else slice(32, 48)
            packed = sums[i, at, TY:]
            for turn in range(2):
                base = 16 + 34 * turn
                own = slice(16 * (2 * turn + side), 16 * (2 * turn + side) + 16)
                outer, before, after = seam[i, own, 128:256], seam[i, own, 0:128], seam[i, own, 256:384]
                packed = jnp.where((lane >= base) & (lane < base + 16), pltpu.roll(outer, base, 1), packed)
                packed = jnp.where((lane >= base + 16) & (lane < base + 32), pltpu.roll(outer, base + 32, 1), packed)
                packed = jnp.where(lane == base + 32, pltpu.roll(before, base + 33, 1), packed)
                packed = jnp.where(lane == base + 33, pltpu.roll(after, base + 33, 1), packed)
                if i == 0:
                    load_at = seam[6, own, 128:256]
                    packed = jnp.where(lane == 84 + 2 * turn, pltpu.roll(load_at, 84 + 2 * turn, 1), packed)
                    packed = jnp.where(lane == 85 + 2 * turn, pltpu.roll(load_at, 86 + 2 * turn, 1), packed)
            send[2 * i + side, :, :TY] = sums[i, at, :TY].astype(BF)
            send[2 * i + side, :, TY:] = packed.astype(BF)
    ends = [sums[i, row : row + 1, :] for i in range(4) for row in (16, 31)]
    send[8] = jnp.concatenate(ends + loads + [jnp.zeros((6, LANES), F32)], 0).astype(BF)


def own_part(total, sc, u, v, b, flat, hal, low, high, force, out, done, pr, load):
    done[...] = jnp.zeros_like(done)
    base = 4 * sc[0]
    bl, s = flat.at[0], flat.at[1]
    upper = jnp.where(sc[0] == 0, step_dt, 0.0)

    def b_rows(k, r):
        if r == 0:
            return sent_rows(low, 8 + k)[8:16]
        if r == TX + 8:
            return sent_rows(high, 8 + k)[0:8]
        at = slice(r - 8, r)
        wet = wet_of(bl[at, :].astype(F32), (base + k).astype(F32))
        return jnp.concatenate([b[k, at, :] * wet, hal[8 + k, at, :]], 1)

    pressures(base, b_rows, pr, load, TX + 16)
    coriolis = coriolis_of(sc[1], total, (8, LANES))[:, :TY]
    for r in range(0, TX, 8):
        rr = slice(r, r + 8)
        lev = bl[rr, :].astype(F32)
        for k in range(4):
            number = (base + k).astype(F32)
            wet = wet_of(lev, number)
            drag = jnp.where(lev == number + 1.0, drag_coef, 0.0)
            east, north = u[k, rr, :], v[k, rr, :]
            gx, gy = grads(pr.at[k], r + 8)
            te = coriolis * north - press_coef * gx[:, :TY] - drag * east
            tn = -coriolis * east - press_coef * gy[:, :TY] - drag * north
            at = slice(r + 20, r + 28)
            fe = jnp.where(upper > 0.0, force[k, at, :TY], 0.0)
            fn = jnp.where(upper > 0.0, force[4 + k, at, :TY], 0.0)
            out[k, rr, :] = wet * (east + step_dt * (te + fe))
            out[4 + k, rr, :] = wet * (north + step_dt * (tn + fn))


def prepare(total, sc, ready, two, mid, seam, rim, mid_in, rim_in, force, ae, an, es, ns, rel, c2, off, above):
    zero8 = jnp.zeros((8, LANES), F32)
    lane = lax.broadcasted_iota(jnp.int32, (8, 128), 1)

    def ended(i, at, outer):
        first = jnp.where(lane == 0, seam[i, at, 256:384], mid[i, at, 0:128])
        last = jnp.where(lane == 127, seam[i, at, 0:128], mid[i, at, TY - 128 :])
        pieces = [first, mid[i, at, 128 : TY - 128], last]
        return jnp.concatenate(pieces + [seam[i, at, 128:256]] if outer else pieces, 1)

    for r in range(0, ROWS, 8):
        rr = slice(r, r + 8)
        level = two[0, rr, :]
        depth = level + 0.125 * level * (level - 1.0)
        over = 1.0 / jnp.maximum(depth, 1.0)
        rel[rr, :] = depth * (1.0 / TOTAL_DEPTH)
        c2[rr, :] = jnp.where(level > 0.0, 0.5 * sub_dt * gravity, 0.0)
        middle = RIM <= r < ROWS - RIM
        at = r - RIM if middle else (r if r < RIM else r - 48)
        at = slice(at, at + 8)
        x = r - HALO
        found = []
        for i in range(4):
            here = ended(i, slice(x, x + 8), True) if middle else rim[i, at, :]
            if not 0 <= x < TX:
                row = r % 16
                found.append(here + rim_in[2 * i + (x > 0), :, :].astype(F32)[row : row + 8])
                continue
            turn, half = x // 32, x % 16
            base = 16 + 34 * turn
            beyond = rim_in[2 * i + x // 16 % 2, :, TY:].astype(F32)[half : half + 8]
            theirs = mid_in[i, x - half : x - half + 16, :].astype(F32)[half : half + 8]
            outer = jnp.where(lane < 16, pltpu.roll(beyond, 128 - base, 1), pltpu.roll(beyond, 96 - base, 1))
            first = jnp.where(lane == 0, pltpu.roll(beyond, 95 - base, 1), theirs[:, 0:128])
            last = jnp.where(lane == 127, pltpu.roll(beyond, 95 - base, 1), theirs[:, TY - 128 :])
            theirs = jnp.concatenate([first, theirs[:, 128 : TY - 128], last, outer], 1)
            if x in (0, TX - 8):
                end = rim_in[8].astype(F32)[2 * i + (x > 0) : 2 * i + (x > 0) + 1]
                row = lax.broadcasted_iota(jnp.int32, (8, LANES), 0)
                theirs = jnp.where(row == (0 if x == 0 else 7), end, theirs)
            found.append(here + theirs)
        if not middle:
            everywhere = level == level
            mine = forced(sc, level, force, slice(r + 4, r + 12), [slice(0, LANES)], everywhere)
            found[:2] = [found[n] + mine[n] for n in range(2)]
        ae[rr, :] = sub_dt * found[0] * over
        an[rr, :] = sub_dt * found[1] * over
        e, n = found[2] * over, found[3] * over
        es[rr, :], ns[rr, :] = e, n

    @pl.when(sc[0] == 0)
    def _():
        off[0] = es[HALO : HALO + TX, :TY]
        off[1] = ns[HALO : HALO + TX, :TY]

    @pl.when(sc[0] != 0)
    def _():
        lane = lax.broadcasted_iota(jnp.int32, (16, 128), 1)
        for x in range(0, TX, 16):
            turn = x // 32
            beyond = rim_in[x // 16 % 2, :, TY:].astype(F32)
            outer = jnp.where(lane < 64, pltpu.roll(beyond, 44 - 2 * turn, 1), pltpu.roll(beyond, 42 - 2 * turn, 1))
            above[x + 8 : x + 24, :TY] = mid_in[4, x : x + 16, :].astype(F32)
            above[x + 8 : x + 24, TY:] = outer
        ends = rim_in[8].astype(F32)
        above[7:8, :], above[TX + 8 : TX + 9, :] = ends[8:9, :], ends[9:10, :]
        for r in range(0, TX, 8):
            gx, gy = grads(above, r)
            at = slice(r + HALO, r + HALO + 8)
            off[0, r : r + 8, :] = es[at, :TY] + (step_dt * press_coef) * gx[:, :TY]
            off[1, r : r + 8, :] = ns[at, :TY] + (step_dt * press_coef) * gy[:, :TY]


def substeps(total, sc, two, ae_in, an_in, es, ns, rel, c2, off, force_in, own, east_out, north_out, surface_out, lv, fx, fy, eb, nb, ae, an):
    zero8 = jnp.zeros((8, LANES), F32)
    for ref in (lv, fx):
        ref[0:8, :] = zero8
        ref[ROWS + 8 : ROWS + 16, :] = zero8
    share = jnp.where(sc[0] > 0, sub_dt, 0.0)
    for r in range(0, ROWS, 8):
        rr = slice(r, r + 8)
        eb[rr, :], nb[rr, :] = es[rr, :], ns[rr, :]
        lv[r + 8 : r + 16, :] = two[1, rr, :]
        if RIM <= r < ROWS - RIM:
            ae[rr, :], an[rr, :] = ae_in[rr, :], an_in[rr, :]
            continue
        level = two[0, rr, :]
        over = share / jnp.maximum(level + 0.125 * level * (level - 1.0), 1.0)
        row = lax.broadcasted_iota(jnp.int32, (8, LANES), 0)
        for n, (old, new) in enumerate(((ae_in, ae), (an_in, an))):
            if HALO <= r < ROWS - HALO:
                theirs = force_in[4].astype(F32)[8 * n : 8 * n + 8]
                theirs = jnp.where((row < 4) if r < RIM else (row >= 4), theirs, 0.0)
            else:
                half = r % 16
                theirs = force_in[2 * n + (r > RIM), :, :].astype(F32)[half : half + 8]
            new[rr, :] = old[rr, :] + over * theirs
    inside = inside_of(sc[1], total, (8, LANES))

    def step(first, carry):
        for r in range(first, ROWS - first, 8):
            rr = slice(r, r + 8)
            here = lv[r + 8 : r + 16, :]
            dx = lv[r + 9 : r + 17, :] - lv[r + 7 : r + 15, :]
            dy = pltpu.roll(here, LANES - 1, 1) - pltpu.roll(here, 1, 1)
            c = c2[rr, :]
            e = eb[rr, :] + (ae[rr, :] - c * dx)
            n = nb[rr, :] + (an[rr, :] - c * dy)
            eb[rr, :] = e
            nb[rr, :] = n
            fx[r + 8 : r + 16, :] = rel[rr, :] * e
            fy[rr, :] = rel[rr, :] * n
        for r in range(first, ROWS - first, 8):
            rr = slice(r, r + 8)
            dx = fx[r + 9 : r + 17, :] - fx[r + 7 : r + 15, :]
            f = fy[rr, :]
            dy = pltpu.roll(f, LANES - 1, 1) - pltpu.roll(f, 1, 1)
            lv[r + 8 : r + 16, :] = inside * (lv[r + 8 : r + 16, :] - (0.5 * sub_dt) * (dx + dy))
        return carry

    lax.fori_loop(0, NSUB // 2, lambda _, carry: step(0, carry), 0, unroll=4)
    lax.fori_loop(0, NSUB // 2, lambda _, carry: step(8, carry), 0, unroll=4)
    base = 4 * sc[0]
    for q in range(0, TX, 8):
        rr, at = slice(q + HALO, q + HALO + 8), slice(q, q + 8)
        level = two[0, rr, :TY]
        fe = eb[rr, :TY] - off[0, at, :] - (step_dt / sub_dt) * ae[rr, :TY]
        fn = nb[rr, :TY] - off[1, at, :] - (step_dt / sub_dt) * an[rr, :TY]
        for k in range(4):
            wet = wet_of(level, (base + k).astype(F32))
            east_out[k, at, :] = own[k, at, :] + wet * fe
            north_out[k, at, :] = own[4 + k, at, :] + wet * fn
        surface_out[at, :] = lv[q + HALO + 8 : q + HALO + 16, :TY]


def call(kernel, name, out_shape, n_in, scratch=(), in_specs=None, cost=None, grid=(), aliases=None, room=20):
    single = not isinstance(out_shape, (list, tuple))

    def body(*refs):
        kernel((lax.axis_index("grp"), lax.axis_index("lat")), *refs)

    return pl.pallas_call(
        body,
        name=name,
        grid=grid,
        out_shape=out_shape,
        in_specs=in_specs or [VMEM] * n_in,
        out_specs=VMEM if single else [VMEM] * len(out_shape),
        scratch_shapes=list(scratch),
        compiler_params=pltpu.CompilerParams(vmem_limit_bytes=room * 2**20),
        cost_estimate=cost,
        input_output_aliases=aliases or {},
    )


def with_total(kernel, total):
    return lambda sc, *refs: kernel(total, sc, *refs)


def micros(us):
    return pl.CostEstimate(flops=int(us * 1e6), bytes_accessed=int(us * 3e6), transcendentals=0)


def shifted(x, axis, by):
    size = lax.axis_size(axis)
    return lax.ppermute(x, axis, [(i, (i + by) % size) for i in range(size)])


def local(u, v, b, wet_mask, bl, s, w_in, b_in, w_mid, b_mid, w_out):
    total = TY * lax.axis_size("lat")
    wide, half = pltpu.VMEM((2, 4, TX, 128), F32), sds((2, TX, 128), BF)
    made = [sds((192, 256), BF), sds((576, 256), BF), sds((192, 320), BF), sds((32, 128)), sds((32, 128))]
    to_down, to_up, flat, *weights = call(
        pack_lat,
        "pack_lat",
        [half, half, sds((2, TX, TY))] + made,
        10,
        [
            wide,
            wide,
            wide,
            pltpu.VMEM((TX, TY), jnp.int32),
            pltpu.VMEM((TX, TY), F32),
            pltpu.SemaphoreType.DMA((2, 5)),
            pltpu.VMEM((9, 8, 32), BF),
            pltpu.VMEM((1, 32), F32),
            pltpu.VMEM((9, 32, 32), BF),
            pltpu.VMEM((1, 32), F32),
            pltpu.VMEM((9, 8, 32), BF),
            pltpu.VMEM((8, 8, 384), F32),
            pltpu.SemaphoreType.DMA((5,)),
        ],
        in_specs=[pl.BlockSpec(memory_space=pltpu.HBM)] * 10,
        room=60,
    )(u, v, b, bl, s, w_in, b_in[None, :], w_mid, b_mid[None, :], jnp.swapaxes(w_out, 1, 2))
    before = shifted(to_up, "lat", 1)
    after = shifted(to_down, "lat", -1)

    near = call(bring, "bring", TOKEN, 1, cost=micros(1))(flat)

    out = sds((16, 16, TY), BF)
    hal, down, up = call(
        with_total(pack_lon, total),
        "pack_lon",
        [sds((FIELDS, TX, 128)), out, out],
        7,
        [pltpu.VMEM((16, LANES), F32)],
    )(near, before, after, u, v, b, flat)
    low = shifted(up, "lon", 1)
    high = shifted(down, "lon", -1)
    inner, ready = call(
        with_total(interior, total),
        "interior",
        [sds((8, FORCED, LANES)), TOKEN],
        9,
        [
            pltpu.VMEM((8, TX, LANES), F32),
            pltpu.VMEM((62 * 32, LANES), BF),
            pltpu.VMEM((62 * 32, LANES), BF),
            pltpu.VMEM((60 * 32, LANES), BF),
        ],
        cost=micros(7),
    )(u, v, flat, hal, *weights)
    mid, mid_send, summed = call(
        with_total(middle_sums, total),
        "middle_sums",
        [sds((6, TX, TY)), sds((5, TX, TY), BF), TOKEN],
        6,
        [pltpu.VMEM((4, TX + 16, TY), F32), pltpu.VMEM((TX + 16, TY), F32)],
        cost=micros(1),
    )(ready, u, v, b, flat, inner)
    mid_in = shifted(mid_send, "grp", 1)
    seam = call(
        with_total(seam_sums, total),
        "seam_sums",
        sds((7, TX, 384)),
        6,
        [pltpu.VMEM((13, TX, 384), F32), pltpu.VMEM((4, TX + 16, 384), F32), pltpu.VMEM((TX + 16, 384), F32)],
        cost=micros(1),
    )(u, v, b, flat, hal, inner)
    rim, rim_send, two, edge = call(
        with_total(rim_sums, total),
        "rim_sums",
        [sds((6, 48, LANES)), sds((9, 16, LANES), BF), sds((2, ROWS, LANES)), sds((8, 64, LANES))],
        9,
        [pltpu.VMEM((13, 32, LANES), F32), pltpu.VMEM((4, 48, LANES), F32), pltpu.VMEM((48, LANES), F32)],
        cost=micros(2),
    )(summed, u, v, b, flat, hal, low, high, seam)
    rim_in = shifted(rim_send, "grp", 1)
    force, force_send = call(
        with_total(edges, total),
        "edges",
        [sds((8, FORCED, LANES)), sds((5, 16, LANES), BF)],
        8,
        [pltpu.VMEM((52 * 32, LANES), BF), pltpu.VMEM((52 * 32, LANES), BF), pltpu.VMEM((55 * 32, LANES), BF)],
        cost=micros(6),
        aliases={7: 0},
    )(edge, two, *weights, inner)
    force_in = shifted(force_send, "grp", 1)
    own, owned = call(
        with_total(own_part, total),
        "own_part",
        [sds((8, TX, TY)), TOKEN],
        8,
        [pltpu.VMEM((4, 96, LANES), F32), pltpu.VMEM((96, LANES), F32)],
        cost=micros(2),
    )(u, v, b, flat, hal, low, high, force)
    start = call(
        with_total(prepare, total),
        "prepare",
        [sds((ROWS, LANES))] * 6 + [sds((2, TX, TY))],
        8,
        [pltpu.VMEM((TX + 16, LANES), F32)],
        cost=micros(1),
    )(owned, two, mid, seam, rim, mid_in, rim_in, force)
    plane = pltpu.VMEM((ROWS, LANES), F32)
    tall = pltpu.VMEM((ROWS + 16, LANES), F32)
    return tuple(
        call(
            with_total(substeps, total),
            "substeps",
            [sds((4, TX, TY)), sds((4, TX, TY)), sds((TX, TY))],
            10,
            [tall, tall] + [plane] * 5,
            cost=micros(5),
        )(two, *start, force_in, own)
    )


def solution(mesh):
    tile = P("grp", "lon", "lat")
    flat = P("lon", "lat")
    return jax.shard_map(
        local,
        mesh=mesh,
        in_specs=(tile, tile, tile, tile, flat, flat, P(), P(), P(), P(), P()),
        out_specs=(tile, tile, flat),
        check_vma=False,
    )
```
